128 devices in a mesh: rep: 8 (over y, x_lo), shard: 16 (over z, x_hi, core).
Axes of the slice: x: 4 (x_hi: 2, x_lo: 2; x = x_hi * 2 + x_lo), y: 4, z: 4, core: 2. Of those that a mesh axis runs over, the one named last changes fastest.
Arguments:
- inputs: float32 [24576, 1024], P(('rep', 'shard')), may hold values from -6 to 6
- cotangent: float32 [24576, 1024], P(('rep', 'shard')), may hold values from -6 to 6
- lengths: int32 [128, 4], P(('rep', 'shard')), may hold values from 0 to 192, as said below
- ln_gain: bfloat16 [2, 1024], P(None, 'shard'), may hold values from 0.5 to 1.5
- ln_bias: bfloat16 [2, 1024], P(None, 'shard'), may hold values from -3 to 3
- w_qkv: bfloat16 [2, 1024, 3072], P(None, 'shard'), may hold values from -0.1875 to 0.1875
- w_attn_out: bfloat16 [2, 1024, 1024], P(None, 'shard'), may hold values from -1 to 1
- w_in: bfloat16 [2, 1024, 4096], P(None, 'shard'), may hold values from -0.1875 to 0.1875
- b_in: bfloat16 [2, 4096], P(None, 'shard'), may hold values from -3 to 3
- w_fc: bfloat16 [2, 4096, 1024], P(None, 'shard'), may hold values from -0.09375 to 0.09375
- b_fc: bfloat16 [2, 1024], P(None, 'shard'), may hold values from -3 to 3
Outputs:
- outputs: float32 [24576, 1024], P(('rep', 'shard'))
- input_grad: float32 [24576, 1024], P(('rep', 'shard'))
- ln_gain_grad: float32 [2, 1024], P(None, 'shard')
- ln_bias_grad: float32 [2, 1024], P(None, 'shard')
- w_qkv_grad: float32 [2, 1024, 3072], P(None, 'shard')
- w_attn_out_grad: float32 [2, 1024, 1024], P(None, 'shard')
- w_in_grad: float32 [2, 1024, 4096], P(None, 'shard')
- b_in_grad: float32 [2, 4096], P(None, 'shard')
- w_fc_grad: float32 [2, 4096, 1024], P(None, 'shard')
- b_fc_grad: float32 [2, 1024], P(None, 'shard')
The draws below stay inside these ranges and needn't reach their ends.
Inputs may be any that keep to these rules, and one draw needn't show every extreme that they name: Row b gives, in order, the lengths of the sequences packed from the start of token buffer b; a length of 0 is an empty slot. A row's lengths sum to 96 or more and to 192 at most, and in every draw some row holds one sequence of exactly 192 tokens.
All inputs are finite; a program needn't handle non-finite values.
Results may differ from the reference program's by a relative error of at most 0.02.
Values may be sent and summed in bfloat16 or wider, within the bound.
A program may use at most 256 MiB of HBM per device.

```python
import math
import jax
import jax.numpy as jnp
from jax import lax

D = 1024
HEADS = 16
HEAD = 64
ROT = 32
FF = 4096
LAYERS = 2
SLOTS = 4
CAP = 192
BUFFERS = 128
TOKENS = 24576


def draw_lengths(key, part):
    key = jax.random.fold_in(key, 7)
    used_key, cut_key, pick_key = jax.random.split(key, 3)
    used_rows = jax.random.randint(used_key, (BUFFERS, 1), CAP // 2, CAP + 1)
    cut_points = jax.random.randint(cut_key, (BUFFERS, SLOTS - 1), 0, used_rows + 1)
    cut_points = jnp.sort(cut_points, axis=1)
    boundaries = jnp.concatenate([jnp.zeros((BUFFERS, 1), jnp.int32), cut_points, used_rows], axis=1)
    seq_lengths = boundaries[:, 1:] - boundaries[:, :-1]
    chosen = jax.random.randint(pick_key, (), 0, BUFFERS)
    single_row = jnp.where(jnp.arange(SLOTS) == 0, CAP, 0)
    picked = (jnp.arange(BUFFERS) == chosen)[:, None]
    return jnp.where(picked, single_row[None, :], seq_lengths).astype(jnp.int32)


def block_scale(stream_key, shape, cuts, low, top_value):
    gain, own = 1.0, jax.random.fold_in(stream_key, 6)
    for dim, shards_of in cuts:
        heights = jnp.exp(jax.random.uniform(jax.random.fold_in(own, dim), (shards_of,), jnp.float32, low / len(cuts), top_value / len(cuts)))
        gain = gain * jnp.repeat(heights, shape[dim] // shards_of).reshape([-1 if axis == dim else 1 for axis in range(len(shape))])
    return gain


def normal_values(rng, shape, deviation, limit, cuts=(), held_as=jnp.bfloat16):
    drawn = deviation * jax.random.normal(rng, shape, jnp.float32)
    if cuts:
        drawn = drawn * block_scale(rng, shape, cuts, -0.22, 0.18)
    return jnp.clip(drawn, -limit, limit).astype(held_as)


def setup_inputs(seed: int = 0) -> dict:
    seeds = jax.random.split(jax.random.key(seed), 12)
    inputs = normal_values(seeds[0], (TOKENS, D), 1.0, 6.0, ((0, 128),), jnp.float32)
    cotangent = normal_values(seeds[1], (TOKENS, D), 1.0, 6.0, ((0, 128),), jnp.float32)
    lengths = draw_lengths(jax.random.fold_in(seeds[11], 71), 0)
    ln_gain = jnp.clip(1.0 + 0.1 * jax.random.normal(seeds[3], (LAYERS, D), jnp.float32), 0.5, 1.5).astype(jnp.bfloat16)
    ln_bias = normal_values(seeds[4], (LAYERS, D), 0.5, 3.0, ((1, 16),))
    w_qkv = normal_values(seeds[5], (LAYERS, D, 3 * D), D ** -0.5, 0.1875, ((1, 16),))
    w_attn_out = normal_values(seeds[6], (LAYERS, D, D), (max(1, D * 2 * SLOTS // CAP)) ** -0.5, 1.0, ((1, 16),))
    w_in = normal_values(seeds[7], (LAYERS, D, FF), D ** -0.5, 0.1875, ((1, 16),))
    b_in = normal_values(seeds[8], (LAYERS, FF), 0.5, 3.0, ((1, 16),))
    w_fc = normal_values(seeds[9], (LAYERS, FF, D), FF ** -0.5, 0.09375, ((1, 16),))
    b_fc = normal_values(seeds[10], (LAYERS, D), 0.5, 3.0, ((1, 16),))
    return dict(inputs=inputs, cotangent=cotangent, lengths=lengths, ln_gain=ln_gain, ln_bias=ln_bias, w_qkv=w_qkv, w_attn_out=w_attn_out, w_in=w_in, b_in=b_in, w_fc=w_fc, b_fc=b_fc)


@jax.custom_vjp
def low(v):
    return lax.optimization_barrier(v.astype(jnp.bfloat16)).astype(jnp.float32)

@jax.custom_vjp
def low_back(v):
    return v

def low_keep(v):
    return (low(v), None)

def low_pass(kept, grad):
    return (grad,)

def back_keep(v):
    return (v, None)

def back_low(kept, grad):
    return (low(grad),)
low.defvjp(low_keep, low_pass)
low_back.defvjp(back_keep, back_low)
EPSILON = 1e-05
NEGATIVE = -1e+30
HIGH = lax.Precision.HIGHEST

def matmul(first_op, second_op):
    return jnp.dot(first_op, second_op, preferred_element_type=jnp.float32, precision=HIGH)

def layer_norm(values, gain_row, bias_row):
    centre = values - lax.optimization_barrier(jnp.mean(values, axis=-1, keepdims=True))
    spread = lax.optimization_barrier(jnp.mean(centre * centre, axis=-1, keepdims=True))
    return centre * lax.rsqrt(spread + EPSILON) * gain_row + bias_row

def rotate(values, cosine_table, sine_table):
    half_rot = ROT // 2
    first_half = values[..., :half_rot]
    second_half = values[..., half_rot:ROT]
    return jnp.concatenate([first_half * cosine_table - second_half * sine_table, second_half * cosine_table + first_half * sine_table, values[..., ROT:]], axis=-1)

def gelu_tanh(values):
    return 0.5 * values * (1.0 + jnp.tanh(0.7978845608028654 * (values + 0.044715 * values * values * values)))

def buffer_layout(lengths):
    offsets = jnp.arange(CAP, dtype=jnp.int32)
    seq_ends = jnp.cumsum(lengths, axis=1).astype(jnp.int32)
    passed = (offsets[None, :, None] >= seq_ends[:, None, :]).astype(jnp.int32)
    segment = lax.optimization_barrier(jnp.sum(passed, axis=2)).astype(jnp.int32)
    seg_start = lax.optimization_barrier(jnp.sum(passed * lengths[:, None, :], axis=2)).astype(jnp.int32)
    return (segment, offsets[None, :] - seg_start)

def attend_buffer(pieces):
    queries, key_rows, value_rows, segment = pieces
    offsets = jnp.arange(CAP, dtype=jnp.int32)
    scores = jnp.einsum('qhd,khd->hqk', queries, key_rows, precision=HIGH) * (1.0 / math.sqrt(HEAD))
    scores = low_back(scores)
    allowed = (segment[:, None] == segment[None, :]) & (offsets[:, None] >= offsets[None, :])
    masked = jnp.where(allowed[None], scores, NEGATIVE)
    row_peak = lax.optimization_barrier(jnp.max(masked, axis=-1, keepdims=True))
    exponent = jnp.exp(masked - row_peak)
    soft_weights = exponent / lax.optimization_barrier(jnp.sum(exponent, axis=-1, keepdims=True))
    return jnp.einsum('hqk,khd->qhd', low(soft_weights), value_rows, precision=HIGH)

def forward(start_rows, weight_set, segment, cosine_table, sine_table):
    ln_gain, ln_bias, w_qkv, w_attn_out, w_in, b_in, w_fc, b_fc = weight_set
    hidden = start_rows
    for depth_index in range(LAYERS):
        normed = low(layer_norm(hidden, ln_gain[depth_index], ln_bias[depth_index]))
        packed = low_back(matmul(normed, w_qkv[depth_index])).reshape(BUFFERS, CAP, 3, HEADS, HEAD)
        queries = low(rotate(packed[:, :, 0], cosine_table, sine_table))
        key_rows = low(rotate(packed[:, :, 1], cosine_table, sine_table))
        value_rows = low(packed[:, :, 2])
        attended = lax.map(jax.checkpoint(attend_buffer), (queries, key_rows, value_rows, segment))
        mixed = low_back(low(attended.reshape(TOKENS, D)))
        pre_act = matmul(normed, w_in[depth_index]) + b_in[depth_index]
        activated = low(gelu_tanh(low_back(pre_act)))
        branch = low_back(matmul(mixed, w_attn_out[depth_index]) + (matmul(activated, w_fc[depth_index]) + b_fc[depth_index]))
        hidden = hidden + branch
    return hidden

def reference(inputs, cotangent, lengths, ln_gain, ln_bias, w_qkv, w_attn_out, w_in, b_in, w_fc, b_fc):
    weight_set = tuple((item.astype(jnp.float32) for item in (ln_gain, ln_bias, w_qkv, w_attn_out, w_in, b_in, w_fc, b_fc)))
    segment, position = buffer_layout(lengths)
    frequency = 10000.0 ** (-jnp.arange(ROT // 2, dtype=jnp.float32) * 2.0 / ROT)
    angles = position.astype(jnp.float32)[:, :, None, None] * frequency
    cosine_table = jnp.cos(angles)
    sine_table = jnp.sin(angles)
    valid_rows = (segment < SLOTS).astype(jnp.float32).reshape(TOKENS, 1)
    outputs, pullback = jax.vjp(lambda start_rows, weights_now: forward(start_rows, weights_now, segment, cosine_table, sine_table), inputs, weight_set)
    input_grad, weight_grads = pullback(cotangent * valid_rows)
    return (outputs, input_grad, weight_grads[0], weight_grads[1], weight_grads[2], weight_grads[3], weight_grads[4], weight_grads[5], weight_grads[6], weight_grads[7])
```

```python
import functools
import math

import jax
import jax.numpy as jnp
from jax import lax
from jax.experimental import pallas as pl
from jax.experimental.pallas import tpu as pltpu
from jax.sharding import Mesh
from jax.sharding import PartitionSpec as P

D = 1024
HEADS = 16
HEAD = 64
ROT = 32
FF = 4096
LAYERS = 2
SLOTS = 4
CAP = 192
LINE = 8
QKV = 384
HID = 512
WIDE = QKV + HID
DEEP = 128 + HID
EPSILON = 1e-05
NEGATIVE = -1e30
AXES = ("y", "xl", "z", "xh", "c")
BF = jnp.bfloat16
F32 = jnp.float32
MESH = pl.DeviceIdType.MESH
VMEM = pltpu.VMEM
DMA = pltpu.SemaphoreType.DMA
ANY = pl.BlockSpec(memory_space=pl.ANY)
INV = pl.BlockSpec(memory_space=pltpu.VMEM)
C0 = 0.7978845608028654
C1 = 0.044715


def div(a, b):
    return lax.div(a, jnp.int32(b))


def rem(a, b):
    return lax.rem(a, jnp.int32(b))


def place():
    y, xl, z, xh, c = (lax.axis_index(a) for a in AXES)
    return y, xl, z, xh, c


def send(src, dst, ss, rs, **dev):
    cp = pltpu.make_async_remote_copy(
        src_ref=src, dst_ref=dst, send_sem=ss, recv_sem=rs, device_id=dev, device_id_type=MESH
    )
    cp.start()


def local(src, dst, sem):
    pltpu.make_async_copy(src, dst, sem).start()


def landed(ref, sem):
    pltpu.make_async_copy(ref, ref, sem).wait()


def loop(n, body):
    lax.fori_loop(0, n, lambda i, _: (body(i), 0)[1], 0)


def signal(sem, **dev):
    pl.semaphore_signal(sem, inc=1, device_id=dev, device_id_type=MESH)


def greet_line(bar, z, c):
    for k in range(1, LINE):
        j = rem(2 * z + c + k, LINE)
        signal(bar, z=div(j, 2), c=rem(j, 2))


def greet_plane(bar, y, x):
    for k in range(1, 16):
        yy = rem(y + k // 4, 4)
        xx = rem(x + k % 4, 4)
        signal(bar, y=yy, xh=div(xx, 2), xl=rem(xx, 2))


def gather_kernel(
    wqkv, win, wo, wfc, sm, tab, w1, w2, sma, tabs,
    cs, cr, as_, ar, bs, br, ts, tr,
):
    y, xl, z, xh, c = place()
    x = 2 * xh + xl
    p = 4 * y + x
    j = 2 * z + c
    bar = pltpu.get_barrier_semaphore()
    greet_line(bar, z, c)
    greet_plane(bar, y, x)
    signal(bar, xl=1 - xl, xh=1 - xh, c=1 - c)
    pl.semaphore_wait(bar, 23)

    mine = pl.ds(pl.multiple_of(64 * p, 64), 64)
    for l in range(LAYERS):
        @pl.when((z == y) & (c == xl))
        def _():
            def to(jj):
                pairs = []
                for part in range(3):
                    cols = pl.ds(pl.multiple_of(part * D + jj * 128, 128), 128)
                    pairs.append((wqkv.at[l, :, cols], w1.at[l, mine, pl.ds(part * 128, 128)]))
                cols = pl.ds(pl.multiple_of(jj * HID, HID), HID)
                pairs.append((win.at[l, :, cols], w1.at[l, mine, pl.ds(QKV, HID)]))
                if l == 0:
                    pairs.append((sm, sma.at[p]))

                @pl.when(jj == j)
                def _():
                    for i, (src, dst) in enumerate(pairs):
                        local(src, dst, ar.at[l, i])

                @pl.when(jj != j)
                def _():
                    for i, (src, dst) in enumerate(pairs):
                        send(src, dst, as_.at[jj, l, i], ar.at[l, i], z=div(jj, 2), c=rem(jj, 2))

            loop(LINE, to)

        pieces = (
            (wo.at[l], w2.at[l, pl.ds(pl.multiple_of(64 * c, 64), 64)]),
            (wfc.at[l], w2.at[l, pl.ds(pl.multiple_of(128 + 256 * c, 64), 256)]),
        )
        for i, (src, dst) in enumerate(pieces):
            send(src, dst, cs.at[l, 0, i], cr.at[l, c, i], xl=1 - xl, xh=1 - xh, c=xh)

            @pl.when(c == xh)
            def _():
                local(src, dst, cr.at[l, c, i])

            @pl.when(c != xh)
            def _():
                send(src, dst, cs.at[l, 1, i], cr.at[l, c, i], c=xh)

    for k in range(1, LINE):
        jj = rem(j + k, LINE)
        send(tab, tabs.at[j], ts.at[k], tr.at[j], z=div(jj, 2), c=rem(jj, 2))
    local(tab, tabs.at[j], tr.at[j])

    for l in range(LAYERS):
        for part in range(3):
            landed(w1.at[l, mine, pl.ds(part * 128, 128)], ar.at[l, part])
        landed(w1.at[l, mine, pl.ds(QKV, HID)], ar.at[l, 3])
        if l == 0:
            landed(sma.at[p], ar.at[l, 4])

        def across(k):
            yy = rem(y + div(k, 4), 4)
            xx = rem(x + rem(k, 4), 4)
            dev = dict(y=yy, xh=div(xx, 2), xl=rem(xx, 2))
            send(w1.at[l, mine], w1.at[l, mine], bs.at[l, k, 0], br.at[l, p, 0], **dev)
            if l == 0:
                send(sma.at[p], sma.at[p], bs.at[l, k, 1], br.at[l, p, 1], **dev)

        loop(15, lambda k: across(k + 1))

    def arrive(l, k):
        q = rem(p + k, 16)
        rows = pl.ds(pl.multiple_of(64 * q, 64), 64)
        landed(w1.at[l, rows], br.at[l, q, 0])
        if l == 0:
            landed(sma.at[q], br.at[l, q, 1])

    for l in range(LAYERS):
        loop(15, lambda k: arrive(l, k + 1))
        for s in range(2):
            landed(w2.at[l, pl.ds(64 * s, 64)], cr.at[l, s, 0])
            landed(w2.at[l, pl.ds(128 + 256 * s, 256)], cr.at[l, s, 1])
    loop(LINE, lambda k: landed(tabs.at[k], tr.at[k]))

    for l in range(LAYERS):

        def left(k):
            landed(w1.at[l, mine], bs.at[l, k, 0])
            if l == 0:
                landed(sma.at[p], bs.at[l, k, 1])

        loop(15, lambda k: left(k + 1))
        landed(wo.at[l], cs.at[l, 0, 0])
        landed(wfc.at[l], cs.at[l, 0, 1])

        @pl.when(c != xh)
        def _():
            landed(wo.at[l], cs.at[l, 1, 0])
            landed(wfc.at[l], cs.at[l, 1, 1])

        @pl.when((z == y) & (c == xl))
        def _():
            def gone(jj):
                @pl.when(jj != j)
                def _():
                    for part in range(3):
                        landed(wqkv.at[l, :, pl.ds(part * D, 128)], as_.at[jj, l, part])
                    landed(win.at[l, :, pl.ds(0, HID)], as_.at[jj, l, 3])
                    if l == 0:
                        landed(sm, as_.at[jj, l, 4])

            loop(LINE, gone)

    for k in range(1, LINE):
        landed(tab, ts.at[k])


def gather_weights(wqkv, win, wo, wfc, sm, tab):
    return pl.pallas_call(
        gather_kernel,
        out_shape=(
            jax.ShapeDtypeStruct((LAYERS, D, WIDE), BF),
            jax.ShapeDtypeStruct((LAYERS, DEEP, D), BF),
            jax.ShapeDtypeStruct((16, 16, 256), BF),
            jax.ShapeDtypeStruct((LINE, CAP, 128), F32),
        ),
        in_specs=[ANY] * 6,
        out_specs=(ANY,) * 4,
        scratch_shapes=[
            DMA((LAYERS, 2, 2)), DMA((LAYERS, 2, 2)),
            DMA((LINE, LAYERS, 5)), DMA((LAYERS, 5)),
            DMA((LAYERS, 16, 2)), DMA((LAYERS, 16, 2)),
            DMA((LINE,)), DMA((LINE,)),
        ],
        compiler_params=pltpu.CompilerParams(collective_id=0, has_side_effects=True),
        name="gather_weights",
    )(wqkv, win, wo, wfc, sm, tab)


def slot_of(z, c, k):
    return 2 * rem(z + k, 4) + c


def rows_start(buf, z, c, ss, rs):
    own = buf.at[2 * z + c]
    send(own, own, ss.at[0], rs.at[0], c=1 - c)
    send(own, own, ss.at[1], rs.at[1], z=rem(z + 1, 4))
    send(own, own, ss.at[2], rs.at[2], z=rem(z + 3, 4))


def rows_near(buf, z, c, ss, rs):
    lo, hi = slot_of(z, c, 3), slot_of(z, c, 1)
    landed(buf.at[lo], rs.at[1])
    a = buf.at[lo, pl.ds(0, CAP // 2)]
    send(a, a, ss.at[3], rs.at[3], z=rem(z + 1, 4))
    send(buf.at[lo], buf.at[lo], ss.at[5], rs.at[5], c=1 - c)
    landed(buf.at[hi], rs.at[2])
    b = buf.at[hi, pl.ds(CAP // 2, CAP // 2)]
    send(b, b, ss.at[4], rs.at[4], z=rem(z + 3, 4))
    send(buf.at[hi], buf.at[hi], ss.at[6], rs.at[6], c=1 - c)


def rows_far(buf, z, c, ss, rs):
    far = slot_of(z, c, 2)
    landed(buf.at[far, pl.ds(0, CAP // 2)], rs.at[3])
    landed(buf.at[far, pl.ds(CAP // 2, CAP // 2)], rs.at[4])
    send(buf.at[far], buf.at[far], ss.at[7], rs.at[7], c=1 - c)


def rows_ready(k, buf, z, c, ss, rs):
    @pl.when(k == 0)
    def _():
        landed(buf.at[2 * z + 1 - c], rs.at[0])

    @pl.when(k == 1)
    def _():
        rows_near(buf, z, c, ss, rs)
        landed(buf.at[slot_of(z, 1 - c, 3)], rs.at[5])

    @pl.when(k == 2)
    def _():
        rows_far(buf, z, c, ss, rs)
        landed(buf.at[slot_of(z, 1 - c, 1)], rs.at[6])

    @pl.when(k == 3)
    def _():
        landed(buf.at[slot_of(z, 1 - c, 2)], rs.at[7])


def rows_left(buf, z, c, ss):
    for i in (0, 1, 2):
        landed(buf.at[2 * z + c], ss.at[i])
    landed(buf.at[0, pl.ds(0, CAP // 2)], ss.at[3])
    landed(buf.at[0, pl.ds(0, CAP // 2)], ss.at[4])
    for i in (5, 6, 7):
        landed(buf.at[0], ss.at[i])


def chip_of(z, k):
    return rem(z + jnp.where(k == 1, 3, jnp.where(k == 0, 0, k - 1)), 4)


def sums_send(k, zz, partial, c, own, sibout, sibin, out, inn, sbs, sbr, rss, rsr):
    sibout[k] = partial(2 * zz + 1 - c).astype(BF)
    send(sibout.at[k], sibin.at[k], sbs.at[k], sbr.at[k], c=1 - c)
    term = partial(2 * zz + c)
    landed(sibin.at[k], sbr.at[k])
    term = term + sibin[k].astype(F32)

    @pl.when(k == 0)
    def _():
        own[...] = term

    @pl.when(k > 0)
    def _():
        out[k - 1] = term.astype(BF)
        send(out.at[k - 1], inn.at[k - 1], rss.at[k - 1], rsr.at[k - 1], z=zz)


def sums_total(own, inn, rsr):
    total = own[...]
    for i in range(3):
        landed(inn.at[i], rsr.at[i])
        total = total + inn[i].astype(F32)
    return total


def sums_left(sibout, out, sbs, rss):
    for i in range(4):
        landed(sibout.at[i], sbs.at[i])
    for i in range(3):
        landed(out.at[i], rss.at[i])


ROW_SEMS = [DMA((8,)), DMA((8,)), DMA((4,)), DMA((4,)), DMA((3,)), DMA((3,))]
SUM_BUFFERS = [
    VMEM((CAP, D), F32),
    VMEM((4, CAP, D), BF),
    VMEM((4, CAP, D), BF),
    VMEM((3, CAP, D), BF),
    VMEM((3, CAP, D), BF),
]


def lanes(shape):
    return lax.broadcasted_iota(jnp.int32, shape, len(shape) - 1)


def turn(v, cos, sin):
    low = rem(lanes(v.shape), 64) < 16
    partner = jnp.where(low, pltpu.roll(v, 112, 1), pltpu.roll(v, 16, 1))
    return v * cos + partner * sin


def nt(a, b):
    return lax.dot_general(a, b, (((1,), (1,)), ((), ())), preferred_element_type=F32)


def tn(a, b):
    return lax.dot_general(a, b, (((0,), (0,)), ((), ())), preferred_element_type=F32)


def nn(a, b):
    return jnp.dot(a, b, preferred_element_type=F32)


def stats(x):
    centre = x - jnp.mean(x, axis=-1, keepdims=True)
    r = lax.rsqrt(jnp.mean(centre * centre, axis=-1, keepdims=True) + EPSILON)
    return centre, r


def forward_kernel(
    x_ref, ln_ref, bin_ref, w1, w2, tab,
    xn_ref, nall_o, qkv_o, p_o, a2_o, pre_o,
    nall, qkv, prob, a2, pre, raw,
    own, sibout, sibin, out, inn,
    ss, rs, sbs, sbr, rss, rsr, save,
):
    y, xl, z, xh, c = place()
    bar = pltpu.get_barrier_semaphore()
    greet_line(bar, z, c)
    centre, r = stats(x_ref[...])
    nall[2 * z + c] = (centre * r * ln_ref[0:1, :] + ln_ref[1:2, :]).astype(BF)
    pl.semaphore_wait(bar, LINE - 1)
    rows_start(nall, z, c, ss, rs)
    pairs = ((nall, nall_o), (qkv, qkv_o), (prob, p_o), (a2, a2_o), (pre, pre_o))

    def step(k):
        zz = chip_of(z, k)
        rows_ready(k, nall, z, c, ss, rs)
        two = pl.ds(2 * zz, 2)
        n = nall[two].reshape(2 * CAP, D)
        raw[...] = nn(n, w1[:, :QKV])
        pre[two] = (nn(n, w1[:, QKV:]) + bin_ref[0:1, :]).reshape(2, CAP, HID)

        def act(i):
            u, t = div(i, 6), rem(i, 6)
            rows = pl.ds(pl.multiple_of(t * 32, 32), 32)
            v = pre[2 * zz + u, rows, :]
            g = 0.5 * v * (1.0 + jnp.tanh(C0 * (v + C1 * v * v * v)))
            a2[2 * zz + u, rows, 128:] = g.astype(BF)

        loop(12, act)
        for u in range(2):
            s = 2 * zz + u
            rows = slice(u * CAP, (u + 1) * CAP)
            cos, sin = tab[s, :, 0:128], tab[s, :, 128:256]
            start = tab[s, :, 256:257]
            q = turn(raw[rows, 0:128], cos, sin).astype(BF)
            kk = turn(raw[rows, 128:256], cos, sin).astype(BF)
            v = raw[rows, 256:384].astype(BF)
            qkv[s, :, 0:128] = q
            qkv[s, :, 128:256] = kk
            qkv[s, :, 256:384] = v
            q = q * jnp.asarray(1.0 / math.sqrt(HEAD), BF)
            key_at = lanes((CAP, CAP))
            query_at = lax.broadcasted_iota(jnp.int32, (CAP, CAP), 0)
            allowed = (key_at >= start.astype(jnp.int32)) & (key_at <= query_at)
            head = lanes((CAP, 128)) < HEAD
            mixed = []
            for h in range(2):
                qh = jnp.where(head if h == 0 else ~head, q, jnp.zeros_like(q))
                score = jnp.where(allowed, nt(qh, kk), NEGATIVE)
                e = jnp.exp(score - jnp.max(score, axis=-1, keepdims=True))
                w = e / jnp.sum(e, axis=-1, keepdims=True)
                prob[2 * s + h] = w
                mixed.append(nn(w.astype(BF), v))
            a2[s, :, 0:128] = jnp.where(head, mixed[0], mixed[1]).astype(BF)

        for i, (src, dst) in enumerate(pairs):
            part = pl.ds(4 * zz, 4) if i == 2 else two
            local(src.at[part], dst.at[part], save.at[k, i])
        sums_send(
            k, zz, lambda s: nn(a2[s], w2[...]), c, own, sibout, sibin, out, inn, sbs, sbr, rss, rsr
        )

    loop(4, step)
    xn_ref[...] = x_ref[...] + (sums_total(own, inn, rsr) + ln_ref[2:3, :])
    for k in range(4):
        for i, (src, dst) in enumerate(pairs):
            part = pl.ds(0, 4) if i == 2 else pl.ds(0, 2)
            landed(src.at[part], save.at[k, i])
    rows_left(nall, z, c, ss)
    sums_left(sibout, out, sbs, rss)


SAVED = (
    ((LINE, CAP, D), BF),
    ((LINE, CAP, QKV), BF),
    ((2 * LINE, CAP, CAP), F32),
    ((LINE, CAP, DEEP), BF),
    ((LINE, CAP, HID), F32),
)


def forward_layer(l, x, ln, b_in, w1, w2, tab):
    return pl.pallas_call(
        forward_kernel,
        out_shape=(jax.ShapeDtypeStruct((CAP, D), F32),)
        + tuple(jax.ShapeDtypeStruct(s, t) for s, t in SAVED),
        in_specs=[INV] * 6,
        out_specs=(INV,) + (ANY,) * 5,
        scratch_shapes=[VMEM(s, t) for s, t in SAVED]
        + [VMEM((2 * CAP, QKV), F32)]
        + SUM_BUFFERS
        + ROW_SEMS
        + [DMA((4, 5))],
        compiler_params=pltpu.CompilerParams(
            collective_id=1 + l, has_side_effects=True, vmem_limit_bytes=56 * 2**20
        ),
        name=f"forward_{l}",
    )(x, ln, b_in, w1, w2, tab)


def backward_kernel(
    g_ref, x_ref, ln_ref, w1, w2, tab, nall_i, qkv_i, p_i, a2_i, pre_i,
    gn_ref, g1q, g1i, g2, lns, loc,
    gall, nall, qkv, prob, a2, pre, raw, dp,
    own, sibout, sibin, out, inn,
    ss, rs, sbs, sbr, rss, rsr, load,
):
    y, xl, z, xh, c = place()
    bar = pltpu.get_barrier_semaphore()
    greet_line(bar, z, c)
    pairs = ((nall_i, nall), (qkv_i, qkv), (p_i, prob), (a2_i, a2), (pre_i, pre))
    for i, (src, dst) in enumerate(pairs):
        local(src, dst, load.at[i])
    gall[2 * z + c] = g_ref[...].astype(BF)
    pl.semaphore_wait(bar, LINE - 1)
    rows_start(gall, z, c, ss, rs)
    for i in (1, 2, 4):
        landed(pairs[i][1], load.at[i])

    def step(k):
        zz = chip_of(z, k)
        rows_ready(k, gall, z, c, ss, rs)
        two = pl.ds(2 * zz, 2)
        g = gall[two].reshape(2 * CAP, D)
        raw[...] = nt(g, w2[...])

        def act(i):
            u, t = div(i, 12), rem(i, 12)
            rows = pl.ds(pl.multiple_of(t * 16, 16), 16)
            v = pre[2 * zz + u, rows, :]
            d = raw[pl.ds(pl.multiple_of(u * CAP + t * 16, 16), 16), 128:]
            t1 = jnp.tanh(C0 * (v + C1 * v * v * v))
            slope = 0.5 * (1.0 + t1) + 0.5 * v * (1.0 - t1 * t1) * (C0 + (3.0 * C0 * C1) * v * v)
            dp[2 * zz + u, rows, QKV:] = (d * slope).astype(BF)

        loop(24, act)
        for u in range(2):
            s = 2 * zz + u
            rows = slice(u * CAP, (u + 1) * CAP)
            cos, sin = tab[s, :, 0:128], tab[s, :, 128:256]
            m = raw[rows, 0:128].astype(BF)
            q, kk, v = qkv[s, :, 0:128], qkv[s, :, 128:256], qkv[s, :, 256:384]
            head = lanes((CAP, 128)) < HEAD
            dq, dk, dv = [], [], []
            for h in range(2):
                mine = head if h == 0 else ~head
                mh = jnp.where(mine, m, jnp.zeros_like(m))
                w = prob[2 * s + h]
                soft = nt(mh, v)
                dv.append(tn(w.astype(BF), mh))
                wd = w * soft
                ds = (wd - w * jnp.sum(wd, axis=-1, keepdims=True)).astype(BF)
                dq.append(nn(ds, kk))
                dk.append(tn(ds, jnp.where(mine, q, jnp.zeros_like(q))))
            scale = 1.0 / math.sqrt(HEAD)
            dq = jnp.where(head, dq[0], dq[1]) * scale
            dk = (dk[0] + dk[1]) * scale
            dp[s, :, 0:128] = turn(dq, cos, -sin).astype(BF)
            dp[s, :, 128:256] = turn(dk, cos, -sin).astype(BF)
            dp[s, :, 256:384] = (dv[0] + dv[1]).astype(BF)
        sums_send(
            k, zz, lambda s: nt(dp[s], w1[...]), c, own, sibout, sibin, out, inn, sbs, sbr, rss, rsr
        )

    loop(4, step)

    rows = LINE * CAP
    g = gall[...].reshape(rows, D)
    landed(a2, load.at[3])
    val = tn(a2[...].reshape(rows, DEEP), g)
    for s in range(2):
        for q in range(4):
            g2[s, q, 0:16, :] = val[64 * s + 16 * q : 64 * s + 16 * q + 16].astype(BF)
            base = 128 + 256 * s + 64 * q
            g2[s, q, 16:80, :] = val[base : base + 64].astype(BF)
    landed(nall, load.at[0])
    d = dp[...].reshape(rows, WIDE)
    for t in range(2):
        val = tn(nall[:, :, t * 512 : (t + 1) * 512].reshape(rows, 512), d).astype(BF)
        for s in range(8):
            sh = 8 * t + s
            zz, hh, cc = sh // 4, (sh // 2) % 2, sh % 2
            for q in range(4):
                part = val[64 * s + 16 * q : 64 * s + 16 * q + 16]
                at = (2 * zz + cc) * 16
                g1q[hh, q, at : at + 16, :] = part[:, :QKV]
                g1i[hh, q, at : at + 16, :] = part[:, QKV:]

    zero = jnp.zeros((1, 128), F32)
    col = pl.ds(pl.multiple_of((2 * z + c) * 128, 128), 128)
    bfc = jnp.zeros((1, 128), F32)
    b_in = jnp.zeros((1, HID), F32)
    for s in range(LINE):
        bfc = bfc + jnp.sum(gall[s, :, col].astype(F32), axis=0, keepdims=True)
        b_in = b_in + jnp.sum(dp[s, :, QKV:].astype(F32), axis=0, keepdims=True)
    loc[...] = jnp.concatenate(
        [zero, zero, bfc] + [b_in[:, 128 * i : 128 * i + 128] for i in range(4)] + [zero], axis=0
    )

    ngrad = sums_total(own, inn, rsr)
    centre, r = stats(x_ref[...])
    xhat = centre * r
    e = ngrad * ln_ref[0:1, :]
    ex = jnp.mean(e * xhat, axis=-1, keepdims=True)
    gn_ref[...] = g_ref[...] + r * (e - jnp.mean(e, axis=-1, keepdims=True) - xhat * ex)
    gain = jnp.sum(ngrad * xhat, axis=0, keepdims=True)
    bias = jnp.sum(ngrad, axis=0, keepdims=True)
    both = jnp.concatenate([gain, bias] + [jnp.zeros((6, D), F32)], axis=0)
    for i in range(LINE):
        lns[i] = both[:, 128 * i : 128 * i + 128]
    rows_left(gall, z, c, ss)
    sums_left(sibout, out, sbs, rss)


def backward_layer(l, g, x, ln, w1, w2, tab, saved):
    return pl.pallas_call(
        backward_kernel,
        out_shape=(
            jax.ShapeDtypeStruct((CAP, D), F32),
            jax.ShapeDtypeStruct((2, 4, 128, QKV), BF),
            jax.ShapeDtypeStruct((2, 4, 128, HID), BF),
            jax.ShapeDtypeStruct((2, 4, 80, D), BF),
            jax.ShapeDtypeStruct((LINE, 8, 128), F32),
            jax.ShapeDtypeStruct((8, 128), F32),
        ),
        in_specs=[INV] * 6 + [ANY] * 5,
        out_specs=(INV,) * 6,
        scratch_shapes=[VMEM((LINE, CAP, D), BF)]
        + [VMEM(s, t) for s, t in SAVED]
        + [VMEM((2 * CAP, DEEP), F32), VMEM((LINE, CAP, WIDE), BF)]
        + SUM_BUFFERS
        + ROW_SEMS
        + [DMA((5,))],
        compiler_params=pltpu.CompilerParams(
            collective_id=3 + l, has_side_effects=True, vmem_limit_bytes=60 * 2**20
        ),
        name=f"backward_{l}",
    )(g, x, ln, w1, w2, tab, *saved)


def reduce_kernel(
    g1q0, g1q1, g1i0, g1i1, g20, g21, lns0, lns1, loc0, loc1,
    fq, fi, fo, ff, fs,
    r1, r2, red1, red2, zs, ps, tot,
    s1, q1, s2, q2, s3, q3, s4, q4, s5, q5, s6, q6, s7, q7, s8, q8,
):
    y, xl, z, xh, c = place()
    x = 2 * xh + xl
    p = 4 * y + x
    j = 2 * z + c
    bar = pltpu.get_barrier_semaphore()
    greet_line(bar, z, c)
    greet_plane(bar, y, x)
    for k in range(1, 8):
        signal(bar, y=rem(y + k // 2, 4), xl=rem(xl + k % 2, 2), c=1 - c)
    pl.semaphore_wait(bar, 29)
    g1q, g1i, g2, lns, loc = (g1q0, g1q1), (g1i0, g1i1), (g20, g21), (lns0, lns1), (loc0, loc1)
    order = (1, 0)

    def member(jj):
        return dict(z=div(jj, 2), c=rem(jj, 2))

    for l in order:

        def small(k):
            jj = rem(j + k, LINE)
            send(lns[l].at[jj], zs.at[l, j], s5.at[l, k], q5.at[l, j], **member(jj))

        loop(LINE - 1, lambda k: small(k + 1))

    for l in order:

        def second(i):
            yy, cc = rem(y + div(i, 2), 4), rem(xl + rem(i, 2), 2)
            src, dst = g2[l].at[cc, yy], r2.at[l, p]
            here = (i == 0) & (xh == c)

            @pl.when(here)
            def _():
                local(src, dst, q2.at[l, p])

            @pl.when(jnp.logical_not(here))
            def _():
                send(src, dst, s2.at[l, i], q2.at[l, p], y=yy, xl=cc, xh=c)

        loop(8, second)

        def first(k):
            yy = rem(y + div(k, 4), 4)
            xx = rem(x + rem(k, 4), 4)
            hh, ll = div(xx, 2), rem(xx, 2)

            @pl.when(ll == 0)
            def _():
                dst = r1.at[l, p, :, pl.ds(0, QKV)]
                send(g1q[l].at[hh, yy], dst, s1.at[l, k], q1.at[l, p], y=yy, xh=hh, xl=ll)

            @pl.when(ll == 1)
            def _():
                send(g1i[l].at[hh, yy], r1.at[l, p], s1.at[l, k], q1.at[l, p], y=yy, xh=hh, xl=ll)

        loop(15, lambda k: first(k + 1))

        @pl.when(xl == 0)
        def _():
            local(g1q[l].at[xh, y], r1.at[l, p, :, pl.ds(0, QKV)], q1.at[l, p])

        @pl.when(xl == 1)
        def _():
            local(g1i[l].at[xh, y], r1.at[l, p], q1.at[l, p])

    for l in order:

        def small_in(k):
            jj = rem(j + k, LINE)
            landed(zs.at[l, jj], q5.at[l, jj])

        zs[l, j] = lns[l][j] + loc[l][...]
        loop(LINE - 1, lambda k: small_in(k + 1))
        total = zs[l, 0]
        for i in range(1, LINE):
            total = total + zs[l, i]
        ps[l, p] = total

        def spread(k):
            yy = rem(y + div(k, 4), 4)
            xx = rem(x + rem(k, 4), 4)
            dev = dict(y=yy, xh=div(xx, 2), xl=rem(xx, 2))
            send(ps.at[l, p], ps.at[l, p], s6.at[l, k], q6.at[l, p], **dev)

        loop(15, lambda k: spread(k + 1))

    row16 = pl.ds(pl.multiple_of(16 * y, 16), 16)
    row64 = pl.ds(pl.multiple_of(64 * y, 64), 64)
    for l in order:
        @pl.when(xh == c)
        def _():
            loop(16, lambda q: landed(r2.at[l, q], q2.at[l, q]))
            for t in range(5):
                rows = slice(16 * t, 16 * t + 16)
                acc = r2[l, 0, rows, :].astype(F32)
                for q in range(1, 16):
                    acc = acc + r2[l, q, rows, :].astype(F32)
                red2[l, rows, :] = acc.astype(BF)

            def out(i):
                yy, ll = rem(y + div(i, 2), 4), rem(xl + rem(i, 2), 2)
                here = (i == 0) & (xl == c)
                parts = (
                    (red2.at[l, pl.ds(0, 16)], fo.at[l, row16]),
                    (red2.at[l, pl.ds(16, 64)], ff.at[l, row64]),
                )
                for n, (src, dst) in enumerate(parts):

                    @pl.when(here)
                    def _():
                        local(src, dst, q4.at[l, y, n])

                    @pl.when(jnp.logical_not(here))
                    def _():
                        send(src, dst, s4.at[l, i, n], q4.at[l, y, n], y=yy, xl=ll, c=xl)

            loop(8, out)

        loop_in = functools.partial(arrive_first, l, xl, r1, q1)
        loop(16, loop_in)
        for t in range(8):
            rows = slice(16 * t, 16 * t + 16)
            acc = r1[l, 0, rows, :].astype(F32)
            for q in range(1, 16):
                acc = acc + r1[l, q, rows, :].astype(F32)
            red1[l, rows, :] = acc.astype(BF)

        def back(jj):
            rows = pl.ds(pl.multiple_of(16 * jj, 16), 16)
            cols = pl.ds(pl.multiple_of(HID * j, HID), HID)

            def move(src, dst, n):
                @pl.when(jj == j)
                def _():
                    local(src, dst, q3.at[l, j, n])

                @pl.when(jj != j)
                def _():
                    send(src, dst, s3.at[l, jj, n], q3.at[l, j, n], **member(jj))

            @pl.when(xl == 0)
            def _():
                for n in range(3):
                    at = pl.ds(pl.multiple_of(n * D + 128 * j, 128), 128)
                    move(red1.at[l, rows, pl.ds(128 * n, 128)], fq.at[l, row16, at], n)

            @pl.when(xl == 1)
            def _():
                move(red1.at[l, rows], fi.at[l, row16, cols], 0)

        loop(LINE, back)

    for l in order:

        def back_in(jj):
            @pl.when(xl == 0)
            def _():
                for n in range(3):
                    at = pl.ds(pl.multiple_of(n * D + 128 * jj, 128), 128)
                    landed(fq.at[l, row16, at], q3.at[l, jj, n])

            @pl.when(xl == 1)
            def _():
                at = pl.ds(pl.multiple_of(HID * jj, HID), HID)
                landed(fi.at[l, row16, at], q3.at[l, jj, 0])

        loop(LINE, back_in)

        def share(i):
            yy, ll = rem(y + div(i, 2), 4), rem(xl + rem(i, 2), 2)
            for v, f in ((0, fq), (1, fi)):

                @pl.when(xl == v)
                def _():
                    at = f.at[l, row16]
                    send(at, at, s7.at[l, i], q7.at[l, y, v], y=yy, xl=ll)

        loop(7, lambda i: share(i + 1))

    for l in order:

        def spread_in(k):
            q = rem(p + k, 16)
            landed(ps.at[l, q], q6.at[l, q])

        loop(15, lambda k: spread_in(k + 1))
        total = ps[l, 0]
        for i in range(1, 16):
            total = total + ps[l, i]
        tot[l, c] = total
        send(tot.at[l, c], tot.at[l, c], s8.at[l], q8.at[l], c=1 - c)
    for l in order:
        landed(tot.at[l, 1 - c], q8.at[l])
    fs[...] = tot[...]

    for l in order:
        for q in range(4):
            landed(fo.at[l, pl.ds(16 * q, 16)], q4.at[l, q, 0])
            landed(ff.at[l, pl.ds(64 * q, 64)], q4.at[l, q, 1])
            for v, f in ((0, fq), (1, fi)):

                @pl.when((xl != v) | (y != q))
                def _():
                    landed(f.at[l, pl.ds(16 * q, 16)], q7.at[l, q, v])

    for l in order:

        def left_line(k):
            landed(lns[l].at[0], s5.at[l, k])

        loop(LINE - 1, lambda k: left_line(k + 1))

        def left_second(i):
            @pl.when(jnp.logical_not((i == 0) & (xh == c)))
            def _():
                landed(r2.at[l, 0], s2.at[l, i])

            @pl.when((xh == c) & jnp.logical_not((i == 0) & (xl == c)))
            def _():
                landed(red2.at[l, pl.ds(0, 16)], s4.at[l, i, 0])
                landed(red2.at[l, pl.ds(16, 64)], s4.at[l, i, 1])

        loop(8, left_second)

        def left_first(k):
            ll = rem(rem(x + rem(k, 4), 4), 2)

            @pl.when(ll == 0)
            def _():
                landed(r1.at[l, 0, :, pl.ds(0, QKV)], s1.at[l, k])

            @pl.when(ll == 1)
            def _():
                landed(r1.at[l, 0], s1.at[l, k])

            landed(ps.at[l, 0], s6.at[l, k])

        loop(15, lambda k: left_first(k + 1))

        def left_back(jj):
            @pl.when((jj != j) & (xl == 0))
            def _():
                for n in range(3):
                    landed(red1.at[l, pl.ds(0, 16), pl.ds(0, 128)], s3.at[l, jj, n])

            @pl.when((jj != j) & (xl == 1))
            def _():
                landed(red1.at[l, pl.ds(0, 16)], s3.at[l, jj, 0])

        loop(LINE, left_back)

        def left_share(i):
            for v, f in ((0, fq), (1, fi)):

                @pl.when(xl == v)
                def _():
                    landed(f.at[l, row16], s7.at[l, i])

        loop(7, lambda i: left_share(i + 1))
        landed(tot.at[l, c], s8.at[l])


def arrive_first(l, xl, r1, q1, q):
    @pl.when(xl == 0)
    def _():
        landed(r1.at[l, q, :, pl.ds(0, QKV)], q1.at[l, q])

    @pl.when(xl == 1)
    def _():
        landed(r1.at[l, q], q1.at[l, q])


def reduce_all(first, second):
    args = [a for pair in zip(first, second) for a in pair]
    n = LAYERS
    return pl.pallas_call(
        reduce_kernel,
        out_shape=(
            jax.ShapeDtypeStruct((n, 64, 3 * D), BF),
            jax.ShapeDtypeStruct((n, 64, FF), BF),
            jax.ShapeDtypeStruct((n, 64, D), BF),
            jax.ShapeDtypeStruct((n, 256, D), BF),
            jax.ShapeDtypeStruct((n, 2, 8, 128), F32),
        ),
        in_specs=[ANY] * 6 + [INV] * 4,
        out_specs=(ANY,) * 4 + (INV,),
        scratch_shapes=[
            VMEM((n, 16, 128, HID), BF), VMEM((n, 16, 80, D), BF),
            VMEM((n, 128, HID), BF), VMEM((n, 80, D), BF),
            VMEM((n, LINE, 8, 128), F32), VMEM((n, 16, 8, 128), F32), VMEM((n, 2, 8, 128), F32),
            DMA((n, 16)), DMA((n, 16)),
            DMA((n, 8)), DMA((n, 16)),
            DMA((n, LINE, 3)), DMA((n, LINE, 3)),
            DMA((n, 8, 2)), DMA((n, 4, 2)),
            DMA((n, LINE)), DMA((n, LINE)),
            DMA((n, 16)), DMA((n, 16)),
            DMA((n, 8)), DMA((n, 4, 2)),
            DMA((n,)), DMA((n,)),
        ],
        compiler_params=pltpu.CompilerParams(
            collective_id=5, has_side_effects=True, vmem_limit_bytes=40 * 2**20
        ),
        name="reduce_all",
    )(*args)


def per_device(
    inputs, cotangent, lengths, ln_gain, ln_bias, w_qkv, w_attn_out, w_in, b_in, w_fc, b_fc
):
    z, xh, c = (lax.axis_index(a) for a in ("z", "xh", "c"))
    j = 2 * z + c
    offsets = jnp.arange(CAP, dtype=jnp.int32)
    seq_ends = jnp.cumsum(lengths[0])
    passed = (offsets[:, None] >= seq_ends[None, :]).astype(jnp.int32)
    segment = jnp.sum(passed, axis=1)
    start = jnp.sum(passed * lengths[0][None, :], axis=1)
    position = offsets - start
    frequency = 10000.0 ** (-jnp.arange(ROT // 2, dtype=F32) * 2.0 / ROT)
    angles = position.astype(F32)[:, None] * frequency
    cosine, sine = jnp.cos(angles), jnp.sin(angles)
    tab = jnp.concatenate(
        [cosine, cosine, -sine, sine, jnp.broadcast_to(start.astype(F32)[:, None], (CAP, 64))],
        axis=1,
    )
    wide = [jnp.pad(v, ((0, 0), (0, 256 - v.shape[1]))) for v in (ln_gain, ln_bias, b_fc, b_in)]
    sm = jnp.pad(jnp.stack(wide, axis=1), ((0, 0), (0, 4), (0, 0))).reshape(16, 256)

    w1, w2, sma, tabs = gather_weights(w_qkv, w_in, w_attn_out, w_fc, sm, tab)

    sma = sma.astype(F32)
    vec = sma.reshape(16, LAYERS, 8, 256)[:, :, :3, :64].transpose(1, 2, 0, 3).reshape(LAYERS, 3, D)
    vec = jnp.pad(vec, ((0, 0), (0, 5), (0, 0)))
    bins = lax.dynamic_slice(sma.reshape(16, LAYERS, 8, 256)[:, :, 3, :], (2 * j, 0, 0), (2, LAYERS, 256))
    bins = jnp.broadcast_to(bins.transpose(1, 0, 2).reshape(LAYERS, 1, HID), (LAYERS, 8, HID))
    one = jnp.ones((LINE, CAP, 32), F32)
    nil = jnp.zeros((LINE, CAP, 32), F32)
    cs, sn = tabs[:, :, 0:32], tabs[:, :, 32:64]
    table = jnp.concatenate(
        [cs, one, cs, one, sn, nil, sn, nil, tabs[:, :, 64:], tabs[:, :, 64:]], axis=-1
    )

    hidden = inputs
    kept = []
    for l in range(LAYERS):
        nxt, *saved = forward_layer(l, hidden, vec[l], bins[l], w1[l], w2[l], table)
        kept.append((hidden, saved))
        hidden = nxt
    grad = cotangent * (segment < SLOTS).astype(F32)[:, None]
    found = [None] * LAYERS
    for l in reversed(range(LAYERS)):
        grad, *found[l] = backward_layer(
            l, grad, kept[l][0], vec[l], w1[l], w2[l], table, kept[l][1]
        )
    fq, fi, fo, ff, fs = reduce_all(found[0], found[1])
    mine = lax.dynamic_index_in_dim(fs, xh, 1, keepdims=False)
    pick = lax.dynamic_slice(mine[:, 0:3], (0, 0, 64 * c), (LAYERS, 3, 64))
    b_in_grad = lax.dynamic_slice(mine[:, 3:7].reshape(LAYERS, HID), (0, 256 * c), (LAYERS, 256))
    return (
        hidden,
        grad,
        pick[:, 0],
        pick[:, 1],
        fq.astype(F32),
        fo.astype(F32),
        fi.astype(F32),
        b_in_grad,
        ff.astype(F32),
        pick[:, 2],
    )


def solution(mesh):
    fine = Mesh(mesh.devices.reshape(4, 2, 4, 2, 2), AXES)
    rows = P(AXES, None)
    shard = ("z", "xh", "c")
    vector, matrix = P(None, shard), P(None, shard, None)
    in_specs = (
        rows, rows, rows, vector, vector, matrix, matrix, matrix, vector, matrix, vector,
    )
    out_specs = (
        rows, rows, vector, vector, matrix, matrix, matrix, vector, matrix, vector,
    )
    return jax.shard_map(
        per_device, mesh=fine, in_specs=in_specs, out_specs=out_specs, check_vma=False
    )
```

```python
import functools
import math

import jax
import jax.numpy as jnp
from jax import lax
from jax.experimental import pallas as pl
from jax.experimental.pallas import tpu as pltpu
from jax.sharding import Mesh
from jax.sharding import PartitionSpec as P

D = 1024
HEADS = 16
HEAD = 64
ROT = 32
FF = 4096
LAYERS = 2
SLOTS = 4
CAP = 192
LINE = 8
QKV = 384
HID = 512
WIDE = QKV + HID
DEEP = 128 + HID
EPSILON = 1e-05
NEGATIVE = -1e30
AXES = ("y", "xl", "z", "xh", "c")
BF = jnp.bfloat16
F32 = jnp.float32
MESH = pl.DeviceIdType.MESH
VMEM = pltpu.VMEM
DMA = pltpu.SemaphoreType.DMA
ANY = pl.BlockSpec(memory_space=pl.ANY)
INV = pl.BlockSpec(memory_space=pltpu.VMEM)
C0 = 0.7978845608028654
C1 = 0.044715


def div(a, b):
    return lax.div(a, jnp.int32(b))


def rem(a, b):
    return lax.rem(a, jnp.int32(b))


def place():
    y, xl, z, xh, c = (lax.axis_index(a) for a in AXES)
    return y, xl, z, xh, c


def send(src, dst, ss, rs, **dev):
    cp = pltpu.make_async_remote_copy(
        src_ref=src, dst_ref=dst, send_sem=ss, recv_sem=rs, device_id=dev, device_id_type=MESH
    )
    cp.start()


def local(src, dst, sem):
    pltpu.make_async_copy(src, dst, sem).start()


def landed(ref, sem):
    pltpu.make_async_copy(ref, ref, sem).wait()


def loop(n, body):
    lax.fori_loop(0, n, lambda i, _: (body(i), 0)[1], 0)


def signal(sem, **dev):
    pl.semaphore_signal(sem, inc=1, device_id=dev, device_id_type=MESH)


def greet_line(bar, z, c):
    for k in range(1, LINE):
        j = rem(2 * z + c + k, LINE)
        signal(bar, z=div(j, 2), c=rem(j, 2))


def greet_plane(bar, y, x):
    for k in range(1, 16):
        yy = rem(y + k // 4, 4)
        xx = rem(x + k % 4, 4)
        signal(bar, y=yy, xh=div(xx, 2), xl=rem(xx, 2))


def gather_start(l, me, wqkv, win, wo, wfc, w1, w2, cs, cr, as_, ar):
    y, xl, z, xh, c, x, p, j = me
    mine = pl.ds(pl.multiple_of(64 * p, 64), 64)

    @pl.when((z == y) & (c == xl))
    def _():
        def to(jj):
            pairs = []
            for part in range(3):
                cols = pl.ds(pl.multiple_of(part * D + jj * 128, 128), 128)
                pairs.append((wqkv.at[l, :, cols], w1.at[l, mine, pl.ds(part * 128, 128)]))
            cols = pl.ds(pl.multiple_of(jj * HID, HID), HID)
            pairs.append((win.at[l, :, cols], w1.at[l, mine, pl.ds(QKV, HID)]))

            @pl.when(jj == j)
            def _():
                for i, (src, dst) in enumerate(pairs):
                    local(src, dst, ar.at[l, i])

            @pl.when(jj != j)
            def _():
                for i, (src, dst) in enumerate(pairs):
                    send(src, dst, as_.at[jj, l, i], ar.at[l, i], z=div(jj, 2), c=rem(jj, 2))

        loop(LINE, to)

    pieces = (
        (wo.at[l], w2.at[l, pl.ds(pl.multiple_of(64 * c, 64), 64)]),
        (wfc.at[l], w2.at[l, pl.ds(pl.multiple_of(128 + 256 * c, 64), 256)]),
    )
    for i, (src, dst) in enumerate(pieces):
        send(src, dst, cs.at[l, 0, i], cr.at[l, c, i], xl=1 - xl, xh=1 - xh, c=xh)

        @pl.when(c == xh)
        def _():
            local(src, dst, cr.at[l, c, i])

        @pl.when(c != xh)
        def _():
            send(src, dst, cs.at[l, 1, i], cr.at[l, c, i], c=xh)


def plane_member(y, x, k):
    xx = rem(x + rem(k, 4), 4)
    return dict(y=rem(y + div(k, 4), 4), xh=div(xx, 2), xl=rem(xx, 2))


def gather_plane(l, me, w1, ar, bs, br):
    y, xl, z, xh, c, x, p, j = me
    mine = pl.ds(pl.multiple_of(64 * p, 64), 64)
    for part in range(3):
        landed(w1.at[l, mine, pl.ds(part * 128, 128)], ar.at[l, part])
    landed(w1.at[l, mine, pl.ds(QKV, HID)], ar.at[l, 3])

    def across(k):
        block = w1.at[l, mine]
        send(block, block, bs.at[l, k], br.at[l, p], **plane_member(y, x, k))

    loop(15, lambda k: across(k + 1))


def gather_wait(l, me, w1, w2, cr, br):
    y, xl, z, xh, c, x, p, j = me

    def arrive(k):
        q = rem(p + k, 16)
        landed(w1.at[l, pl.ds(pl.multiple_of(64 * q, 64), 64)], br.at[l, q])

    loop(15, lambda k: arrive(k + 1))
    for s in range(2):
        landed(w2.at[l, pl.ds(64 * s, 64)], cr.at[l, s, 0])
        landed(w2.at[l, pl.ds(128 + 256 * s, 256)], cr.at[l, s, 1])


def gather_left(l, me, wqkv, win, wo, wfc, w1, cs, as_, bs):
    y, xl, z, xh, c, x, p, j = me
    loop(15, lambda k: landed(w1.at[l, pl.ds(0, 64)], bs.at[l, k + 1]))
    landed(wo.at[l], cs.at[l, 0, 0])
    landed(wfc.at[l], cs.at[l, 0, 1])

    @pl.when(c != xh)
    def _():
        landed(wo.at[l], cs.at[l, 1, 0])
        landed(wfc.at[l], cs.at[l, 1, 1])

    @pl.when((z == y) & (c == xl))
    def _():
        def gone(jj):
            @pl.when(jj != j)
            def _():
                for part in range(3):
                    landed(wqkv.at[l, :, pl.ds(part * D, 128)], as_.at[jj, l, part])
                landed(win.at[l, :, pl.ds(0, HID)], as_.at[jj, l, 3])

        loop(LINE, gone)


HALF = CAP // 2


def slot_of(z, c, k):
    return 2 * rem(z + k, 4) + c


def rows_start(buf, z, c, ss, rs):
    own = buf.at[2 * z + c]
    a, b = buf.at[2 * z + c, pl.ds(0, HALF)], buf.at[2 * z + c, pl.ds(HALF, HALF)]
    send(own, own, ss.at[0], rs.at[0], c=1 - c)
    up, down = dict(z=rem(z + 1, 4)), dict(z=rem(z + 3, 4))
    send(a, a, ss.at[1], rs.at[1], **up)
    send(b, b, ss.at[3], rs.at[3], **down)
    send(b, b, ss.at[2], rs.at[2], **up)
    send(a, a, ss.at[4], rs.at[4], **down)


def rows_near(buf, z, c, ss, rs):
    lo, hi = slot_of(z, c, 3), slot_of(z, c, 1)
    a = buf.at[lo, pl.ds(0, HALF)]
    b = buf.at[hi, pl.ds(HALF, HALF)]
    landed(a, rs.at[1])
    send(a, a, ss.at[5], rs.at[5], z=rem(z + 1, 4))
    landed(b, rs.at[3])
    send(b, b, ss.at[6], rs.at[6], z=rem(z + 3, 4))
    landed(b, rs.at[2])
    send(buf.at[lo], buf.at[lo], ss.at[7], rs.at[7], c=1 - c)
    landed(a, rs.at[4])
    send(buf.at[hi], buf.at[hi], ss.at[8], rs.at[8], c=1 - c)


def rows_far(buf, z, c, ss, rs):
    far = slot_of(z, c, 2)
    landed(buf.at[far, pl.ds(0, HALF)], rs.at[5])
    landed(buf.at[far, pl.ds(HALF, HALF)], rs.at[6])
    send(buf.at[far], buf.at[far], ss.at[9], rs.at[9], c=1 - c)


def rows_ready(k, buf, z, c, ss, rs):
    @pl.when(k == 0)
    def _():
        landed(buf.at[2 * z + 1 - c], rs.at[0])

    @pl.when(k == 1)
    def _():
        rows_near(buf, z, c, ss, rs)
        landed(buf.at[slot_of(z, 1 - c, 3)], rs.at[7])

    @pl.when(k == 2)
    def _():
        rows_far(buf, z, c, ss, rs)
        landed(buf.at[slot_of(z, 1 - c, 1)], rs.at[8])

    @pl.when(k == 3)
    def _():
        landed(buf.at[slot_of(z, 1 - c, 2)], rs.at[9])


def rows_left(buf, ss):
    for i in (0, 7, 8, 9):
        landed(buf.at[0], ss.at[i])
    for i in range(1, 7):
        landed(buf.at[0, pl.ds(0, HALF)], ss.at[i])


def chip_of(z, k):
    return rem(z + jnp.where(k == 1, 3, jnp.where(k == 0, 0, k - 1)), 4)


def sums_send(k, zz, partial, c, own, sibout, sibin, out, inn, sbs, sbr, rss, rsr):
    sibout[k] = partial(2 * zz + 1 - c).astype(BF)
    send(sibout.at[k], sibin.at[k], sbs.at[k], sbr.at[k], c=1 - c)
    term = partial(2 * zz + c)
    landed(sibin.at[k], sbr.at[k])
    term = term + sibin[k].astype(F32)

    @pl.when(k == 0)
    def _():
        own[...] = term

    @pl.when(k > 0)
    def _():
        out[k - 1] = term.astype(BF)
        send(out.at[k - 1], inn.at[k - 1], rss.at[k - 1], rsr.at[k - 1], z=zz)


def sums_total(own, inn, rsr):
    total = own[...]
    for i in range(3):
        landed(inn.at[i], rsr.at[i])
        total = total + inn[i].astype(F32)
    return total


def sums_left(sibout, out, sbs, rss):
    for i in range(4):
        landed(sibout.at[i], sbs.at[i])
    for i in range(3):
        landed(out.at[i], rss.at[i])


def lanes(shape):
    return lax.broadcasted_iota(jnp.int32, shape, len(shape) - 1)


def turn(v, cos, sin):
    low = rem(lanes(v.shape), 64) < 16
    partner = jnp.where(low, pltpu.roll(v, 112, 1), pltpu.roll(v, 16, 1))
    return v * cos + partner * sin


def nt(a, b):
    return lax.dot_general(a, b, (((1,), (1,)), ((), ())), preferred_element_type=F32)


def tn(a, b):
    return lax.dot_general(a, b, (((0,), (0,)), ((), ())), preferred_element_type=F32)


def nn(a, b):
    return jnp.dot(a, b, preferred_element_type=F32)


def stats(x):
    centre = x - jnp.mean(x, axis=-1, keepdims=True)
    r = lax.rsqrt(jnp.mean(centre * centre, axis=-1, keepdims=True) + EPSILON)
    return centre, r


def expand(t):
    lane = lanes(t.shape)
    rot = rem(lane, 64) < ROT
    first = lane < 64
    cos = jnp.where(rot, jnp.where(first, t, pltpu.roll(t, 64, 1)), 1.0)
    sin = jnp.where(rot, jnp.where(first, pltpu.roll(t, 96, 1), pltpu.roll(t, 32, 1)), 0.0)
    return cos, sin, t[:, 64:65]


def forward_pass(l, z, c, x, vec, bins, w1, w2, tabs, nall, qkv, prob, a2, pre, raw, sums, rows, spill):
    ss, rs = rows
    centre, r = stats(x[...])
    row = 8 * l
    nall[2 * z + c] = (centre * r * vec[row : row + 1, :] + vec[row + 1 : row + 2, :]).astype(BF)
    rows_start(nall, z, c, ss, rs)

    def step(k):
        zz = chip_of(z, k)
        rows_ready(k, nall, z, c, ss, rs)
        two = pl.ds(2 * zz, 2)
        n = nall[two].reshape(2 * CAP, D)
        raw[:, 0:QKV] = nn(n, w1[:, :QKV])
        pre[two] = (nn(n, w1[:, QKV:]) + bins[row : row + 1, :]).reshape(2, CAP, HID)

        def act(i):
            u, t = div(i, 6), rem(i, 6)
            at = pl.ds(pl.multiple_of(t * 32, 32), 32)
            v = pre[2 * zz + u, at, :]
            g = 0.5 * v * (1.0 + jnp.tanh(C0 * (v + C1 * v * v * v)))
            a2[2 * zz + u, at, 128:] = g.astype(BF)

        loop(12, act)
        for u in range(2):
            s = 2 * zz + u
            at = slice(u * CAP, (u + 1) * CAP)
            cos, sin, start = expand(tabs[s])
            q = turn(raw[at, 0:128], cos, sin).astype(BF)
            kk = turn(raw[at, 128:256], cos, sin).astype(BF)
            v = raw[at, 256:384].astype(BF)
            qkv[s, :, 0:128] = q
            qkv[s, :, 128:256] = kk
            qkv[s, :, 256:384] = v
            q = q * jnp.asarray(1.0 / math.sqrt(HEAD), BF)
            key_at = lanes((CAP, CAP))
            query_at = lax.broadcasted_iota(jnp.int32, (CAP, CAP), 0)
            allowed = (key_at >= start.astype(jnp.int32)) & (key_at <= query_at)
            head = lanes((CAP, 128)) < HEAD
            mixed = []
            for h in range(2):
                qh = jnp.where(head if h == 0 else ~head, q, jnp.zeros_like(q))
                score = jnp.where(allowed, nt(qh, kk), NEGATIVE)
                e = jnp.exp(score - jnp.max(score, axis=-1, keepdims=True))
                w = e / jnp.sum(e, axis=-1, keepdims=True)
                prob[2 * s + h] = w
                mixed.append(nn(w.astype(BF), v))
            a2[s, :, 0:128] = jnp.where(head, mixed[0], mixed[1]).astype(BF)
        if spill is not None:
            prob_o, pre_o, sem = spill
            local(prob.at[pl.ds(4 * zz, 4)], prob_o.at[pl.ds(4 * zz, 4)], sem.at[k, 0])
            local(pre.at[two], pre_o.at[two], sem.at[k, 1])
        sums_send(k, zz, lambda s: nn(a2[s], w2[...]), c, *sums)

    loop(4, step)
    own, _, _, out, inn, _, _, rss, rsr = sums
    return x[...] + (sums_total(own, inn, rsr) + vec[row + 2 : row + 3, :])


def backward_pass(
    l, z, c, g_ref, x, vec, w1, w2, tabs, nall, qkv, prob, a2, pre, raw, gall, dp,
    g1q, g1i, g2, lns, loc, sums, rows, hook,
):
    ss, rs = rows
    gall[2 * z + c] = g_ref[...].astype(BF)
    rows_start(gall, z, c, ss, rs)
    hook(0)

    def step(k):
        zz = chip_of(z, k)
        rows_ready(k, gall, z, c, ss, rs)
        two = pl.ds(2 * zz, 2)
        g = gall[two].reshape(2 * CAP, D)
        raw[...] = nt(g, w2[...])

        def act(i):
            u, t = div(i, 12), rem(i, 12)
            at = pl.ds(pl.multiple_of(t * 16, 16), 16)
            v = pre[2 * zz + u, at, :]
            d = raw[pl.ds(pl.multiple_of(u * CAP + t * 16, 16), 16), 128:]
            t1 = jnp.tanh(C0 * (v + C1 * v * v * v))
            slope = 0.5 * (1.0 + t1) + 0.5 * v * (1.0 - t1 * t1) * (C0 + (3.0 * C0 * C1) * v * v)
            dp[2 * zz + u, at, QKV:] = (d * slope).astype(BF)

        loop(24, act)
        for u in range(2):
            s = 2 * zz + u
            at = slice(u * CAP, (u + 1) * CAP)
            cos, sin, _ = expand(tabs[s])
            m = raw[at, 0:128].astype(BF)
            q, kk, v = qkv[s, :, 0:128], qkv[s, :, 128:256], qkv[s, :, 256:384]
            head = lanes((CAP, 128)) < HEAD
            dq, dk, dv = [], [], []
            for h in range(2):
                mine = head if h == 0 else ~head
                mh = jnp.where(mine, m, jnp.zeros_like(m))
                w = prob[2 * s + h]
                soft = nt(mh, v)
                dv.append(tn(w.astype(BF), mh))
                wd = w * soft
                ds = (wd - w * jnp.sum(wd, axis=-1, keepdims=True)).astype(BF)
                dq.append(nn(ds, kk))
                dk.append(tn(ds, jnp.where(mine, q, jnp.zeros_like(q))))
            scale = 1.0 / math.sqrt(HEAD)
            dq = jnp.where(head, dq[0], dq[1]) * scale
            dk = (dk[0] + dk[1]) * scale
            dp[s, :, 0:128] = turn(dq, cos, -sin).astype(BF)
            dp[s, :, 128:256] = turn(dk, cos, -sin).astype(BF)
            dp[s, :, 256:384] = (dv[0] + dv[1]).astype(BF)
        sums_send(k, zz, lambda s: nt(dp[s], w1[...]), c, *sums)

    loop(4, step)
    hook(1)

    rows = LINE * CAP
    g = gall[...].reshape(rows, D)
    val = tn(a2[...].reshape(rows, DEEP), g)
    for s in range(2):
        for q in range(4):
            g2[s, q, 0:16, :] = val[64 * s + 16 * q : 64 * s + 16 * q + 16].astype(BF)
            base = 128 + 256 * s + 64 * q
            g2[s, q, 16:80, :] = val[base : base + 64].astype(BF)
    hook(2)
    d = dp[...].reshape(rows, WIDE)
    for t in range(2):
        val = tn(nall[:, :, t * 512 : (t + 1) * 512].reshape(rows, 512), d).astype(BF)
        for s in range(8):
            sh = 8 * t + s
            zz, hh, cc = sh // 4, (sh // 2) % 2, sh % 2
            for q in range(4):
                part = val[64 * s + 16 * q : 64 * s + 16 * q + 16]
                at = (2 * zz + cc) * 16
                g1q[hh, q, at : at + 16, :] = part[:, :QKV]
                g1i[hh, q, at : at + 16, :] = part[:, QKV:]
    hook(3)

    zero = jnp.zeros((1, 128), F32)
    col = pl.ds(pl.multiple_of((2 * z + c) * 128, 128), 128)
    bfc = jnp.zeros((1, 128), F32)
    b_in = jnp.zeros((1, HID), F32)
    for s in range(LINE):
        bfc = bfc + jnp.sum(gall[s, :, col].astype(F32), axis=0, keepdims=True)
        b_in = b_in + jnp.sum(dp[s, :, QKV:].astype(F32), axis=0, keepdims=True)
    loc[...] = jnp.concatenate(
        [zero, zero, bfc] + [b_in[:, 128 * i : 128 * i + 128] for i in range(4)] + [zero], axis=0
    )
    own, _, _, out, inn, _, _, rss, rsr = sums
    ngrad = sums_total(own, inn, rsr)
    centre, r = stats(x[...])
    xhat = centre * r
    e = ngrad * vec[8 * l : 8 * l + 1, :]
    ex = jnp.mean(e * xhat, axis=-1, keepdims=True)
    gain = jnp.sum(ngrad * xhat, axis=0, keepdims=True)
    bias = jnp.sum(ngrad, axis=0, keepdims=True)
    both = jnp.concatenate([gain, bias] + [jnp.zeros((6, D), F32)], axis=0)
    for i in range(LINE):
        lns[i] = both[:, 128 * i : 128 * i + 128]
    return g_ref[...] + r * (e - jnp.mean(e, axis=-1, keepdims=True) - xhat * ex)


def member(jj):
    return dict(z=div(jj, 2), c=rem(jj, 2))


def small_start(l, me, lns, zs, s5, q5):
    j = me[7]

    def go(k):
        jj = rem(j + k, LINE)
        send(lns.at[l, jj], zs.at[l, j], s5.at[l, k], q5.at[l, j], **member(jj))

    loop(LINE - 1, lambda k: go(k + 1))


def small_spread(l, me, lns, loc, zs, ps, q5, s6, q6):
    y, xl, z, xh, c, x, p, j = me

    def small_in(k):
        jj = rem(j + k, LINE)
        landed(zs.at[l, jj], q5.at[l, jj])

    loop(LINE - 1, lambda k: small_in(k + 1))
    zs[l, j] = lns[l, j] + loc[l]
    total = zs[l, 0]
    for i in range(1, LINE):
        total = total + zs[l, i]
    ps[l, p] = total

    def spread(k):
        send(ps.at[l, p], ps.at[l, p], s6.at[l, k], q6.at[l, p], **plane_member(y, x, k))

    loop(15, lambda k: spread(k + 1))


def small_last(l, me, ps, tot, q6, s8, q8):
    y, xl, z, xh, c, x, p, j = me

    def spread_in(k):
        q = rem(p + k, 16)
        landed(ps.at[l, q], q6.at[l, q])

    loop(15, lambda k: spread_in(k + 1))
    total = ps[l, 0]
    for i in range(1, 16):
        total = total + ps[l, i]
    tot[l, c] = total
    send(tot.at[l, c], tot.at[l, c], s8.at[l], q8.at[l], c=1 - c)


def second_start(l, me, g2, r2, s2, q2):
    y, xl, z, xh, c, x, p, j = me

    def second(i):
        yy, cc = rem(y + div(i, 2), 4), rem(xl + rem(i, 2), 2)
        src, dst = g2.at[cc, yy], r2.at[l, p]
        here = (i == 0) & (xh == c)

        @pl.when(here)
        def _():
            local(src, dst, q2.at[l, p])

        @pl.when(jnp.logical_not(here))
        def _():
            send(src, dst, s2.at[l, i], q2.at[l, p], y=yy, xl=cc, xh=c)

    loop(8, second)


def first_start(l, me, g1q, g1i, r1, s1, q1):
    y, xl, z, xh, c, x, p, j = me

    def first(k):
        yy = rem(y + div(k, 4), 4)
        xx = rem(x + rem(k, 4), 4)
        hh, ll = div(xx, 2), rem(xx, 2)

        @pl.when(ll == 0)
        def _():
            dst = r1.at[l, p, :, pl.ds(0, QKV)]
            send(g1q.at[hh, yy], dst, s1.at[l, k], q1.at[l, p], y=yy, xh=hh, xl=ll)

        @pl.when(ll == 1)
        def _():
            send(g1i.at[hh, yy], r1.at[l, p], s1.at[l, k], q1.at[l, p], y=yy, xh=hh, xl=ll)

    loop(15, lambda k: first(k + 1))

    @pl.when(xl == 0)
    def _():
        local(g1q.at[xh, y], r1.at[l, p, :, pl.ds(0, QKV)], q1.at[l, p])

    @pl.when(xl == 1)
    def _():
        local(g1i.at[xh, y], r1.at[l, p], q1.at[l, p])


def second_sum(l, me, r2, red2, fo, ff, q2, s4, q4):
    y, xl, z, xh, c, x, p, j = me
    row16 = pl.ds(pl.multiple_of(16 * y, 16), 16)
    row64 = pl.ds(pl.multiple_of(64 * y, 64), 64)

    @pl.when(xh == c)
    def _():
        loop(16, lambda q: landed(r2.at[l, q], q2.at[l, q]))

        def add(t):
            at = pl.ds(pl.multiple_of(16 * t, 16), 16)
            acc = r2[l, 0, at, :].astype(F32)
            for q in range(1, 16):
                acc = acc + r2[l, q, at, :].astype(F32)
            red2[l, at, :] = acc.astype(BF)

        loop(5, add)

        def out(i):
            yy, ll = rem(y + div(i, 2), 4), rem(xl + rem(i, 2), 2)
            here = (i == 0) & (xl == c)
            parts = (
                (red2.at[l, pl.ds(0, 16)], fo.at[l, row16]),
                (red2.at[l, pl.ds(16, 64)], ff.at[l, row64]),
            )
            for n, (src, dst) in enumerate(parts):

                @pl.when(here)
                def _():
                    local(src, dst, q4.at[l, y, n])

                @pl.when(jnp.logical_not(here))
                def _():
                    send(src, dst, s4.at[l, i, n], q4.at[l, y, n], y=yy, xl=ll, c=xl)

        loop(8, out)


def first_sum(l, me, r1, red1, fq, fi, q1, s3, q3):
    y, xl, z, xh, c, x, p, j = me
    row16 = pl.ds(pl.multiple_of(16 * y, 16), 16)

    def arrive(q):
        @pl.when(xl == 0)
        def _():
            landed(r1.at[l, q, :, pl.ds(0, QKV)], q1.at[l, q])

        @pl.when(xl == 1)
        def _():
            landed(r1.at[l, q], q1.at[l, q])

    loop(16, arrive)

    def add(t):
        at = pl.ds(pl.multiple_of(16 * t, 16), 16)
        acc = r1[l, 0, at, :].astype(F32)
        for q in range(1, 16):
            acc = acc + r1[l, q, at, :].astype(F32)
        red1[l, at, :] = acc.astype(BF)

    loop(8, add)

    def back(jj):
        at = pl.ds(pl.multiple_of(16 * jj, 16), 16)

        def move(src, dst, n):
            @pl.when(jj == j)
            def _():
                local(src, dst, q3.at[l, j, n])

            @pl.when(jj != j)
            def _():
                send(src, dst, s3.at[l, jj, n], q3.at[l, j, n], **member(jj))

        @pl.when(xl == 0)
        def _():
            for n in range(3):
                cols = pl.ds(pl.multiple_of(n * D + 128 * j, 128), 128)
                move(red1.at[l, at, pl.ds(128 * n, 128)], fq.at[l, row16, cols], n)

        @pl.when(xl == 1)
        def _():
            cols = pl.ds(pl.multiple_of(HID * j, HID), HID)
            move(red1.at[l, at], fi.at[l, row16, cols], 0)

    loop(LINE, back)


def first_share(l, me, fq, fi, q3, s7, q7):
    y, xl, z, xh, c, x, p, j = me
    row16 = pl.ds(pl.multiple_of(16 * y, 16), 16)

    def back_in(jj):
        @pl.when(xl == 0)
        def _():
            for n in range(3):
                at = pl.ds(pl.multiple_of(n * D + 128 * jj, 128), 128)
                landed(fq.at[l, row16, at], q3.at[l, jj, n])

        @pl.when(xl == 1)
        def _():
            at = pl.ds(pl.multiple_of(HID * jj, HID), HID)
            landed(fi.at[l, row16, at], q3.at[l, jj, 0])

    loop(LINE, back_in)

    def share(i):
        yy, ll = rem(y + div(i, 2), 4), rem(xl + rem(i, 2), 2)
        for v, f in ((0, fq), (1, fi)):

            @pl.when(xl == v)
            def _():
                at = f.at[l, row16]
                send(at, at, s7.at[l, i], q7.at[l, y, v], y=yy, xl=ll)

    loop(7, lambda i: share(i + 1))


def owners_in(l, me, fq, fi, fo, ff, q4, q7):
    y, xl, z, xh, c, x, p, j = me
    for q in range(4):
        landed(fo.at[l, pl.ds(16 * q, 16)], q4.at[l, q, 0])
        landed(ff.at[l, pl.ds(64 * q, 64)], q4.at[l, q, 1])
        for v, f in ((0, fq), (1, fi)):

            @pl.when((xl != v) | (y != q))
            def _():
                landed(f.at[l, pl.ds(16 * q, 16)], q7.at[l, q, v])


def first_left(l, me, r1, s1):
    x = me[5]

    def go(k):
        ll = rem(rem(x + rem(k, 4), 4), 2)

        @pl.when(ll == 0)
        def _():
            landed(r1.at[l, 0, :, pl.ds(0, QKV)], s1.at[l, k])

        @pl.when(ll == 1)
        def _():
            landed(r1.at[l, 0], s1.at[l, k])

    loop(15, lambda k: go(k + 1))


def second_left(l, me, r2, s2):
    y, xl, z, xh, c, x, p, j = me

    def go(i):
        @pl.when(jnp.logical_not((i == 0) & (xh == c)))
        def _():
            landed(r2.at[l, 0], s2.at[l, i])

    loop(8, go)


def owners_left(l, me, lns, ps, tot, red1, red2, fq, fi, s3, s4, s5, s6, s7, s8):
    y, xl, z, xh, c, x, p, j = me
    row16 = pl.ds(pl.multiple_of(16 * y, 16), 16)
    loop(LINE - 1, lambda k: landed(lns.at[l, 0], s5.at[l, k + 1]))
    loop(15, lambda k: landed(ps.at[l, 0], s6.at[l, k + 1]))

    def left_second(i):
        @pl.when((xh == c) & jnp.logical_not((i == 0) & (xl == c)))
        def _():
            landed(red2.at[l, pl.ds(0, 16)], s4.at[l, i, 0])
            landed(red2.at[l, pl.ds(16, 64)], s4.at[l, i, 1])

    loop(8, left_second)

    def left_back(jj):
        @pl.when((jj != j) & (xl == 0))
        def _():
            for n in range(3):
                landed(red1.at[l, pl.ds(0, 16), pl.ds(0, 128)], s3.at[l, jj, n])

        @pl.when((jj != j) & (xl == 1))
        def _():
            landed(red1.at[l, pl.ds(0, 16)], s3.at[l, jj, 0])

    loop(LINE, left_back)

    def left_share(i):
        for v, f in ((0, fq), (1, fi)):

            @pl.when(xl == v)
            def _():
                landed(f.at[l, row16], s7.at[l, i])

    loop(7, lambda i: left_share(i + 1))
    landed(tot.at[l, c], s8.at[l])


def whole_kernel(
    wqkv, win, wo, wfc, sm, tab, x0, cot,
    x2_ref, g0_ref, fs_ref, fq, fi, fo, ff, prob_o, pre_o,
    w1, w2, sma, tabs, vec, bins,
    nall, qkv, a2, prob, pre, raw, gall, dp, x1,
    own, sibout, sibin, out, inn,
    g1q, g1i, g2, lns, loc, r1, r2, red1, red2, zs, ps, tot,
    cs, cr, as_, ar, bs, br, ts, tr, ms, mr, ns, nr,
    rows_s, rows_r, sbs, sbr, rss, rsr, spill, fill,
    s1, q1, s2, q2, s3, q3, s4, q4, s5, q5, s6, q6, s7, q7, s8, q8,
):
    y, xl, z, xh, c = place()
    x = 2 * xh + xl
    p = 4 * y + x
    j = 2 * z + c
    me = (y, xl, z, xh, c, x, p, j)
    bar = pltpu.get_barrier_semaphore()
    greet_line(bar, z, c)
    greet_plane(bar, y, x)
    for k in range(1, 8):
        signal(bar, y=rem(y + k // 2, 4), xl=rem(xl + k % 2, 2), c=1 - c)
    signal(bar, xl=1 - xl, xh=1 - xh, c=1 - c)
    pl.semaphore_wait(bar, 30)

    source = (z == y) & (c == xl)

    @pl.when(source)
    def _():
        def to(jj):
            @pl.when(jj == j)
            def _():
                local(sm, sma.at[p], mr)

            @pl.when(jj != j)
            def _():
                send(sm, sma.at[p], ms.at[jj], mr, **member(jj))

        loop(LINE, to)

    for l in range(LAYERS):
        gather_start(l, me, wqkv, win, wo, wfc, w1, w2, cs, cr, as_, ar)
    for k in range(1, LINE):
        jj = rem(j + k, LINE)
        send(tab, tabs.at[j], ts.at[k], tr.at[j], **member(jj))
    local(tab, tabs.at[j], tr.at[j])
    landed(sma.at[p], mr)

    def small_out(k):
        send(sma.at[p], sma.at[p], ns.at[k], nr.at[p], **plane_member(y, x, k))

    loop(15, lambda k: small_out(k + 1))
    gather_plane(0, me, w1, ar, bs, br)

    def small_in(k):
        q = rem(p + k, 16)
        landed(sma.at[q], nr.at[q])

    loop(15, lambda k: small_in(k + 1))
    half = lanes((16, 128)) < 64
    for t in range(8):
        vec[:, 128 * t : 128 * t + 128] = jnp.where(half, sma[2 * t, :, :128], sma[2 * t + 1, :, :128])
    for l in range(LAYERS):
        at = 8 * l + 3
        bins[8 * l : 8 * l + 1, 0:256] = sma[2 * j, at : at + 1, :]
        bins[8 * l : 8 * l + 1, 256:512] = sma[2 * j + 1, at : at + 1, :]

    def sums_of(n):
        return (
            own, sibout, sibin, out, inn, sbs.at[n], sbr.at[n], rss.at[n], rsr.at[n],
        )

    def rows_of(n):
        return rows_s.at[n], rows_r.at[n]

    def done(n, buf):
        rows_left(buf, rows_s.at[n])
        sums_left(sibout, out, sbs.at[n], rss.at[n])

    loop(LINE, lambda k: landed(tabs.at[k], tr.at[k]))
    gather_wait(0, me, w1, w2, cr, br)
    gather_plane(1, me, w1, ar, bs, br)
    x1[...] = forward_pass(
        0, z, c, x0, vec, bins, w1.at[0], w2.at[0], tabs, nall.at[0], qkv.at[0], prob, a2.at[0], pre,
        raw, sums_of(0), rows_of(0), (prob_o, pre_o, spill),
    )
    done(0, nall.at[0])
    for k in range(4):
        landed(prob.at[pl.ds(0, 4)], spill.at[k, 0])
        landed(pre.at[pl.ds(0, 2)], spill.at[k, 1])
    gather_wait(1, me, w1, w2, cr, br)
    x2_ref[...] = forward_pass(
        1, z, c, x1, vec, bins, w1.at[1], w2.at[1], tabs, nall.at[1], qkv.at[1], prob, a2.at[1], pre,
        raw, sums_of(1), rows_of(1), None,
    )
    done(1, nall.at[1])
    g0_ref[...] = cot[...] * tab[:, 96:97]

    def hook1(n):
        if n == 1:
            local(prob_o, prob, fill.at[0])
            local(pre_o, pre, fill.at[1])
        if n == 2:
            second_start(1, me, g2, r2, s2, q2)
        if n == 3:
            first_start(1, me, g1q, g1i, r1, s1, q1)

    g0_ref[...] = backward_pass(
        1, z, c, g0_ref, x1, vec, w1.at[1], w2.at[1], tabs, nall.at[1], qkv.at[1], prob, a2.at[1], pre,
        raw, gall.at[1], dp, g1q, g1i, g2, lns.at[1], loc.at[1], sums_of(2), rows_of(2), hook1,
    )
    done(2, gall.at[1])
    small_start(1, me, lns, zs, s5, q5)

    def hook0(n):
        if n == 0:
            landed(prob, fill.at[0])
            landed(pre, fill.at[1])
        if n == 1:
            small_spread(1, me, lns, loc, zs, ps, q5, s6, q6)
            second_sum(1, me, r2, red2, fo, ff, q2, s4, q4)
            second_left(1, me, r2, s2)
        if n == 2:
            second_start(0, me, g2, r2, s2, q2)
            first_sum(1, me, r1, red1, fq, fi, q1, s3, q3)
            first_left(1, me, r1, s1)
        if n == 3:
            first_start(0, me, g1q, g1i, r1, s1, q1)

    g0_ref[...] = backward_pass(
        0, z, c, g0_ref, x0, vec, w1.at[0], w2.at[0], tabs, nall.at[0], qkv.at[0], prob, a2.at[0], pre,
        raw, gall.at[0], dp, g1q, g1i, g2, lns.at[0], loc.at[0], sums_of(3), rows_of(3), hook0,
    )
    small_start(0, me, lns, zs, s5, q5)
    done(3, gall.at[0])
    first_share(1, me, fq, fi, q3, s7, q7)
    small_last(1, me, ps, tot, q6, s8, q8)
    small_spread(0, me, lns, loc, zs, ps, q5, s6, q6)
    second_sum(0, me, r2, red2, fo, ff, q2, s4, q4)
    first_sum(0, me, r1, red1, fq, fi, q1, s3, q3)
    first_share(0, me, fq, fi, q3, s7, q7)
    small_last(0, me, ps, tot, q6, s8, q8)
    for l in (1, 0):
        landed(tot.at[l, 1 - c], q8.at[l])
        fs_ref[l] = tot[l]
        owners_in(l, me, fq, fi, fo, ff, q4, q7)
    second_left(0, me, r2, s2)
    first_left(0, me, r1, s1)
    for l in range(LAYERS):
        owners_left(l, me, lns, ps, tot, red1, red2, fq, fi, s3, s4, s5, s6, s7, s8)
        gather_left(l, me, wqkv, win, wo, wfc, w1, cs, as_, bs)
    for k in range(1, LINE):
        landed(tab, ts.at[k])
    loop(15, lambda k: landed(sma.at[0], ns.at[k + 1]))

    @pl.when(source)
    def _():
        def gone(jj):
            @pl.when(jj != j)
            def _():
                landed(sm, ms.at[jj])

        loop(LINE, gone)


def whole(wqkv, win, wo, wfc, sm, tab, x0, cot):
    n = LAYERS
    return pl.pallas_call(
        whole_kernel,
        out_shape=(
            jax.ShapeDtypeStruct((CAP, D), F32),
            jax.ShapeDtypeStruct((CAP, D), F32),
            jax.ShapeDtypeStruct((n, 2, 8, 128), F32),
            jax.ShapeDtypeStruct((n, 64, 3 * D), BF),
            jax.ShapeDtypeStruct((n, 64, FF), BF),
            jax.ShapeDtypeStruct((n, 64, D), BF),
            jax.ShapeDtypeStruct((n, 256, D), BF),
            jax.ShapeDtypeStruct((2 * LINE, CAP, CAP), F32),
            jax.ShapeDtypeStruct((LINE, CAP, HID), F32),
        ),
        in_specs=[ANY] * 4 + [INV] * 4,
        out_specs=(INV,) * 3 + (ANY,) * 6,
        scratch_shapes=[
            VMEM((n, D, WIDE), BF), VMEM((n, DEEP, D), BF), VMEM((16, 16, 256), F32),
            VMEM((LINE, CAP, 128), F32), VMEM((16, D), F32), VMEM((16, HID), F32),
            VMEM((n, LINE, CAP, D), BF), VMEM((n, LINE, CAP, QKV), BF), VMEM((n, LINE, CAP, DEEP), BF),
            VMEM((2 * LINE, CAP, CAP), F32), VMEM((LINE, CAP, HID), F32), VMEM((2 * CAP, DEEP), F32),
            VMEM((n, LINE, CAP, D), BF), VMEM((LINE, CAP, WIDE), BF),
            VMEM((CAP, D), F32),
            VMEM((CAP, D), F32), VMEM((4, CAP, D), BF), VMEM((4, CAP, D), BF),
            VMEM((3, CAP, D), BF), VMEM((3, CAP, D), BF),
            VMEM((2, 4, 128, QKV), BF), VMEM((2, 4, 128, HID), BF), VMEM((2, 4, 80, D), BF),
            VMEM((n, LINE, 8, 128), F32), VMEM((n, 8, 128), F32),
            VMEM((n, 16, 128, HID), BF), VMEM((n, 16, 80, D), BF),
            VMEM((n, 128, HID), BF), VMEM((n, 80, D), BF),
            VMEM((n, LINE, 8, 128), F32), VMEM((n, 16, 8, 128), F32), VMEM((n, 2, 8, 128), F32),
            DMA((n, 2, 2)), DMA((n, 2, 2)), DMA((LINE, n, 4)), DMA((n, 4)),
            DMA((n, 16)), DMA((n, 16)), DMA((LINE,)), DMA((LINE,)),
            DMA((LINE,)), DMA, DMA((16,)), DMA((16,)),
            DMA((4, 10)), DMA((4, 10)), DMA((4, 4)), DMA((4, 4)), DMA((4, 3)), DMA((4, 3)),
            DMA((4, 2)), DMA((2,)),
            DMA((n, 16)), DMA((n, 16)),
            DMA((n, 8)), DMA((n, 16)),
            DMA((n, LINE, 3)), DMA((n, LINE, 3)),
            DMA((n, 8, 2)), DMA((n, 4, 2)),
            DMA((n, LINE)), DMA((n, LINE)),
            DMA((n, 16)), DMA((n, 16)),
            DMA((n, 8)), DMA((n, 4, 2)),
            DMA((n,)), DMA((n,)),
        ],
        compiler_params=pltpu.CompilerParams(
            collective_id=0, has_side_effects=True, vmem_limit_bytes=63 * 2**20
        ),
        name="whole",
    )(wqkv, win, wo, wfc, sm, tab, x0, cot)


def per_device(
    inputs, cotangent, lengths, ln_gain, ln_bias, w_qkv, w_attn_out, w_in, b_in, w_fc, b_fc
):
    xh, c = (lax.axis_index(a) for a in ("xh", "c"))
    offsets = jnp.arange(CAP, dtype=jnp.int32)
    seq_ends = jnp.cumsum(lengths[0])
    passed = (offsets[:, None] >= seq_ends[None, :]).astype(jnp.int32)
    segment = jnp.sum(passed, axis=1)
    start = jnp.sum(passed * lengths[0][None, :], axis=1)
    position = offsets - start
    frequency = 10000.0 ** (-jnp.arange(ROT // 2, dtype=F32) * 2.0 / ROT)
    angles = position.astype(F32)[:, None] * frequency
    cosine, sine = jnp.cos(angles), jnp.sin(angles)
    valid = (segment < SLOTS).astype(F32)
    tab = jnp.concatenate(
        [cosine, cosine, -sine, sine]
        + [jnp.broadcast_to(v[:, None], (CAP, 32)) for v in (start.astype(F32), valid)],
        axis=1,
    )
    wide = [jnp.concatenate([v] * (256 // v.shape[1]), axis=1) for v in (ln_gain, ln_bias, b_fc, b_in)]
    sm = jnp.stack(wide + [jnp.zeros_like(b_in)] * 4, axis=1).reshape(16, 256).astype(F32)

    hidden, grad, fs, fq, fi, fo, ff, _, _ = whole(
        w_qkv, w_in, w_attn_out, w_fc, sm, tab, inputs, cotangent
    )
    mine = lax.dynamic_index_in_dim(fs, xh, 1, keepdims=False)
    pick = lax.dynamic_slice(mine[:, 0:3], (0, 0, 64 * c), (LAYERS, 3, 64))
    b_in_grad = lax.dynamic_slice(mine[:, 3:7].reshape(LAYERS, HID), (0, 256 * c), (LAYERS, 256))
    return (
        hidden,
        grad,
        pick[:, 0],
        pick[:, 1],
        fq.astype(F32),
        fo.astype(F32),
        fi.astype(F32),
        b_in_grad,
        ff.astype(F32),
        pick[:, 2],
    )


def solution(mesh):
    fine = Mesh(mesh.devices.reshape(4, 2, 4, 2, 2), AXES)
    rows = P(AXES, None)
    shard = ("z", "xh", "c")
    vector, matrix = P(None, shard), P(None, shard, None)
    in_specs = (
        rows, rows, rows, vector, vector, matrix, matrix, matrix, vector, matrix, vector,
    )
    out_specs = (
        rows, rows, vector, vector, matrix, matrix, matrix, vector, matrix, vector,
    )
    return jax.shard_map(
        per_device, mesh=fine, in_specs=in_specs, out_specs=out_specs, check_vma=False
    )
```

```python
import functools
import math

import jax
import jax.numpy as jnp
from jax import lax
from jax.experimental import pallas as pl
from jax.experimental.pallas import tpu as pltpu
from jax.sharding import Mesh
from jax.sharding import PartitionSpec as P

D = 1024
HEADS = 16
HEAD = 64
ROT = 32
FF = 4096
LAYERS = 2
SLOTS = 4
CAP = 192
LINE = 8
QKV = 384
HID = 512
WIDE = QKV + HID
DEEP = 128 + HID
EPSILON = 1e-05
NEGATIVE = -1e30
AXES = ("y", "xl", "z", "xh", "c")
BF = jnp.bfloat16
F32 = jnp.float32
MESH = pl.DeviceIdType.MESH
VMEM = pltpu.VMEM
DMA = pltpu.SemaphoreType.DMA
ANY = pl.BlockSpec(memory_space=pl.ANY)
INV = pl.BlockSpec(memory_space=pltpu.VMEM)
C0 = 0.7978845608028654
C1 = 0.044715


def div(a, b):
    return lax.div(a, jnp.int32(b))


def rem(a, b):
    return lax.rem(a, jnp.int32(b))


def place():
    y, xl, z, xh, c = (lax.axis_index(a) for a in AXES)
    return y, xl, z, xh, c


def send(src, dst, ss, rs, **dev):
    cp = pltpu.make_async_remote_copy(
        src_ref=src, dst_ref=dst, send_sem=ss, recv_sem=rs, device_id=dev, device_id_type=MESH
    )
    cp.start()


def local(src, dst, sem):
    pltpu.make_async_copy(src, dst, sem).start()


def landed(ref, sem):
    pltpu.make_async_copy(ref, ref, sem).wait()


def loop(n, body):
    lax.fori_loop(0, n, lambda i, _: (body(i), 0)[1], 0)


def signal(sem, **dev):
    pl.semaphore_signal(sem, inc=1, device_id=dev, device_id_type=MESH)


def greet_line(bar, z, c):
    for k in range(1, LINE):
        j = rem(2 * z + c + k, LINE)
        signal(bar, z=div(j, 2), c=rem(j, 2))


def greet_plane(bar, y, x):
    for k in range(1, 16):
        yy = rem(y + k // 4, 4)
        xx = rem(x + k % 4, 4)
        signal(bar, y=yy, xh=div(xx, 2), xl=rem(xx, 2))


def rows64(q):
    return pl.ds(pl.multiple_of(64 * q, 64), 64)


def second_rows(s, y):
    return (
        pl.ds(pl.multiple_of(64 * s + 16 * y, 16), 16),
        pl.ds(pl.multiple_of(128 + 256 * s + 64 * y, 16), 64),
    )


def half_cols(h):
    return pl.ds(pl.multiple_of(512 * h, 512), 512)


PARTS = (pl.ds(QKV, HID), pl.ds(0, QKV))


def weights_z(l, me, wqkv, win, wo, wfc, w1, w2, as_, ar, cs, cr):
    y, xl, z, xh, c, x, p, j = me
    mine = rows64(p)

    @pl.when((z == y) & (c == xl))
    def _():
        def to(jj):
            pairs = []
            for part in range(3):
                cols = pl.ds(pl.multiple_of(part * D + jj * 128, 128), 128)
                pairs.append((wqkv.at[l, :, cols], w1.at[l, mine, pl.ds(part * 128, 128)]))
            cols = pl.ds(pl.multiple_of(jj * HID, HID), HID)
            pairs.append((win.at[l, :, cols], w1.at[l, mine, PARTS[0]]))

            @pl.when(jj == j)
            def _():
                for i, (src, dst) in enumerate(pairs):
                    local(src, dst, ar.at[l, i])

            @pl.when(jj != j)
            def _():
                for i, (src, dst) in enumerate(pairs):
                    send(src, dst, as_.at[jj, l, i], ar.at[l, i], z=div(jj, 2), c=rem(jj, 2))

        loop(LINE, to)

    quarter = (pl.ds(pl.multiple_of(16 * y, 16), 16), pl.ds(pl.multiple_of(64 * y, 64), 64))
    whole_rows = (
        pl.ds(pl.multiple_of(64 * c, 64), 64), pl.ds(pl.multiple_of(128 + 256 * c, 64), 256)
    )
    place_rows = second_rows(c, y)
    for i, w in enumerate((wo, wfc)):
        cols = half_cols(xl)
        dst = w2.at[l, place_rows[i], cols]
        send(
            w.at[l, quarter[i], cols], dst, cs.at[l, 0, i], cr.at[l, c, i], xl=1 - xl, xh=1 - xh, c=xh
        )
        full = w2.at[l, whole_rows[i]]

        @pl.when(c == xh)
        def _():
            local(w.at[l], full, cr.at[l, c, i])

        @pl.when(c != xh)
        def _():
            send(w.at[l], full, cs.at[l, 1, i], cr.at[l, c, i], c=xh)


def along_y(y, d):
    return dict(y=rem(y + d, 4))


def along_x(x, d):
    xx = rem(x + d, 4)
    return dict(xh=div(xx, 2), xl=rem(xx, 2))


def plane_member(y, x, k):
    return {**along_y(y, div(k, 4)), **along_x(x, rem(k, 4))}


def pass_block(l, part, q, b, stage, me, w1, bs, br):
    y, xl, z, xh, c, x, p, j = me
    block = w1.at[l, rows64(q), PARTS[part]]
    for d in (1, 2, 3):
        first = along_y(y, d) if part == 0 else along_x(x, d)
        second = along_x(x, d) if part == 0 else along_y(y, d)
        dev = first if stage == 0 else second
        at = d - 1 + (0 if stage == 0 else 3 + 3 * b)
        send(block, block, bs.at[l, part, at], br.at[l, q, part], **dev)


def weights_p1(l, me, w1, ar, bs, br):
    y, xl, z, xh, c, x, p, j = me
    for part in range(3):
        landed(w1.at[l, rows64(p), pl.ds(part * 128, 128)], ar.at[l, part])
    landed(w1.at[l, rows64(p), PARTS[0]], ar.at[l, 3])
    for part in range(2):
        pass_block(l, part, p, 0, 0, me, w1, bs, br)
    for part in range(2):
        pass_block(l, part, p, 0, 1, me, w1, bs, br)


def weights_p2(l, me, w1, bs, br):
    y, xl, z, xh, c, x, p, j = me
    for b in (1, 3, 2):
        for part in range(2):
            q = 4 * rem(y + b, 4) + x if part == 0 else 4 * y + rem(x + b, 4)
            landed(w1.at[l, rows64(q), PARTS[part]], br.at[l, q, part])
            pass_block(l, part, q, b, 1, me, w1, bs, br)


def weights_f1(l, me, w2, cr, xs, xr):
    y, xl, z, xh, c, x, p, j = me

    @pl.when(xh != c)
    def _():
        for s in range(2):
            for i, at in enumerate(second_rows(s, y)):
                block = w2.at[l, at, half_cols(1 - xl)]
                landed(block, cr.at[l, s, i])
                send(block, block, xs.at[l, s, i], xr.at[l, s, i], xl=1 - xl)


def weights_f2(l, me, w2, xr, ys, yr):
    y, xl, z, xh, c, x, p, j = me

    @pl.when(xh != c)
    def _():
        for s in range(2):
            for i, at in enumerate(second_rows(s, y)):
                landed(w2.at[l, at, half_cols(xl)], xr.at[l, s, i])
                block = w2.at[l, at]
                for d in (1, 2, 3):
                    send(block, block, ys.at[l, d, s, i], yr.at[l, y, s, i], **along_y(y, d))


def weights_in1(l, me, w1, br):
    y, xl, z, xh, c, x, p, j = me

    def arrive(k):
        b, d = div(k, 4), rem(k, 4)
        q = 4 * rem(y + b, 4) + rem(x + d, 4)

        @pl.when(d != 0)
        def _():
            landed(w1.at[l, rows64(q), PARTS[0]], br.at[l, q, 0])

        @pl.when(b != 0)
        def _():
            landed(w1.at[l, rows64(q), PARTS[1]], br.at[l, q, 1])

    loop(16, arrive)


def weights_in2(l, me, w2, cr, yr):
    y, xl, z, xh, c, x, p, j = me

    @pl.when(xh == c)
    def _():
        for s in range(2):
            landed(w2.at[l, pl.ds(64 * s, 64)], cr.at[l, s, 0])
            landed(w2.at[l, pl.ds(128 + 256 * s, 256)], cr.at[l, s, 1])

    @pl.when(xh != c)
    def _():
        def arrive(k):
            yy = rem(y + k, 4)
            for s in range(2):
                for i, at in enumerate(second_rows(s, yy)):
                    landed(w2.at[l, at], yr.at[l, yy, s, i])

        loop(3, lambda k: arrive(k + 1))


def weights_left(l, me, wqkv, win, wo, wfc, w1, w2, as_, cs, bs, xs, ys):
    y, xl, z, xh, c, x, p, j = me
    for part in range(2):
        loop(15, lambda k: landed(w1.at[l, pl.ds(0, 64), PARTS[part]], bs.at[l, part, k]))
    for i, n in enumerate((16, 64)):
        landed(w2.at[l, pl.ds(0, n), pl.ds(0, 512)], cs.at[l, 0, i])

    @pl.when(c != xh)
    def _():
        landed(wo.at[l], cs.at[l, 1, 0])
        landed(wfc.at[l], cs.at[l, 1, 1])
        for s in range(2):
            for i, n in enumerate((16, 64)):
                landed(w2.at[l, pl.ds(0, n), pl.ds(0, 512)], xs.at[l, s, i])
                for d in (1, 2, 3):
                    landed(w2.at[l, pl.ds(0, n)], ys.at[l, d, s, i])

    @pl.when((z == y) & (c == xl))
    def _():
        def gone(jj):
            @pl.when(jj != j)
            def _():
                for part in range(3):
                    landed(wqkv.at[l, :, pl.ds(part * D, 128)], as_.at[jj, l, part])
                landed(win.at[l, :, pl.ds(0, HID)], as_.at[jj, l, 3])

        loop(LINE, gone)


HALF = CAP // 2


def slot_of(z, c, k):
    return 2 * rem(z + k, 4) + c


def rows_sibling(buf, z, c, ss, rs):
    own = buf.at[2 * z + c]
    send(own, own, ss.at[0], rs.at[0], c=1 - c)


def rows_send(buf, z, c, ss, rs):
    a, b = buf.at[2 * z + c, pl.ds(0, HALF)], buf.at[2 * z + c, pl.ds(HALF, HALF)]
    up, down = dict(z=rem(z + 1, 4)), dict(z=rem(z + 3, 4))
    send(a, a, ss.at[1], rs.at[1], **up)
    send(b, b, ss.at[3], rs.at[3], **down)
    send(b, b, ss.at[2], rs.at[2], **up)
    send(a, a, ss.at[4], rs.at[4], **down)


def rows_pass(buf, z, c, ss, rs):
    lo, hi = slot_of(z, c, 3), slot_of(z, c, 1)
    a = buf.at[lo, pl.ds(0, HALF)]
    b = buf.at[hi, pl.ds(HALF, HALF)]
    landed(a, rs.at[1])
    send(a, a, ss.at[5], rs.at[5], z=rem(z + 1, 4))
    landed(b, rs.at[3])
    send(b, b, ss.at[6], rs.at[6], z=rem(z + 3, 4))


def rows_near(buf, z, c, ss, rs):
    lo, hi = slot_of(z, c, 3), slot_of(z, c, 1)
    landed(buf.at[lo, pl.ds(HALF, HALF)], rs.at[2])
    send(buf.at[lo], buf.at[lo], ss.at[7], rs.at[7], c=1 - c)
    landed(buf.at[hi, pl.ds(0, HALF)], rs.at[4])
    send(buf.at[hi], buf.at[hi], ss.at[8], rs.at[8], c=1 - c)


def rows_near_in(buf, z, c, rs):
    landed(buf.at[slot_of(z, 1 - c, 3)], rs.at[7])
    landed(buf.at[slot_of(z, 1 - c, 1)], rs.at[8])


def rows_far(buf, z, c, ss, rs):
    far = slot_of(z, c, 2)
    landed(buf.at[far, pl.ds(0, HALF)], rs.at[5])
    landed(buf.at[far, pl.ds(HALF, HALF)], rs.at[6])
    send(buf.at[far], buf.at[far], ss.at[9], rs.at[9], c=1 - c)


def rows_left(buf, ss):
    for i in (0, 7, 8, 9):
        landed(buf.at[0], ss.at[i])
    for i in range(1, 7):
        landed(buf.at[0, pl.ds(0, HALF)], ss.at[i])


def rows_before(k, buf, z, c, ss, rs):
    @pl.when(k == 0)
    def _():
        landed(buf.at[2 * z + 1 - c], rs.at[0])

    @pl.when((k == 1) & (c == 0))
    def _():
        rows_pass(buf, z, c, ss, rs)
        rows_near(buf, z, c, ss, rs)

    @pl.when((k == 2) & (c == 1))
    def _():
        rows_near(buf, z, c, ss, rs)

    @pl.when(((k == 1) & (c == 1)) | ((k == 2) & (c == 0)))
    def _():
        rows_near_in(buf, z, c, rs)

    @pl.when(k == 3)
    def _():
        @pl.when(c == 1)
        def _():
            rows_far(buf, z, c, ss, rs)

        landed(buf.at[slot_of(z, 1 - c, 2)], rs.at[9])


def rows_midway(k, buf, z, c, ss, rs):
    @pl.when((k == 0) & (c == 1))
    def _():
        rows_send(buf, z, c, ss, rs)

    @pl.when((k == 1) & (c == 1))
    def _():
        rows_pass(buf, z, c, ss, rs)

    @pl.when((k == 2) & (c == 0))
    def _():
        rows_far(buf, z, c, ss, rs)


def slots(k, z):
    near = (k == 1) | (k == 2)
    chip = rem(z + jnp.where(k == 3, 2, 0), 4)
    first = jnp.where(near, 2 * rem(z + 3, 4) + k - 1, 2 * chip)
    second = jnp.where(near, 2 * rem(z + 1, 4) + k - 1, 2 * chip + 1)
    return near, first, second


def sums_send(k, z, c, partial, own, sibout, sibin, out, inn, sbs, sbr, rss, rsr):
    near, first, second = slots(k, z)
    far = jnp.where(k == 0, 0, 1)
    mine = near & (c == k - 1)
    base = first - jnp.where(near, 0, rem(first, 2))
    t0 = partial(jnp.where(near, first, base + 1 - c))
    m0 = jnp.where(near, 2, far)

    @pl.when(jnp.logical_not(mine))
    def _():
        sibout[m0] = t0.astype(BF)
        send(sibout.at[m0], sibin.at[m0], sbs.at[m0], sbr.at[m0], c=1 - c)

    @pl.when(mine)
    def _():
        landed(sibin.at[2], sbr.at[2])
        out[0] = (t0 + sibin[2].astype(F32)).astype(BF)
        send(out.at[0], inn.at[0], rss.at[0], rsr.at[0], z=rem(z + 3, 4))

    t1 = partial(jnp.where(near, second, base + c))
    theirs = near & (c != k - 1)

    @pl.when(theirs)
    def _():
        sibout[3] = t1.astype(BF)
        send(sibout.at[3], sibin.at[3], sbs.at[3], sbr.at[3], c=1 - c)

    @pl.when(jnp.logical_not(theirs))
    def _():
        m1 = jnp.where(near, 3, far)
        landed(sibin.at[m1], sbr.at[m1])
        both = t1 + sibin[m1].astype(F32)

        @pl.when(k == 0)
        def _():
            own[...] = both

        @pl.when(k != 0)
        def _():
            o = jnp.where(near, 1, 2)
            out[o] = both.astype(BF)
            send(out.at[o], inn.at[o], rss.at[o], rsr.at[o], z=rem(z + jnp.where(near, 1, 2), 4))


def sums_total(own, inn, rsr):
    total = own[...]
    for i in range(3):
        landed(inn.at[i], rsr.at[i])
        total = total + inn[i].astype(F32)
    return total


def sums_left(sibout, out, sbs, rss):
    for i in range(4):
        landed(sibout.at[i], sbs.at[i])
    for i in range(3):
        landed(out.at[i], rss.at[i])


def lanes(shape):
    return lax.broadcasted_iota(jnp.int32, shape, len(shape) - 1)


def turn(v, cos, sin):
    low = rem(lanes(v.shape), 64) < 16
    partner = jnp.where(low, pltpu.roll(v, 112, 1), pltpu.roll(v, 16, 1))
    return v * cos + partner * sin


def nt(a, b):
    return lax.dot_general(a, b, (((1,), (1,)), ((), ())), preferred_element_type=F32)


def tn(a, b):
    return lax.dot_general(a, b, (((0,), (0,)), ((), ())), preferred_element_type=F32)


def nn(a, b):
    return jnp.dot(a, b, preferred_element_type=F32)


def stats(x):
    centre = x - jnp.mean(x, axis=-1, keepdims=True)
    r = lax.rsqrt(jnp.mean(centre * centre, axis=-1, keepdims=True) + EPSILON)
    return centre, r


def expand(t):
    lane = lanes(t.shape)
    rot = rem(lane, 64) < ROT
    first = lane < 64
    cos = jnp.where(rot, jnp.where(first, t, pltpu.roll(t, 64, 1)), 1.0)
    sin = jnp.where(rot, jnp.where(first, pltpu.roll(t, 96, 1), pltpu.roll(t, 32, 1)), 0.0)
    return cos, sin, t[:, 64:65]


def expand(t):
    lane = lanes(t.shape)
    rot = rem(lane, 64) < ROT
    first = lane < 64
    cos = jnp.where(rot, jnp.where(first, t, pltpu.roll(t, 64, 1)), 1.0)
    sin = jnp.where(rot, jnp.where(first, pltpu.roll(t, 96, 1), pltpu.roll(t, 32, 1)), 0.0)
    return cos, sin, t[:, 64:65]


def normed_rows(l, x, vec):
    centre, r = stats(x[...])
    return (centre * r * vec[8 * l : 8 * l + 1, :] + vec[8 * l + 1 : 8 * l + 2, :]).astype(BF)


def forward_pass(
    l, z, c, x, vec, bins, w1, w2, tabs, nall, qkv, prob, a2, pre, raw, sums, rows, spill, early, hook
):
    ss, rs = rows
    row = 8 * l

    def step(i):
        k = jnp.where(i == 0, 3, jnp.where(i == 3, 0, i)) if early else i
        hook(i)
        if not early:
            rows_before(k, nall, z, c, ss, rs)
        _, sa, sb = slots(k, z)
        n = jnp.concatenate([nall[sa], nall[sb]], axis=0)
        raw[:, 0:QKV] = nn(n, w1[:, :QKV])
        val = nn(n, w1[:, QKV:]) + bins[row : row + 1, :]
        pre[sa] = val[:CAP]
        pre[sb] = val[CAP:]

        def act(i):
            u, t = div(i, 6), rem(i, 6)
            s = jnp.where(u == 0, sa, sb)
            at = pl.ds(pl.multiple_of(t * 32, 32), 32)
            v = pre[s, at, :]
            g = 0.5 * v * (1.0 + jnp.tanh(C0 * (v + C1 * v * v * v)))
            a2[s, at, 128:] = g.astype(BF)

        loop(12, act)
        if not early:
            rows_midway(k, nall, z, c, ss, rs)
        for u, s in enumerate((sa, sb)):
            at = slice(u * CAP, (u + 1) * CAP)
            cos, sin, start = expand(tabs[s])
            q = turn(raw[at, 0:128], cos, sin).astype(BF)
            kk = turn(raw[at, 128:256], cos, sin).astype(BF)
            v = raw[at, 256:384].astype(BF)
            qkv[s, :, 0:128] = q
            qkv[s, :, 128:256] = kk
            qkv[s, :, 256:384] = v
            q = q * jnp.asarray(1.0 / math.sqrt(HEAD), BF)
            key_at = lanes((CAP, CAP))
            query_at = lax.broadcasted_iota(jnp.int32, (CAP, CAP), 0)
            allowed = (key_at >= start.astype(jnp.int32)) & (key_at <= query_at)
            head = lanes((CAP, 128)) < HEAD
            mixed = []
            for h in range(2):
                qh = jnp.where(head if h == 0 else ~head, q, jnp.zeros_like(q))
                score = jnp.where(allowed, nt(qh, kk), NEGATIVE)
                e = jnp.exp(score - jnp.max(score, axis=-1, keepdims=True))
                w = e / jnp.sum(e, axis=-1, keepdims=True)
                prob[2 * s + h] = w
                mixed.append(nn(w.astype(BF), v))
            a2[s, :, 0:128] = jnp.where(head, mixed[0], mixed[1]).astype(BF)
        if spill is not None:
            prob_o, pre_o, sem = spill
            for u, s in enumerate((sa, sb)):
                local(prob.at[pl.ds(2 * s, 2)], prob_o.at[pl.ds(2 * s, 2)], sem.at[k, 0, u])
                local(pre.at[s], pre_o.at[s], sem.at[k, 1, u])
        hook(i, 1)
        sums_send(k, z, c, lambda s: nn(a2[s], w2[...]), *sums)

    loop(4, step)
    own, _, _, out, inn, _, _, rss, rsr = sums
    return x[...] + (sums_total(own, inn, rsr) + vec[row + 2 : row + 3, :])


def backward_pass(
    l, z, c, g_ref, x, vec, w1, w2, tabs, nall, qkv, prob, a2, pre, raw, gall, dp,
    g1q, g1i, g2, lns, loc, sums, rows, hook,
):
    ss, rs = rows
    gall[2 * z + c] = g_ref[...].astype(BF)
    rows_sibling(gall, z, c, ss, rs)

    @pl.when(c == 0)
    def _():
        rows_send(gall, z, c, ss, rs)

    hook(0)

    def step(k):
        hook(k, 1)
        rows_before(k, gall, z, c, ss, rs)
        _, sa, sb = slots(k, z)
        g = jnp.concatenate([gall[sa], gall[sb]], axis=0)
        raw[...] = nt(g, w2[...])

        def act(i):
            u, t = div(i, 12), rem(i, 12)
            s = jnp.where(u == 0, sa, sb)
            at = pl.ds(pl.multiple_of(t * 16, 16), 16)
            v = pre[s, at, :]
            d = raw[pl.ds(pl.multiple_of(u * CAP + t * 16, 16), 16), 128:]
            t1 = jnp.tanh(C0 * (v + C1 * v * v * v))
            slope = 0.5 * (1.0 + t1) + 0.5 * v * (1.0 - t1 * t1) * (C0 + (3.0 * C0 * C1) * v * v)
            dp[s, at, QKV:] = (d * slope).astype(BF)

        loop(24, act)
        rows_midway(k, gall, z, c, ss, rs)
        for u, s in enumerate((sa, sb)):
            at = slice(u * CAP, (u + 1) * CAP)
            cos, sin, _ = expand(tabs[s])
            m = raw[at, 0:128].astype(BF)
            q, kk, v = qkv[s, :, 0:128], qkv[s, :, 128:256], qkv[s, :, 256:384]
            head = lanes((CAP, 128)) < HEAD
            dq, dk, dv = [], [], []
            for h in range(2):
                mine = head if h == 0 else ~head
                mh = jnp.where(mine, m, jnp.zeros_like(m))
                w = prob[2 * s + h]
                soft = nt(mh, v)
                dv.append(tn(w.astype(BF), mh))
                wd = w * soft
                ds = (wd - w * jnp.sum(wd, axis=-1, keepdims=True)).astype(BF)
                dq.append(nn(ds, kk))
                dk.append(tn(ds, jnp.where(mine, q, jnp.zeros_like(q))))
            scale = 1.0 / math.sqrt(HEAD)
            dq = jnp.where(head, dq[0], dq[1]) * scale
            dk = (dk[0] + dk[1]) * scale
            dp[s, :, 0:128] = turn(dq, cos, -sin).astype(BF)
            dp[s, :, 128:256] = turn(dk, cos, -sin).astype(BF)
            dp[s, :, 256:384] = (dv[0] + dv[1]).astype(BF)
        sums_send(k, z, c, lambda s: nt(dp[s], w1[...]), *sums)

    loop(4, step)
    hook(4)

    rows = LINE * CAP
    g = gall[...].reshape(rows, D)
    val = tn(a2[...].reshape(rows, DEEP), g)
    for s in range(2):
        for q in range(4):
            g2[s, q, 0:16, :] = val[64 * s + 16 * q : 64 * s + 16 * q + 16].astype(BF)
            base = 128 + 256 * s + 64 * q
            g2[s, q, 16:80, :] = val[base : base + 64].astype(BF)
    hook(5)
    d = dp[...].reshape(rows, WIDE)
    for t in range(2):
        val = tn(nall[:, :, t * 512 : (t + 1) * 512].reshape(rows, 512), d).astype(BF)
        for s in range(8):
            sh = 8 * t + s
            zz, hh, cc = sh // 4, (sh // 2) % 2, sh % 2
            for q in range(4):
                part = val[64 * s + 16 * q : 64 * s + 16 * q + 16]
                at = (2 * zz + cc) * 16
                g1q[hh, q, at : at + 16, :] = part[:, :QKV]
                g1i[hh, q, at : at + 16, :] = part[:, QKV:]
    hook(6)

    zero = jnp.zeros((1, 128), F32)
    col = pl.ds(pl.multiple_of((2 * z + c) * 128, 128), 128)
    bfc = jnp.zeros((1, 128), F32)
    b_in = jnp.zeros((1, HID), F32)
    for s in range(LINE):
        bfc = bfc + jnp.sum(gall[s, :, col].astype(F32), axis=0, keepdims=True)
        b_in = b_in + jnp.sum(dp[s, :, QKV:].astype(F32), axis=0, keepdims=True)
    loc[...] = jnp.concatenate(
        [zero, zero, bfc] + [b_in[:, 128 * i : 128 * i + 128] for i in range(4)] + [zero], axis=0
    )
    own, _, _, out, inn, _, _, rss, rsr = sums
    ngrad = sums_total(own, inn, rsr)
    centre, r = stats(x[...])
    xhat = centre * r
    e = ngrad * vec[8 * l : 8 * l + 1, :]
    ex = jnp.mean(e * xhat, axis=-1, keepdims=True)
    gain = jnp.sum(ngrad * xhat, axis=0, keepdims=True)
    bias = jnp.sum(ngrad, axis=0, keepdims=True)
    both = jnp.concatenate([gain, bias] + [jnp.zeros((6, D), F32)], axis=0)
    for i in range(LINE):
        lns[i] = both[:, 128 * i : 128 * i + 128]
    return g_ref[...] + r * (e - jnp.mean(e, axis=-1, keepdims=True) - xhat * ex)


def member(jj):
    return dict(z=div(jj, 2), c=rem(jj, 2))


def small_start(l, me, lns, zs, s5, q5):
    j = me[7]

    def go(k):
        jj = rem(j + k, LINE)
        send(lns.at[l, jj], zs.at[l, j], s5.at[l, k], q5.at[l, j], **member(jj))

    loop(LINE - 1, lambda k: go(k + 1))


def small_spread(l, me, lns, loc, zs, ps, q5, s6, q6):
    y, xl, z, xh, c, x, p, j = me

    def small_in(k):
        jj = rem(j + k, LINE)
        landed(zs.at[l, jj], q5.at[l, jj])

    loop(LINE - 1, lambda k: small_in(k + 1))
    zs[l, j] = lns[l, j] + loc[l]
    total = zs[l, 0]
    for i in range(1, LINE):
        total = total + zs[l, i]
    ps[l, p] = total

    def spread(k):
        send(ps.at[l, p], ps.at[l, p], s6.at[l, k], q6.at[l, p], **plane_member(y, x, k))

    loop(15, lambda k: spread(k + 1))


def small_last(l, me, ps, tot, q6, s8, q8):
    y, xl, z, xh, c, x, p, j = me

    def spread_in(k):
        q = rem(p + k, 16)
        landed(ps.at[l, q], q6.at[l, q])

    loop(15, lambda k: spread_in(k + 1))
    total = ps[l, 0]
    for i in range(1, 16):
        total = total + ps[l, i]
    tot[l, c] = total
    send(tot.at[l, c], tot.at[l, c], s8.at[l], q8.at[l], c=1 - c)


def second_p1(l, me, g2, ga1, gb1, s, q):
    y, xl, z, xh, c, x, p, j = me
    left, right = pl.ds(0, 512), pl.ds(512, 512)
    for d in (1, 2, 3):
        dev = along_x(x, d)

        @pl.when(dev["xh"] == c)
        def _():
            send(
                g2.at[dev["xl"], :, :, left], ga1.at[l, d - 1], s.at[l, 0, d], q.at[l, 0, d], **dev
            )

        yy = along_y(y, d)
        send(g2.at[:, yy["y"], :, right], gb1.at[l, d - 1], s.at[l, 1, d], q.at[l, 1, d], **yy)


def second_p2(l, me, g2, ga1, gb1, ga2, gb2, sga, sgb, s, q):
    y, xl, z, xh, c, x, p, j = me
    for d in (1, 2, 3):
        landed(gb1.at[l, d - 1], q.at[l, 1, d])

    def add_right(i):
        h, t = div(i, 5), rem(i, 5)
        at = pl.ds(pl.multiple_of(16 * t, 16), 16)
        acc = g2[h, y, at, 512:].astype(F32)
        for d in range(3):
            acc = acc + gb1[l, d, h, at, :].astype(F32)
        sgb[h, at, :] = acc.astype(BF)

    loop(10, add_right)
    for d in (1, 2, 3):
        dev = along_x(x, d)

        @pl.when(dev["xh"] == c)
        def _():
            send(sgb.at[dev["xl"]], gb2.at[l, d - 1], s.at[l, 2, d], q.at[l, 2, d], **dev)

    @pl.when(xh == c)
    def _():
        for d in (1, 2, 3):
            landed(ga1.at[l, d - 1], q.at[l, 0, d])

        def add_left(i):
            yy, t = div(i, 5), rem(i, 5)
            at = pl.ds(pl.multiple_of(16 * t, 16), 16)
            acc = g2[xl, yy, at, 0:512].astype(F32)
            for d in range(3):
                acc = acc + ga1[l, d, yy, at, :].astype(F32)
            sga[yy, at, :] = acc.astype(BF)

        loop(20, add_left)
        for d in (1, 2, 3):
            yy = along_y(y, d)
            send(sga.at[yy["y"]], ga2.at[l, d - 1], s.at[l, 3, d], q.at[l, 3, d], **yy)


def second_p3(l, me, ga2, gb2, sga, sgb, red2, fo, ff, s, q, s4, q4):
    y, xl, z, xh, c, x, p, j = me
    row16 = pl.ds(pl.multiple_of(16 * y, 16), 16)
    row64 = pl.ds(pl.multiple_of(64 * y, 64), 64)

    @pl.when(xh == c)
    def _():
        for d in (1, 2, 3):
            landed(gb2.at[l, d - 1], q.at[l, 2, d])
            landed(ga2.at[l, d - 1], q.at[l, 3, d])

        def add(t):
            at = pl.ds(pl.multiple_of(16 * t, 16), 16)
            a = sga[y, at, :].astype(F32)
            b = sgb[xl, at, :].astype(F32)
            for d in range(3):
                a = a + ga2[l, d, at, :].astype(F32)
                b = b + gb2[l, d, at, :].astype(F32)
            red2[l, at, 0:512] = a.astype(BF)
            red2[l, at, 512:1024] = b.astype(BF)

        loop(5, add)

        def out(i):
            yy, ll = rem(y + div(i, 2), 4), rem(xl + rem(i, 2), 2)
            here = (i == 0) & (xl == c)
            parts = (
                (red2.at[l, pl.ds(0, 16)], fo.at[l, row16]),
                (red2.at[l, pl.ds(16, 64)], ff.at[l, row64]),
            )
            for n, (src, dst) in enumerate(parts):

                @pl.when(here)
                def _():
                    local(src, dst, q4.at[l, y, n])

                @pl.when(jnp.logical_not(here))
                def _():
                    send(src, dst, s4.at[l, i, n], q4.at[l, y, n], y=yy, xl=ll, c=xl)

        loop(8, out)


def second_left(l, me, g2, sga, sgb, s):
    y, xl, z, xh, c, x, p, j = me
    left, right = pl.ds(0, 512), pl.ds(512, 512)
    for d in (1, 2, 3):
        landed(g2.at[:, 0, :, right], s.at[l, 1, d])

        @pl.when(along_x(x, d)["xh"] == c)
        def _():
            landed(g2.at[0, :, :, left], s.at[l, 0, d])
            landed(sgb.at[0], s.at[l, 2, d])

        @pl.when(xh == c)
        def _():
            landed(sga.at[0], s.at[l, 3, d])


def by_kind(ll, f):
    @pl.when(ll == 0)
    def _():
        f(pl.ds(0, QKV), 0)

    @pl.when(ll == 1)
    def _():
        f(pl.ds(0, HID), 1)


TOP, LOW = pl.ds(0, 64), pl.ds(64, 64)


def first_p1(l, me, g1q, g1i, ra1, rbq, rbi, s, q):
    y, xl, z, xh, c, x, p, j = me
    for d in (1, 2, 3):
        dev = along_x(x, d)
        hh = dev["xh"]

        def go(cols, kind):
            src = (g1q, g1i)[kind].at[hh, :, TOP]
            send(src, ra1.at[l, d - 1, :, :, cols], s.at[l, 0, d], q.at[l, 0, d], **dev)

        by_kind(dev["xl"], go)
        yy = along_y(y, d)
        send(g1q.at[:, yy["y"], LOW], rbq.at[l, d - 1], s.at[l, 1, d], q.at[l, 1, d], **yy)
        send(g1i.at[:, yy["y"], LOW], rbi.at[l, d - 1], s.at[l, 2, d], q.at[l, 2, d], **yy)


def first_p2(l, me, g1q, g1i, ra1, rbq, rbi, ra2, rb2, sra, sbq, sbi, s, q):
    y, xl, z, xh, c, x, p, j = me
    for d in (1, 2, 3):
        by_kind(xl, lambda cols, kind: landed(ra1.at[l, d - 1, :, :, cols], q.at[l, 0, d]))

    def add_top(i):
        yy, t = div(i, 4), rem(i, 4)
        at = pl.ds(pl.multiple_of(16 * t, 16), 16)

        def go(cols, kind):
            acc = (g1q, g1i)[kind][xh, yy, at, :].astype(F32)
            for d in range(3):
                acc = acc + ra1[l, d, yy, at, cols].astype(F32)
            sra[yy, at, cols] = acc.astype(BF)

        by_kind(xl, go)

    loop(16, add_top)
    for d in (1, 2, 3):
        yy = along_y(y, d)

        def go(cols, kind):
            src = sra.at[yy["y"], :, cols]
            send(src, ra2.at[l, d - 1, :, cols], s.at[l, 3, d], q.at[l, 3, d], **yy)

        by_kind(xl, go)
    for d in (1, 2, 3):
        landed(rbq.at[l, d - 1], q.at[l, 1, d])
        landed(rbi.at[l, d - 1], q.at[l, 2, d])

    def add_low(i):
        h, t = div(i, 4), rem(i, 4)
        at = pl.ds(pl.multiple_of(16 * t, 16), 16)
        here = pl.ds(pl.multiple_of(64 + 16 * t, 16), 16)
        a = g1q[h, y, here, :].astype(F32)
        b = g1i[h, y, here, :].astype(F32)
        for d in range(3):
            a = a + rbq[l, d, h, at, :].astype(F32)
            b = b + rbi[l, d, h, at, :].astype(F32)
        sbq[h, at, :] = a.astype(BF)
        sbi[h, at, :] = b.astype(BF)

    loop(8, add_low)
    for d in (1, 2, 3):
        dev = along_x(x, d)
        hh = dev["xh"]

        def go(cols, kind):
            src = (sbq, sbi)[kind].at[hh]
            send(src, rb2.at[l, d - 1, :, cols], s.at[l, 4, d], q.at[l, 4, d], **dev)

        by_kind(dev["xl"], go)


def first_p3(l, me, ra2, rb2, sra, sbq, sbi, red1, fq, fi, s, q, s3, q3):
    y, xl, z, xh, c, x, p, j = me
    for d in (1, 2, 3):
        by_kind(xl, lambda cols, kind: landed(ra2.at[l, d - 1, :, cols], q.at[l, 3, d]))
        by_kind(xl, lambda cols, kind: landed(rb2.at[l, d - 1, :, cols], q.at[l, 4, d]))

    def add(t):
        at = pl.ds(pl.multiple_of(16 * t, 16), 16)

        def go(cols, kind):
            a = sra[y, at, cols].astype(F32)
            b = (sbq, sbi)[kind][xh, at, :].astype(F32)
            for d in range(3):
                a = a + ra2[l, d, at, cols].astype(F32)
                b = b + rb2[l, d, at, cols].astype(F32)
            red1[l, at, cols] = a.astype(BF)
            red1[l, pl.ds(pl.multiple_of(64 + 16 * t, 16), 16), cols] = b.astype(BF)

        by_kind(xl, go)

    loop(4, add)
    row16 = pl.ds(pl.multiple_of(16 * y, 16), 16)

    def back(jj):
        at = pl.ds(pl.multiple_of(16 * jj, 16), 16)

        def move(src, dst, n):
            @pl.when(jj == j)
            def _():
                local(src, dst, q3.at[l, j, n])

            @pl.when(jj != j)
            def _():
                send(src, dst, s3.at[l, jj, n], q3.at[l, j, n], **member(jj))

        @pl.when(xl == 0)
        def _():
            for n in range(3):
                cols = pl.ds(pl.multiple_of(n * D + 128 * j, 128), 128)
                move(red1.at[l, at, pl.ds(128 * n, 128)], fq.at[l, row16, cols], n)

        @pl.when(xl == 1)
        def _():
            cols = pl.ds(pl.multiple_of(HID * j, HID), HID)
            move(red1.at[l, at], fi.at[l, row16, cols], 0)

    loop(LINE, back)


def first_left(l, me, g1q, g1i, sra, sbq, sbi, s):
    y, xl, z, xh, c, x, p, j = me
    for d in (1, 2, 3):
        there = along_x(x, d)["xl"]
        by_kind(there, lambda cols, kind: landed((g1q, g1i)[kind].at[0, :, TOP], s.at[l, 0, d]))
        landed(g1q.at[:, 0, LOW], s.at[l, 1, d])
        landed(g1i.at[:, 0, LOW], s.at[l, 2, d])
        by_kind(xl, lambda cols, kind: landed(sra.at[0, :, cols], s.at[l, 3, d]))
        by_kind(there, lambda cols, kind: landed((sbq, sbi)[kind].at[0], s.at[l, 4, d]))


def first_share(l, me, fq, fi, q3, s7, q7):
    y, xl, z, xh, c, x, p, j = me
    row16 = pl.ds(pl.multiple_of(16 * y, 16), 16)

    def back_in(jj):
        @pl.when(xl == 0)
        def _():
            for n in range(3):
                at = pl.ds(pl.multiple_of(n * D + 128 * jj, 128), 128)
                landed(fq.at[l, row16, at], q3.at[l, jj, n])

        @pl.when(xl == 1)
        def _():
            at = pl.ds(pl.multiple_of(HID * jj, HID), HID)
            landed(fi.at[l, row16, at], q3.at[l, jj, 0])

    loop(LINE, back_in)

    def share(i):
        yy, ll = rem(y + div(i, 2), 4), rem(xl + rem(i, 2), 2)
        for v, f in ((0, fq), (1, fi)):

            @pl.when(xl == v)
            def _():
                at = f.at[l, row16]
                send(at, at, s7.at[l, i], q7.at[l, y, v], y=yy, xl=ll)

    loop(7, lambda i: share(i + 1))


def owners_in(l, me, fq, fi, fo, ff, q4, q7):
    y, xl, z, xh, c, x, p, j = me
    for q in range(4):
        landed(fo.at[l, pl.ds(16 * q, 16)], q4.at[l, q, 0])
        landed(ff.at[l, pl.ds(64 * q, 64)], q4.at[l, q, 1])
        for v, f in ((0, fq), (1, fi)):

            @pl.when((xl != v) | (y != q))
            def _():
                landed(f.at[l, pl.ds(16 * q, 16)], q7.at[l, q, v])


def owners_left(l, me, lns, ps, tot, red1, red2, fq, fi, s3, s4, s5, s6, s7, s8):
    y, xl, z, xh, c, x, p, j = me
    row16 = pl.ds(pl.multiple_of(16 * y, 16), 16)
    loop(LINE - 1, lambda k: landed(lns.at[l, 0], s5.at[l, k + 1]))
    loop(15, lambda k: landed(ps.at[l, 0], s6.at[l, k + 1]))

    def left_second(i):
        @pl.when((xh == c) & jnp.logical_not((i == 0) & (xl == c)))
        def _():
            landed(red2.at[l, pl.ds(0, 16)], s4.at[l, i, 0])
            landed(red2.at[l, pl.ds(16, 64)], s4.at[l, i, 1])

    loop(8, left_second)

    def left_back(jj):
        @pl.when((jj != j) & (xl == 0))
        def _():
            for n in range(3):
                landed(red1.at[l, pl.ds(0, 16), pl.ds(0, 128)], s3.at[l, jj, n])

        @pl.when((jj != j) & (xl == 1))
        def _():
            landed(red1.at[l, pl.ds(0, 16)], s3.at[l, jj, 0])

    loop(LINE, left_back)

    def left_share(i):
        for v, f in ((0, fq), (1, fi)):

            @pl.when(xl == v)
            def _():
                landed(f.at[l, row16], s7.at[l, i])

    loop(7, lambda i: left_share(i + 1))
    landed(tot.at[l, c], s8.at[l])


def no_hook(*a):
    pass


def whole_kernel(
    wqkv, win, wo, wfc, sm, tab, x0, cot,
    x2_ref, g0_ref, fs_ref, fq, fi, fo, ff, prob_o, pre_o,
    w1, w2, sma, tabs, vec, bins,
    nall, qkv, a2, prob, pre, raw, gall, dp, x1,
    own, sibout, sibin, out, inn,
    g1q, g1i, g2, lns, loc, ga1, gb1, ga2, gb2, sga, sgb, ra1, rbq, rbi, ra2, rb2, sra, sbq, sbi,
    red1, red2, zs, ps, tot,
    as_, ar, bs, br, cs, cr, xs, xr, ys, yr, ts, tr, ms, mr, ns, nr,
    rows_s, rows_r, sbs, sbr, rss, rsr, spill, fill,
    s1, q1, s2, q2, s3, q3, s4, q4, s5, q5, s6, q6, s7, q7, s8, q8,
):
    y, xl, z, xh, c = place()
    x = 2 * xh + xl
    p = 4 * y + x
    j = 2 * z + c
    me = (y, xl, z, xh, c, x, p, j)
    bar = pltpu.get_barrier_semaphore()
    greet_line(bar, z, c)
    greet_plane(bar, y, x)
    for k in range(1, 8):
        signal(bar, y=rem(y + k // 2, 4), xl=rem(xl + k % 2, 2), c=1 - c)
    signal(bar, xl=1 - xl, xh=1 - xh, c=1 - c)
    pl.semaphore_wait(bar, 30)

    source = (z == y) & (c == xl)

    @pl.when(source)
    def _():
        def to(jj):
            @pl.when(jj == j)
            def _():
                local(sm, sma.at[p], mr)

            @pl.when(jj != j)
            def _():
                send(sm, sma.at[p], ms.at[jj], mr, **member(jj))

        loop(LINE, to)

    weights_z(0, me, wqkv, win, wo, wfc, w1, w2, as_, ar, cs, cr)
    landed(sma.at[p], mr)

    def small_out(k):
        send(sma.at[p], sma.at[p], ns.at[k], nr.at[p], **plane_member(y, x, k))

    loop(15, lambda k: small_out(k + 1))
    weights_p1(0, me, w1, ar, bs, br)
    for k in range(1, LINE):
        jj = rem(j + k, LINE)
        send(tab, tabs.at[j], ts.at[k], tr.at[j], **member(jj))
    local(tab, tabs.at[j], tr.at[j])

    def small_in(k):
        q = rem(p + k, 16)
        landed(sma.at[q], nr.at[q])

    loop(15, lambda k: small_in(k + 1))
    half = lanes((16, 128)) < 64
    for t in range(8):
        vec[:, 128 * t : 128 * t + 128] = jnp.where(half, sma[2 * t, :, :128], sma[2 * t + 1, :, :128])
    for l in range(LAYERS):
        at = 8 * l + 3
        bins[8 * l : 8 * l + 1, 0:256] = sma[2 * j, at : at + 1, :]
        bins[8 * l : 8 * l + 1, 256:512] = sma[2 * j + 1, at : at + 1, :]

    def sums_of(n):
        return (
            own, sibout, sibin, out, inn, sbs.at[n], sbr.at[n], rss.at[n], rsr.at[n],
        )

    def rows_of(n):
        return rows_s.at[n], rows_r.at[n]

    def done(n, buf):
        rows_left(buf, rows_s.at[n])
        sums_left(sibout, out, sbs.at[n], rss.at[n])

    n0 = nall.at[0]
    ss, rs = rows_of(0)
    n0[2 * z + c] = normed_rows(0, x0, vec)
    rows_sibling(n0, z, c, ss, rs)
    rows_send(n0, z, c, ss, rs)
    weights_p2(0, me, w1, bs, br)
    weights_f1(0, me, w2, cr, xs, xr)
    rows_pass(n0, z, c, ss, rs)
    weights_f2(0, me, w2, xr, ys, yr)
    rows_near(n0, z, c, ss, rs)
    rows_far(n0, z, c, ss, rs)
    landed(n0.at[2 * z + 1 - c], rs.at[0])
    rows_near_in(n0, z, c, rs)
    loop(LINE, lambda k: landed(tabs.at[k], tr.at[k]))
    weights_in1(0, me, w1, br)
    landed(n0.at[slot_of(z, 1 - c, 2)], rs.at[9])
    weights_z(1, me, wqkv, win, wo, wfc, w1, w2, as_, ar, cs, cr)

    def hook_f0(i, late=0):
        if late:

            @pl.when(i == 0)
            def _():
                weights_in2(0, me, w2, cr, yr)

        else:

            @pl.when(i == 1)
            def _():
                weights_p1(1, me, w1, ar, bs, br)

            @pl.when(i == 2)
            def _():
                weights_f1(1, me, w2, cr, xs, xr)
                weights_p2(1, me, w1, bs, br)

            @pl.when(i == 3)
            def _():
                weights_f2(1, me, w2, xr, ys, yr)

    x1[...] = forward_pass(
        0, z, c, x0, vec, bins, w1.at[0], w2.at[0], tabs, n0, qkv.at[0], prob, a2.at[0], pre,
        raw, sums_of(0), rows_of(0), (prob_o, pre_o, spill), True, hook_f0,
    )

    n1 = nall.at[1]
    ss, rs = rows_of(1)
    n1[2 * z + c] = normed_rows(1, x1, vec)
    rows_sibling(n1, z, c, ss, rs)

    @pl.when(c == 0)
    def _():
        rows_send(n1, z, c, ss, rs)

    done(0, n0)
    for k in range(4):
        for u in range(2):
            landed(prob.at[pl.ds(0, 2)], spill.at[k, 0, u])
            landed(pre.at[0], spill.at[k, 1, u])
    weights_in1(1, me, w1, br)
    weights_in2(1, me, w2, cr, yr)
    x2_ref[...] = forward_pass(
        1, z, c, x1, vec, bins, w1.at[1], w2.at[1], tabs, n1, qkv.at[1], prob, a2.at[1], pre,
        raw, sums_of(1), rows_of(1), None, False, no_hook,
    )
    done(1, n1)

    g0_ref[...] = cot[...] * tab[:, 96:97]

    def hook1(n, inside=0):
        if inside:
            return
        if n == 4:
            local(prob_o, prob, fill.at[0])
            local(pre_o, pre, fill.at[1])
        if n == 5:
            second_p1(1, me, g2, ga1, gb1, s2, q2)
        if n == 6:
            first_p1(1, me, g1q, g1i, ra1, rbq, rbi, s1, q1)

    g0_ref[...] = backward_pass(
        1, z, c, g0_ref, x1, vec, w1.at[1], w2.at[1], tabs, n1, qkv.at[1], prob, a2.at[1], pre,
        raw, gall.at[1], dp, g1q, g1i, g2, lns.at[1], loc.at[1], sums_of(2), rows_of(2), hook1,
    )
    small_start(1, me, lns, zs, s5, q5)
    done(2, gall.at[1])

    def hook0(n, inside=0):
        if inside:

            @pl.when(n == 1)
            def _():
                small_spread(1, me, lns, loc, zs, ps, q5, s6, q6)

            @pl.when(n == 2)
            def _():
                second_p2(1, me, g2, ga1, gb1, ga2, gb2, sga, sgb, s2, q2)
                first_p2(1, me, g1q, g1i, ra1, rbq, rbi, ra2, rb2, sra, sbq, sbi, s1, q1)

            @pl.when(n == 3)
            def _():
                second_p3(1, me, ga2, gb2, sga, sgb, red2, fo, ff, s2, q2, s4, q4)
                first_p3(1, me, ra2, rb2, sra, sbq, sbi, red1, fq, fi, s1, q1, s3, q3)

            return
        if n == 0:
            landed(prob, fill.at[0])
            landed(pre, fill.at[1])
        if n == 4:
            second_left(1, me, g2, sga, sgb, s2)
            first_left(1, me, g1q, g1i, sra, sbq, sbi, s1)
            first_share(1, me, fq, fi, q3, s7, q7)
        if n == 5:
            second_p1(0, me, g2, ga1, gb1, s2, q2)
        if n == 6:
            first_p1(0, me, g1q, g1i, ra1, rbq, rbi, s1, q1)

    g0_ref[...] = backward_pass(
        0, z, c, g0_ref, x0, vec, w1.at[0], w2.at[0], tabs, n0, qkv.at[0], prob, a2.at[0], pre,
        raw, gall.at[0], dp, g1q, g1i, g2, lns.at[0], loc.at[0], sums_of(3), rows_of(3), hook0,
    )
    small_start(0, me, lns, zs, s5, q5)
    second_p2(0, me, g2, ga1, gb1, ga2, gb2, sga, sgb, s2, q2)
    first_p2(0, me, g1q, g1i, ra1, rbq, rbi, ra2, rb2, sra, sbq, sbi, s1, q1)
    small_spread(0, me, lns, loc, zs, ps, q5, s6, q6)
    second_p3(0, me, ga2, gb2, sga, sgb, red2, fo, ff, s2, q2, s4, q4)
    first_p3(0, me, ra2, rb2, sra, sbq, sbi, red1, fq, fi, s1, q1, s3, q3)
    small_last(1, me, ps, tot, q6, s8, q8)
    small_last(0, me, ps, tot, q6, s8, q8)
    first_share(0, me, fq, fi, q3, s7, q7)
    done(3, gall.at[0])
    second_left(0, me, g2, sga, sgb, s2)
    first_left(0, me, g1q, g1i, sra, sbq, sbi, s1)
    for l in range(LAYERS):
        weights_left(l, me, wqkv, win, wo, wfc, w1, w2, as_, cs, bs, xs, ys)
    for k in range(1, LINE):
        landed(tab, ts.at[k])
    loop(15, lambda k: landed(sma.at[0], ns.at[k + 1]))

    @pl.when(source)
    def _():
        def gone(jj):
            @pl.when(jj != j)
            def _():
                landed(sm, ms.at[jj])

        loop(LINE, gone)

    for l in (1, 0):
        landed(tot.at[l, 1 - c], q8.at[l])
        fs_ref[l] = tot[l]
        owners_in(l, me, fq, fi, fo, ff, q4, q7)
        owners_left(l, me, lns, ps, tot, red1, red2, fq, fi, s3, s4, s5, s6, s7, s8)


def whole(wqkv, win, wo, wfc, sm, tab, x0, cot):
    n = LAYERS
    return pl.pallas_call(
        whole_kernel,
        out_shape=(
            jax.ShapeDtypeStruct((CAP, D), F32),
            jax.ShapeDtypeStruct((CAP, D), F32),
            jax.ShapeDtypeStruct((n, 2, 8, 128), F32),
            jax.ShapeDtypeStruct((n, 64, 3 * D), BF),
            jax.ShapeDtypeStruct((n, 64, FF), BF),
            jax.ShapeDtypeStruct((n, 64, D), BF),
            jax.ShapeDtypeStruct((n, 256, D), BF),
            jax.ShapeDtypeStruct((2 * LINE, CAP, CAP), F32),
            jax.ShapeDtypeStruct((LINE, CAP, HID), F32),
        ),
        in_specs=[ANY] * 4 + [INV] * 4,
        out_specs=(INV,) * 3 + (ANY,) * 6,
        scratch_shapes=[
            VMEM((n, D, WIDE), BF), VMEM((n, DEEP, D), BF), VMEM((16, 16, 256), F32),
            VMEM((LINE, CAP, 128), F32), VMEM((16, D), F32), VMEM((16, HID), F32),
            VMEM((n, LINE, CAP, D), BF), VMEM((n, LINE, CAP, QKV), BF), VMEM((n, LINE, CAP, DEEP), BF),
            VMEM((2 * LINE, CAP, CAP), F32), VMEM((LINE, CAP, HID), F32), VMEM((2 * CAP, DEEP), F32),
            VMEM((n, LINE, CAP, D), BF), VMEM((LINE, CAP, WIDE), BF),
            VMEM((CAP, D), F32),
            VMEM((CAP, D), F32), VMEM((4, CAP, D), BF), VMEM((4, CAP, D), BF),
            VMEM((3, CAP, D), BF), VMEM((3, CAP, D), BF),
            VMEM((2, 4, 128, QKV), BF), VMEM((2, 4, 128, HID), BF), VMEM((2, 4, 80, D), BF),
            VMEM((n, LINE, 8, 128), F32), VMEM((n, 8, 128), F32),
            VMEM((n, 3, 4, 80, 512), BF), VMEM((n, 3, 2, 80, 512), BF),
            VMEM((n, 3, 80, 512), BF), VMEM((n, 3, 80, 512), BF),
            VMEM((4, 80, 512), BF), VMEM((2, 80, 512), BF),
            VMEM((n, 3, 4, 64, HID), BF), VMEM((n, 3, 2, 64, QKV), BF), VMEM((n, 3, 2, 64, HID), BF),
            VMEM((n, 3, 64, HID), BF), VMEM((n, 3, 64, HID), BF),
            VMEM((4, 64, HID), BF), VMEM((2, 64, QKV), BF), VMEM((2, 64, HID), BF),
            VMEM((n, 128, HID), BF), VMEM((n, 80, D), BF),
            VMEM((n, LINE, 8, 128), F32), VMEM((n, 16, 8, 128), F32), VMEM((n, 2, 8, 128), F32),
            DMA((LINE, n, 4)), DMA((n, 4)), DMA((n, 2, 15)), DMA((n, 16, 2)),
            DMA((n, 2, 2)), DMA((n, 2, 2)), DMA((n, 2, 2)), DMA((n, 2, 2)),
            DMA((n, 4, 2, 2)), DMA((n, 4, 2, 2)),
            DMA((LINE,)), DMA((LINE,)), DMA((LINE,)), DMA, DMA((16,)), DMA((16,)),
            DMA((4, 10)), DMA((4, 10)), DMA((4, 4)), DMA((4, 4)), DMA((4, 3)), DMA((4, 3)),
            DMA((4, 2, 2)), DMA((2,)),
            DMA((n, 5, 4)), DMA((n, 5, 4)), DMA((n, 4, 4)), DMA((n, 4, 4)),
            DMA((n, LINE, 3)), DMA((n, LINE, 3)),
            DMA((n, 8, 2)), DMA((n, 4, 2)),
            DMA((n, LINE)), DMA((n, LINE)),
            DMA((n, 16)), DMA((n, 16)),
            DMA((n, 8)), DMA((n, 4, 2)),
            DMA((n,)), DMA((n,)),
        ],
        compiler_params=pltpu.CompilerParams(
            collective_id=0, has_side_effects=True, vmem_limit_bytes=63 * 2**20
        ),
        name="whole",
    )(wqkv, win, wo, wfc, sm, tab, x0, cot)


def per_device(
    inputs, cotangent, lengths, ln_gain, ln_bias, w_qkv, w_attn_out, w_in, b_in, w_fc, b_fc
):
    xh, c = (lax.axis_index(a) for a in ("xh", "c"))
    offsets = jnp.arange(CAP, dtype=jnp.int32)
    seq_ends = jnp.cumsum(lengths[0])
    passed = (offsets[:, None] >= seq_ends[None, :]).astype(jnp.int32)
    segment = jnp.sum(passed, axis=1)
    start = jnp.sum(passed * lengths[0][None, :], axis=1)
    position = offsets - start
    frequency = 10000.0 ** (-jnp.arange(ROT // 2, dtype=F32) * 2.0 / ROT)
    angles = position.astype(F32)[:, None] * frequency
    cosine, sine = jnp.cos(angles), jnp.sin(angles)
    valid = (segment < SLOTS).astype(F32)
    tab = jnp.concatenate(
        [cosine, cosine, -sine, sine]
        + [jnp.broadcast_to(v[:, None], (CAP, 32)) for v in (start.astype(F32), valid)],
        axis=1,
    )
    wide = [jnp.concatenate([v] * (256 // v.shape[1]), axis=1) for v in (ln_gain, ln_bias, b_fc, b_in)]
    sm = jnp.stack(wide + [jnp.zeros_like(b_in)] * 4, axis=1).reshape(16, 256).astype(F32)

    hidden, grad, fs, fq, fi, fo, ff, _, _ = whole(
        w_qkv, w_in, w_attn_out, w_fc, sm, tab, inputs, cotangent
    )
    mine = lax.dynamic_index_in_dim(fs, xh, 1, keepdims=False)
    pick = lax.dynamic_slice(mine[:, 0:3], (0, 0, 64 * c), (LAYERS, 3, 64))
    b_in_grad = lax.dynamic_slice(mine[:, 3:7].reshape(LAYERS, HID), (0, 256 * c), (LAYERS, 256))
    return (
        hidden,
        grad,
        pick[:, 0],
        pick[:, 1],
        fq.astype(F32),
        fo.astype(F32),
        fi.astype(F32),
        b_in_grad,
        ff.astype(F32),
        pick[:, 2],
    )


def solution(mesh):
    fine = Mesh(mesh.devices.reshape(4, 2, 4, 2, 2), AXES)
    rows = P(AXES, None)
    shard = ("z", "xh", "c")
    vector, matrix = P(None, shard), P(None, shard, None)
    in_specs = (
        rows, rows, rows, vector, vector, matrix, matrix, matrix, vector, matrix, vector,
    )
    out_specs = (
        rows, rows, vector, vector, matrix, matrix, matrix, vector, matrix, vector,
    )
    return jax.shard_map(
        per_device, mesh=fine, in_specs=in_specs, out_specs=out_specs, check_vma=False
    )
```

```python
import functools
import math

import jax
import jax.numpy as jnp
from jax import lax
from jax.experimental import pallas as pl
from jax.experimental.pallas import tpu as pltpu
from jax.sharding import Mesh
from jax.sharding import PartitionSpec as P

D = 1024
HEADS = 16
HEAD = 64
ROT = 32
FF = 4096
LAYERS = 2
SLOTS = 4
CAP = 192
LINE = 8
QKV = 384
HID = 512
WIDE = QKV + HID
DEEP = 128 + HID
EPSILON = 1e-05
NEGATIVE = -1e30
AXES = ("y", "xl", "z", "xh", "c")
BF = jnp.bfloat16
F32 = jnp.float32
MESH = pl.DeviceIdType.MESH
VMEM = pltpu.VMEM
DMA = pltpu.SemaphoreType.DMA
ANY = pl.BlockSpec(memory_space=pl.ANY)
INV = pl.BlockSpec(memory_space=pltpu.VMEM)
C0 = 0.7978845608028654
C1 = 0.044715


def div(a, b):
    return lax.div(a, jnp.int32(b))


def rem(a, b):
    return lax.rem(a, jnp.int32(b))


def place():
    y, xl, z, xh, c = (lax.axis_index(a) for a in AXES)
    return y, xl, z, xh, c


def send(src, dst, ss, rs, **dev):
    cp = pltpu.make_async_remote_copy(
        src_ref=src, dst_ref=dst, send_sem=ss, recv_sem=rs, device_id=dev, device_id_type=MESH
    )
    cp.start()


def local(src, dst, sem):
    pltpu.make_async_copy(src, dst, sem).start()


def landed(ref, sem):
    pltpu.make_async_copy(ref, ref, sem).wait()


def loop(n, body):
    lax.fori_loop(0, n, lambda i, _: (body(i), 0)[1], 0)


def signal(sem, **dev):
    pl.semaphore_signal(sem, inc=1, device_id=dev, device_id_type=MESH)


def greet_line(bar, z, c):
    for k in range(1, LINE):
        j = rem(2 * z + c + k, LINE)
        signal(bar, z=div(j, 2), c=rem(j, 2))


def greet_plane(bar, y, x):
    for k in range(1, 16):
        yy = rem(y + k // 4, 4)
        xx = rem(x + k % 4, 4)
        signal(bar, y=yy, xh=div(xx, 2), xl=rem(xx, 2))


def rows64(q):
    return pl.ds(pl.multiple_of(64 * q, 64), 64)


def second_rows(s, y):
    return (
        pl.ds(pl.multiple_of(64 * s + 16 * y, 16), 16),
        pl.ds(pl.multiple_of(128 + 256 * s + 64 * y, 16), 64),
    )


def half_cols(h):
    return pl.ds(pl.multiple_of(512 * h, 512), 512)


PARTS = (pl.ds(QKV, HID), pl.ds(0, QKV))


def weights_z(l, me, wqkv, win, wo, wfc, w1, w2, as_, ar, cs, cr):
    y, xl, z, xh, c, x, p, j = me
    mine = rows64(p)

    @pl.when((z == y) & (c == xl))
    def _():
        def to(jj):
            pairs = []
            for part in range(3):
                cols = pl.ds(pl.multiple_of(part * D + jj * 128, 128), 128)
                pairs.append((wqkv.at[l, :, cols], w1.at[l, mine, pl.ds(part * 128, 128)]))
            cols = pl.ds(pl.multiple_of(jj * HID, HID), HID)
            pairs.append((win.at[l, :, cols], w1.at[l, mine, PARTS[0]]))

            @pl.when(jj == j)
            def _():
                for i, (src, dst) in enumerate(pairs):
                    local(src, dst, ar.at[l])

            @pl.when(jj != j)
            def _():
                for i, (src, dst) in enumerate(pairs):
                    send(src, dst, as_.at[l], ar.at[l], z=div(jj, 2), c=rem(jj, 2))

        loop(LINE, to)

    quarter = (pl.ds(pl.multiple_of(16 * y, 16), 16), pl.ds(pl.multiple_of(64 * y, 64), 64))
    whole_rows = (
        pl.ds(pl.multiple_of(64 * c, 64), 64), pl.ds(pl.multiple_of(128 + 256 * c, 64), 256)
    )
    place_rows = second_rows(c, y)
    for i, w in enumerate((wo, wfc)):
        cols = half_cols(xl)
        dst = w2.at[l, place_rows[i], cols]
        send(
            w.at[l, quarter[i], cols], dst, cs.at[l, 0], cr.at[l], xl=1 - xl, xh=1 - xh, c=xh
        )
        full = w2.at[l, whole_rows[i]]

        @pl.when(c == xh)
        def _():
            local(w.at[l], full, cr.at[l])

        @pl.when(c != xh)
        def _():
            send(w.at[l], full, cs.at[l, 1], cr.at[l], c=xh)


def along_y(y, d):
    return dict(y=rem(y + d, 4))


def along_x(x, d):
    xx = rem(x + d, 4)
    return dict(xh=div(xx, 2), xl=rem(xx, 2))


def plane_member(y, x, k):
    return {**along_y(y, div(k, 4)), **along_x(x, rem(k, 4))}


def pass_block(l, part, q, stage, me, w1, bs, br):
    y, xl, z, xh, c, x, p, j = me
    block = w1.at[l, rows64(q), PARTS[part]]
    for d in (1, 2, 3):
        dev = along_y(y, d) if part == stage else along_x(x, d)
        rs = br.at[l, 3 * part + d] if stage == 0 else br.at[l, 0]
        send(block, block, bs.at[l], rs, **dev)


def weights_p1(l, me, w1, ar, bs, br):
    y, xl, z, xh, c, x, p, j = me
    landed(w1.at[l, rows64(p)], ar.at[l])
    for stage in range(2):
        for part in range(2):
            pass_block(l, part, p, stage, me, w1, bs, br)


def weights_p2(l, me, w1, bs, br):
    y, xl, z, xh, c, x, p, j = me
    for d in (1, 3, 2):
        for part in range(2):
            q = 4 * rem(y + 4 - d, 4) + x if part == 0 else 4 * y + rem(x + 4 - d, 4)
            landed(w1.at[l, rows64(q), PARTS[part]], br.at[l, 3 * part + d])
            pass_block(l, part, q, 1, me, w1, bs, br)


def weights_f1(l, me, w2, cr, xs, xr):
    y, xl, z, xh, c, x, p, j = me

    @pl.when(xh != c)
    def _():
        landed(w2.at[l, pl.ds(0, 80)], cr.at[l])
        for s in range(2):
            for at in second_rows(s, y):
                block = w2.at[l, at, half_cols(1 - xl)]
                send(block, block, xs.at[l], xr.at[l], xl=1 - xl)


def weights_f2(l, me, w2, xr, ys, yr):
    y, xl, z, xh, c, x, p, j = me

    @pl.when(xh != c)
    def _():
        landed(w2.at[l, pl.ds(0, 80)], xr.at[l])
        for s in range(2):
            for at in second_rows(s, y):
                block = w2.at[l, at]
                for d in (1, 2, 3):
                    send(block, block, ys.at[l], yr.at[l], **along_y(y, d))


def weights_in1(l, w1, br):
    landed(w1.at[l, pl.ds(0, 768)], br.at[l, 0])


def weights_in2(l, me, w2, cr, yr):
    y, xl, z, xh, c, x, p, j = me

    @pl.when(xh == c)
    def _():
        landed(w2.at[l], cr.at[l])

    @pl.when(xh != c)
    def _():
        landed(w2.at[l, pl.ds(0, 480)], yr.at[l])


def weights_left(l, me, w1, w2, as_, cs, bs, xs, ys):
    y, xl, z, xh, c, x, p, j = me
    landed(w1.at[l, pl.ds(0, 960)], bs.at[l])
    landed(w2.at[l, pl.ds(0, 80), pl.ds(0, 512)], cs.at[l, 0])

    @pl.when(c != xh)
    def _():
        landed(w2.at[l, pl.ds(0, 320)], cs.at[l, 1])
        landed(w2.at[l, pl.ds(0, 80)], xs.at[l])
        landed(w2.at[l, pl.ds(0, 480)], ys.at[l])

    @pl.when((z == y) & (c == xl))
    def _():
        landed(w1.at[l, pl.ds(0, 448)], as_.at[l])


HALF = CAP // 2


def slot_of(z, c, k):
    return 2 * rem(z + k, 4) + c


def rows_sibling(buf, z, c, ss, rs):
    own = buf.at[2 * z + c]
    send(own, own, ss, rs.at[0], c=1 - c)


def rows_send(buf, z, c, ss, rs):
    a, b = buf.at[2 * z + c, pl.ds(0, HALF)], buf.at[2 * z + c, pl.ds(HALF, HALF)]
    up, down = dict(z=rem(z + 1, 4)), dict(z=rem(z + 3, 4))
    send(a, a, ss, rs.at[1], **up)
    send(b, b, ss, rs.at[3], **down)
    send(b, b, ss, rs.at[2], **up)
    send(a, a, ss, rs.at[4], **down)


def rows_pass(buf, z, c, ss, rs):
    lo, hi = slot_of(z, c, 3), slot_of(z, c, 1)
    a = buf.at[lo, pl.ds(0, HALF)]
    b = buf.at[hi, pl.ds(HALF, HALF)]
    landed(a, rs.at[1])
    send(a, a, ss, rs.at[5], z=rem(z + 1, 4))
    landed(b, rs.at[3])
    send(b, b, ss, rs.at[5], z=rem(z + 3, 4))


def rows_near(buf, z, c, ss, rs):
    lo, hi = slot_of(z, c, 3), slot_of(z, c, 1)
    landed(buf.at[lo, pl.ds(HALF, HALF)], rs.at[2])
    send(buf.at[lo], buf.at[lo], ss, rs.at[6], c=1 - c)
    landed(buf.at[hi, pl.ds(0, HALF)], rs.at[4])
    send(buf.at[hi], buf.at[hi], ss, rs.at[6], c=1 - c)


def rows_near_in(buf, rs):
    landed(buf.at[pl.ds(0, 2)], rs.at[6])


def rows_far(buf, z, c, ss, rs):
    far = buf.at[slot_of(z, c, 2)]
    landed(far, rs.at[5])
    send(far, far, ss, rs.at[7], c=1 - c)


def rows_far_in(buf, rs):
    landed(buf.at[0], rs.at[7])


def rows_left(buf, ss):
    landed(buf.at[pl.ds(0, 7)], ss)


def rows_before(k, buf, z, c, ss, rs):
    @pl.when(k == 0)
    def _():
        landed(buf.at[2 * z + 1 - c], rs.at[0])

    @pl.when((k == 1) & (c == 0))
    def _():
        rows_pass(buf, z, c, ss, rs)
        rows_near(buf, z, c, ss, rs)

    @pl.when((k == 2) & (c == 1))
    def _():
        rows_near(buf, z, c, ss, rs)

    @pl.when(((k == 1) & (c == 1)) | ((k == 2) & (c == 0)))
    def _():
        rows_near_in(buf, rs)

    @pl.when(k == 3)
    def _():
        @pl.when(c == 1)
        def _():
            rows_far(buf, z, c, ss, rs)

        rows_far_in(buf, rs)


def rows_midway(k, buf, z, c, ss, rs):
    @pl.when((k == 0) & (c == 1))
    def _():
        rows_send(buf, z, c, ss, rs)

    @pl.when((k == 1) & (c == 1))
    def _():
        rows_pass(buf, z, c, ss, rs)

    @pl.when((k == 2) & (c == 0))
    def _():
        rows_far(buf, z, c, ss, rs)


def slots(k, z):
    near = (k == 1) | (k == 2)
    chip = rem(z + jnp.where(k == 3, 2, 0), 4)
    first = jnp.where(near, 2 * rem(z + 3, 4) + k - 1, 2 * chip)
    second = jnp.where(near, 2 * rem(z + 1, 4) + k - 1, 2 * chip + 1)
    return near, first, second


def sums_send(k, z, c, partial, own, sibout, sibin, out, inn, sbs, sbr, rss, rsr):
    near, first, second = slots(k, z)
    far = jnp.where(k == 0, 0, 1)
    mine = near & (c == k - 1)
    base = first - jnp.where(near, 0, rem(first, 2))
    t0 = partial(jnp.where(near, first, base + 1 - c))
    m0 = jnp.where(near, 2, far)

    @pl.when(jnp.logical_not(mine))
    def _():
        sibout[m0] = t0.astype(BF)
        send(sibout.at[m0], sibin.at[m0], sbs, sbr.at[m0], c=1 - c)

    @pl.when(mine)
    def _():
        landed(sibin.at[2], sbr.at[2])
        out[0] = (t0 + sibin[2].astype(F32)).astype(BF)
        send(out.at[0], inn.at[0], rss, rsr, z=rem(z + 3, 4))

    t1 = partial(jnp.where(near, second, base + c))
    theirs = near & (c != k - 1)

    @pl.when(theirs)
    def _():
        sibout[3] = t1.astype(BF)
        send(sibout.at[3], sibin.at[3], sbs, sbr.at[3], c=1 - c)

    @pl.when(jnp.logical_not(theirs))
    def _():
        m1 = jnp.where(near, 3, far)
        landed(sibin.at[m1], sbr.at[m1])
        both = t1 + sibin[m1].astype(F32)

        @pl.when(k == 0)
        def _():
            own[...] = both

        @pl.when(k != 0)
        def _():
            o = jnp.where(near, 1, 2)
            out[o] = both.astype(BF)
            send(out.at[o], inn.at[o], rss, rsr, z=rem(z + jnp.where(near, 1, 2), 4))


def sums_total(own, inn, rsr):
    landed(inn, rsr)
    total = own[...]
    for i in range(3):
        total = total + inn[i].astype(F32)
    return total


def lanes(shape):
    return lax.broadcasted_iota(jnp.int32, shape, len(shape) - 1)


def turn(v, cos, sin):
    low = rem(lanes(v.shape), 64) < 16
    partner = jnp.where(low, pltpu.roll(v, 112, 1), pltpu.roll(v, 16, 1))
    return v * cos + partner * sin


def nt(a, b):
    return lax.dot_general(a, b, (((1,), (1,)), ((), ())), preferred_element_type=F32)


def tn(a, b):
    return lax.dot_general(a, b, (((0,), (0,)), ((), ())), preferred_element_type=F32)


def nn(a, b):
    return jnp.dot(a, b, preferred_element_type=F32)


def stats(x):
    centre = x - jnp.mean(x, axis=-1, keepdims=True)
    r = lax.rsqrt(jnp.mean(centre * centre, axis=-1, keepdims=True) + EPSILON)
    return centre, r


def expand(t):
    lane = lanes(t.shape)
    rot = rem(lane, 64) < ROT
    first = lane < 64
    cos = jnp.where(rot, jnp.where(first, t, pltpu.roll(t, 64, 1)), 1.0)
    sin = jnp.where(rot, jnp.where(first, pltpu.roll(t, 96, 1), pltpu.roll(t, 32, 1)), 0.0)
    return cos, sin, t[:, 64:65]


def expand(t):
    lane = lanes(t.shape)
    rot = rem(lane, 64) < ROT
    first = lane < 64
    cos = jnp.where(rot, jnp.where(first, t, pltpu.roll(t, 64, 1)), 1.0)
    sin = jnp.where(rot, jnp.where(first, pltpu.roll(t, 96, 1), pltpu.roll(t, 32, 1)), 0.0)
    return cos, sin, t[:, 64:65]


def normed_rows(l, x, vec):
    centre, r = stats(x[...])
    return (centre * r * vec[8 * l : 8 * l + 1, :] + vec[8 * l + 1 : 8 * l + 2, :]).astype(BF)


def forward_pass(
    l, z, c, vec, bins, w1, w2, tabs, nall, qkv, prob, a2, pre, raw, sums, rows, spill, early, hook
):
    ss, rs = rows
    row = 8 * l

    def step(i):
        k = jnp.where(i == 0, 3, jnp.where(i == 3, 0, i)) if early else i
        hook(i)
        if not early:
            rows_before(k, nall, z, c, ss, rs)
        _, sa, sb = slots(k, z)
        n = jnp.concatenate([nall[sa], nall[sb]], axis=0)
        raw[:, 0:QKV] = nn(n, w1[:, :QKV])
        val = nn(n, w1[:, QKV:]) + bins[row : row + 1, :]
        pre[sa] = val[:CAP]
        pre[sb] = val[CAP:]

        def act(i):
            u, t = div(i, 6), rem(i, 6)
            s = jnp.where(u == 0, sa, sb)
            at = pl.ds(pl.multiple_of(t * 32, 32), 32)
            v = pre[s, at, :]
            g = 0.5 * v * (1.0 + jnp.tanh(C0 * (v + C1 * v * v * v)))
            a2[s, at, 128:] = g.astype(BF)

        loop(12, act)
        if not early:
            rows_midway(k, nall, z, c, ss, rs)
        for u, s in enumerate((sa, sb)):
            at = slice(u * CAP, (u + 1) * CAP)
            cos, sin, start = expand(tabs[s])
            q = turn(raw[at, 0:128], cos, sin).astype(BF)
            kk = turn(raw[at, 128:256], cos, sin).astype(BF)
            v = raw[at, 256:384].astype(BF)
            qkv[s, :, 0:128] = q
            qkv[s, :, 128:256] = kk
            qkv[s, :, 256:384] = v
            q = q * jnp.asarray(1.0 / math.sqrt(HEAD), BF)
            key_at = lanes((CAP, CAP))
            query_at = lax.broadcasted_iota(jnp.int32, (CAP, CAP), 0)
            allowed = (key_at >= start.astype(jnp.int32)) & (key_at <= query_at)
            head = lanes((CAP, 128)) < HEAD
            mixed = []
            for h in range(2):
                qh = jnp.where(head if h == 0 else ~head, q, jnp.zeros_like(q))
                score = jnp.where(allowed, nt(qh, kk), NEGATIVE)
                e = jnp.exp(score - jnp.max(score, axis=-1, keepdims=True))
                w = e / jnp.sum(e, axis=-1, keepdims=True)
                prob[2 * s + h] = w
                mixed.append(nn(w.astype(BF), v))
            a2[s, :, 0:128] = jnp.where(head, mixed[0], mixed[1]).astype(BF)
        if spill is not None:
            prob_o, pre_o, sem = spill
            for s in (sa, sb):
                local(prob.at[pl.ds(2 * s, 2)], prob_o.at[pl.ds(2 * s, 2)], sem.at[0])
                local(pre.at[s], pre_o.at[s], sem.at[1])
        hook(i, 1)
        sums_send(k, z, c, lambda s: nn(a2[s], w2[...]), *sums)

    loop(4, step)


def forward_rows(l, x, vec, sums):
    own, _, _, out, inn, _, _, rss, rsr = sums
    return x[...] + (sums_total(own, inn, rsr) + vec[8 * l + 2 : 8 * l + 3, :])


def backward_pass(
    z, c, w1, w2, tabs, qkv, prob, pre, raw, gall, dp, sums, rows, early, hook
):
    ss, rs = rows

    def step(i):
        k = jnp.where(i == 0, 3, jnp.where(i == 3, 0, i)) if early else i
        hook(i)
        if not early:
            rows_before(k, gall, z, c, ss, rs)
        _, sa, sb = slots(k, z)
        g = jnp.concatenate([gall[sa], gall[sb]], axis=0)
        raw[...] = nt(g, w2[...])

        def act(i):
            u, t = div(i, 12), rem(i, 12)
            s = jnp.where(u == 0, sa, sb)
            at = pl.ds(pl.multiple_of(t * 16, 16), 16)
            v = pre[s, at, :]
            d = raw[pl.ds(pl.multiple_of(u * CAP + t * 16, 16), 16), 128:]
            t1 = jnp.tanh(C0 * (v + C1 * v * v * v))
            slope = 0.5 * (1.0 + t1) + 0.5 * v * (1.0 - t1 * t1) * (C0 + (3.0 * C0 * C1) * v * v)
            dp[s, at, QKV:] = (d * slope).astype(BF)

        loop(24, act)
        if not early:
            rows_midway(k, gall, z, c, ss, rs)
        for u, s in enumerate((sa, sb)):
            at = slice(u * CAP, (u + 1) * CAP)
            cos, sin, _ = expand(tabs[s])
            m = raw[at, 0:128].astype(BF)
            q, kk, v = qkv[s, :, 0:128], qkv[s, :, 128:256], qkv[s, :, 256:384]
            head = lanes((CAP, 128)) < HEAD
            dq, dk, dv = [], [], []
            for h in range(2):
                mine = head if h == 0 else ~head
                mh = jnp.where(mine, m, jnp.zeros_like(m))
                w = prob[2 * s + h]
                soft = nt(mh, v)
                dv.append(tn(w.astype(BF), mh))
                wd = w * soft
                ds = (wd - w * jnp.sum(wd, axis=-1, keepdims=True)).astype(BF)
                dq.append(nn(ds, kk))
                dk.append(tn(ds, jnp.where(mine, q, jnp.zeros_like(q))))
            scale = 1.0 / math.sqrt(HEAD)
            dq = jnp.where(head, dq[0], dq[1]) * scale
            dk = (dk[0] + dk[1]) * scale
            dp[s, :, 0:128] = turn(dq, cos, -sin).astype(BF)
            dp[s, :, 128:256] = turn(dk, cos, -sin).astype(BF)
            dp[s, :, 256:384] = (dv[0] + dv[1]).astype(BF)
        sums_send(k, z, c, lambda s: nt(dp[s], w1[...]), *sums)

    loop(4, step)


def second_grads(a2, gall, g2):
    rows = LINE * CAP
    g = gall[...].reshape(rows, D)
    val = tn(a2[...].reshape(rows, DEEP), g)
    for s in range(2):
        for q in range(4):
            g2[s, q, 0:16, :] = val[64 * s + 16 * q : 64 * s + 16 * q + 16].astype(BF)
            base = 128 + 256 * s + 64 * q
            g2[s, q, 16:80, :] = val[base : base + 64].astype(BF)


def first_grads(nall, dp, g1q, g1i):
    rows = LINE * CAP
    d = dp[...].reshape(rows, WIDE)
    for t in range(2):
        val = tn(nall[:, :, t * 512 : (t + 1) * 512].reshape(rows, 512), d).astype(BF)
        for s in range(8):
            sh = 8 * t + s
            zz, hh, cc = sh // 4, (sh // 2) % 2, sh % 2
            for q in range(4):
                part = val[64 * s + 16 * q : 64 * s + 16 * q + 16]
                at = (2 * zz + cc) * 16
                g1q[hh, q, at : at + 16, :] = part[:, :QKV]
                g1i[hh, q, at : at + 16, :] = part[:, QKV:]


def backward_rows(l, z, c, g_ref, x, vec, gall, dp, lns, loc, sums):
    zero = jnp.zeros((1, 128), F32)
    col = pl.ds(pl.multiple_of((2 * z + c) * 128, 128), 128)
    bfc = jnp.zeros((1, 128), F32)
    b_in = jnp.zeros((1, HID), F32)
    for s in range(LINE):
        bfc = bfc + jnp.sum(gall[s, :, col].astype(F32), axis=0, keepdims=True)
        b_in = b_in + jnp.sum(dp[s, :, QKV:].astype(F32), axis=0, keepdims=True)
    loc[...] = jnp.concatenate(
        [zero, zero, bfc] + [b_in[:, 128 * i : 128 * i + 128] for i in range(4)] + [zero], axis=0
    )
    own, _, _, out, inn, _, _, rss, rsr = sums
    ngrad = sums_total(own, inn, rsr)
    centre, r = stats(x[...])
    xhat = centre * r
    e = ngrad * vec[8 * l : 8 * l + 1, :]
    ex = jnp.mean(e * xhat, axis=-1, keepdims=True)
    gain = jnp.sum(ngrad * xhat, axis=0, keepdims=True)
    bias = jnp.sum(ngrad, axis=0, keepdims=True)
    both = jnp.concatenate([gain, bias] + [jnp.zeros((6, D), F32)], axis=0)
    for i in range(LINE):
        lns[i] = both[:, 128 * i : 128 * i + 128]
    return g_ref[...] + r * (e - jnp.mean(e, axis=-1, keepdims=True) - xhat * ex)


def member(jj):
    return dict(z=div(jj, 2), c=rem(jj, 2))


def small_start(l, me, lns, zs, s5, q5):
    j = me[7]

    def go(k):
        jj = rem(j + k, LINE)
        send(lns.at[l, jj], zs.at[l, j], s5.at[l], q5.at[l], **member(jj))

    loop(LINE - 1, lambda k: go(k + 1))


def small_spread(l, me, lns, loc, zs, ps, q5, s6, q6):
    y, xl, z, xh, c, x, p, j = me

    landed(zs.at[l, pl.ds(0, LINE - 1)], q5.at[l])
    zs[l, j] = lns[l, j] + loc[l]
    total = zs[l, 0]
    for i in range(1, LINE):
        total = total + zs[l, i]
    ps[l, p] = total

    def spread(k):
        send(ps.at[l, p], ps.at[l, p], s6.at[l], q6.at[l], **plane_member(y, x, k))

    loop(15, lambda k: spread(k + 1))


def small_last(l, me, ps, tot, q6, s8, q8):
    y, xl, z, xh, c, x, p, j = me

    landed(ps.at[l, pl.ds(0, 15)], q6.at[l])
    total = ps[l, 0]
    for i in range(1, 16):
        total = total + ps[l, i]
    tot[l, c] = total
    send(tot.at[l, c], tot.at[l, c], s8.at[l], q8.at[l], c=1 - c)


def second_p1(l, me, g2, ga1, gb1, s, q):
    y, xl, z, xh, c, x, p, j = me
    left, right = pl.ds(0, 512), pl.ds(512, 512)
    for d in (1, 2, 3):
        dev = along_x(x, d)

        @pl.when(dev["xh"] == c)
        def _():
            send(
                g2.at[dev["xl"], :, :, left], ga1.at[l, d - 1], s.at[l, 0], q.at[l, 0], **dev
            )

        yy = along_y(y, d)
        send(g2.at[:, yy["y"], :, right], gb1.at[l, d - 1], s.at[l, 1], q.at[l, 1], **yy)


def second_p2(l, me, g2, ga1, gb1, ga2, gb2, sga, sgb, s, q):
    y, xl, z, xh, c, x, p, j = me
    landed(gb1.at[l], q.at[l, 1])

    def add_right(i):
        h, t = div(i, 5), rem(i, 5)
        at = pl.ds(pl.multiple_of(16 * t, 16), 16)
        acc = g2[h, y, at, 512:].astype(F32)
        for d in range(3):
            acc = acc + gb1[l, d, h, at, :].astype(F32)
        sgb[h, at, :] = acc.astype(BF)

    loop(10, add_right)
    for d in (1, 2, 3):
        dev = along_x(x, d)

        @pl.when(dev["xh"] == c)
        def _():
            send(sgb.at[dev["xl"]], gb2.at[l, d - 1], s.at[l, 2], q.at[l, 2], **dev)

    @pl.when(xh == c)
    def _():
        landed(ga1.at[l], q.at[l, 0])

        def add_left(i):
            yy, t = div(i, 5), rem(i, 5)
            at = pl.ds(pl.multiple_of(16 * t, 16), 16)
            acc = g2[xl, yy, at, 0:512].astype(F32)
            for d in range(3):
                acc = acc + ga1[l, d, yy, at, :].astype(F32)
            sga[yy, at, :] = acc.astype(BF)

        loop(20, add_left)
        for d in (1, 2, 3):
            yy = along_y(y, d)
            send(sga.at[yy["y"]], ga2.at[l, d - 1], s.at[l, 3], q.at[l, 3], **yy)


def second_p3(l, me, ga2, gb2, sga, sgb, red2, fo, ff, s, q, s4, q4):
    y, xl, z, xh, c, x, p, j = me
    row16 = pl.ds(pl.multiple_of(16 * y, 16), 16)
    row64 = pl.ds(pl.multiple_of(64 * y, 64), 64)

    @pl.when(xh == c)
    def _():
        landed(gb2.at[l], q.at[l, 2])
        landed(ga2.at[l], q.at[l, 3])

        def add(t):
            at = pl.ds(pl.multiple_of(16 * t, 16), 16)
            a = sga[y, at, :].astype(F32)
            b = sgb[xl, at, :].astype(F32)
            for d in range(3):
                a = a + ga2[l, d, at, :].astype(F32)
                b = b + gb2[l, d, at, :].astype(F32)
            red2[l, at, 0:512] = a.astype(BF)
            red2[l, at, 512:1024] = b.astype(BF)

        loop(5, add)

        parts = (
            (red2.at[l, pl.ds(0, 16)], fo.at[l, row16]),
            (red2.at[l, pl.ds(16, 64)], ff.at[l, row64]),
        )
        for src, dst in parts:
            send(src, dst, s4.at[l, 0], q4.at[l, 0], xl=1 - xl, c=xl)

            @pl.when(xl == c)
            def _():
                local(src, dst, q4.at[l, 0])

            @pl.when(xl != c)
            def _():
                send(src, dst, s4.at[l, 1], q4.at[l, 0], c=xl)


def second_share(l, me, w2, fo, ff, q4, s4):
    y = me[0]
    row16 = pl.ds(pl.multiple_of(16 * y, 16), 16)
    row64 = pl.ds(pl.multiple_of(64 * y, 64), 64)
    landed(w2.at[l, pl.ds(0, 80)], q4.at[l, 0])
    for block in (fo.at[l, row16], ff.at[l, row64]):
        for d in (1, 2, 3):
            send(block, block, s4.at[l, 2], q4.at[l, 1], **along_y(y, d))


def second_left(l, me, ga1, gb1, ga2, gb2, s):
    y, xl, z, xh, c, x, p, j = me
    landed(gb1.at[l], s.at[l, 1])
    for same, n in ((True, 1), (False, 2)):

        @pl.when((xh == c) if same else (xh != c))
        def _():
            landed(ga1.at[l, pl.ds(0, n)], s.at[l, 0])
            landed(gb2.at[l, pl.ds(0, n)], s.at[l, 2])

    @pl.when(xh == c)
    def _():
        landed(ga2.at[l], s.at[l, 3])


def by_kind(ll, f):
    @pl.when(ll == 0)
    def _():
        f(pl.ds(0, QKV), 0)

    @pl.when(ll == 1)
    def _():
        f(pl.ds(0, HID), 1)


TOP, LOW = pl.ds(0, 64), pl.ds(64, 64)


def first_p1(l, me, g1q, g1i, ra1, rbq, rbi, s, q):
    y, xl, z, xh, c, x, p, j = me
    for d in (1, 2, 3):
        dev = along_x(x, d)
        hh = dev["xh"]

        def go(cols, kind):
            src = (g1q, g1i)[kind].at[hh, :, TOP]
            send(src, ra1.at[l, d - 1, :, :, cols], s.at[l, d], q.at[l, 0], **dev)

        by_kind(dev["xl"], go)
        yy = along_y(y, d)
        send(g1q.at[:, yy["y"], LOW], rbq.at[l, d - 1], s.at[l, 0], q.at[l, 1], **yy)
        send(g1i.at[:, yy["y"], LOW], rbi.at[l, d - 1], s.at[l, 0], q.at[l, 1], **yy)


def first_p2(l, me, w1, g1q, g1i, ra1, rbq, rbi, ra2, rb2, sra, sbq, sbi, s, q):
    y, xl, z, xh, c, x, p, j = me
    by_kind(xl, lambda cols, kind: landed(ra1.at[l, :, :, :, cols], q.at[l, 0]))

    def add_top(i):
        yy, t = div(i, 4), rem(i, 4)
        at = pl.ds(pl.multiple_of(16 * t, 16), 16)

        def go(cols, kind):
            acc = (g1q, g1i)[kind][xh, yy, at, :].astype(F32)
            for d in range(3):
                acc = acc + ra1[l, d, yy, at, cols].astype(F32)
            sra[yy, at, cols] = acc.astype(BF)

        by_kind(xl, go)

    loop(16, add_top)
    for d in (1, 2, 3):
        yy = along_y(y, d)

        def go(cols, kind):
            src = sra.at[yy["y"], :, cols]
            send(src, ra2.at[l, d - 1, :, cols], s.at[l, 4], q.at[l, 2], **yy)

        by_kind(xl, go)
    landed(w1.at[l, pl.ds(0, 384)], q.at[l, 1])

    def add_low(i):
        h, t = div(i, 4), rem(i, 4)
        at = pl.ds(pl.multiple_of(16 * t, 16), 16)
        here = pl.ds(pl.multiple_of(64 + 16 * t, 16), 16)
        a = g1q[h, y, here, :].astype(F32)
        b = g1i[h, y, here, :].astype(F32)
        for d in range(3):
            a = a + rbq[l, d, h, at, :].astype(F32)
            b = b + rbi[l, d, h, at, :].astype(F32)
        sbq[h, at, :] = a.astype(BF)
        sbi[h, at, :] = b.astype(BF)

    loop(8, add_low)
    for d in (1, 2, 3):
        dev = along_x(x, d)
        hh = dev["xh"]

        def go(cols, kind):
            src = (sbq, sbi)[kind].at[hh]
            send(src, rb2.at[l, d - 1, :, cols], s.at[l, 4 + d], q.at[l, 3], **dev)

        by_kind(dev["xl"], go)


def first_p3(l, me, ra2, rb2, sra, sbq, sbi, red1, fq, fi, s, q, s3, q3):
    y, xl, z, xh, c, x, p, j = me
    by_kind(xl, lambda cols, kind: landed(ra2.at[l, :, :, cols], q.at[l, 2]))
    by_kind(xl, lambda cols, kind: landed(rb2.at[l, :, :, cols], q.at[l, 3]))

    def add(t):
        at = pl.ds(pl.multiple_of(16 * t, 16), 16)

        def go(cols, kind):
            a = sra[y, at, cols].astype(F32)
            b = (sbq, sbi)[kind][xh, at, :].astype(F32)
            for d in range(3):
                a = a + ra2[l, d, at, cols].astype(F32)
                b = b + rb2[l, d, at, cols].astype(F32)
            red1[l, at, cols] = a.astype(BF)
            red1[l, pl.ds(pl.multiple_of(64 + 16 * t, 16), 16), cols] = b.astype(BF)

        by_kind(xl, go)

    loop(4, add)
    row16 = pl.ds(pl.multiple_of(16 * y, 16), 16)

    def back(jj):
        at = pl.ds(pl.multiple_of(16 * jj, 16), 16)

        def move(src, dst):
            @pl.when(jj == j)
            def _():
                local(src, dst, q3.at[l])

            @pl.when(jj != j)
            def _():
                send(src, dst, s3.at[l], q3.at[l], **member(jj))

        @pl.when(xl == 0)
        def _():
            for n in range(3):
                cols = pl.ds(pl.multiple_of(n * D + 128 * j, 128), 128)
                move(red1.at[l, at, pl.ds(128 * n, 128)], fq.at[l, row16, cols])

        @pl.when(xl == 1)
        def _():
            cols = pl.ds(pl.multiple_of(HID * j, HID), HID)
            move(red1.at[l, at], fi.at[l, row16, cols])

    loop(LINE, back)


def first_left(l, me, w1, ra1, ra2, rb2, s):
    y, xl, z, xh, c, x, p, j = me
    landed(w1.at[l, pl.ds(0, 384)], s.at[l, 0])
    for d in (1, 2, 3):
        there = along_x(x, d)["xl"]
        by_kind(there, lambda cols, kind: landed(ra1.at[l, 0, :, :, cols], s.at[l, d]))
        by_kind(there, lambda cols, kind: landed(rb2.at[l, 0, :, cols], s.at[l, 4 + d]))
    by_kind(xl, lambda cols, kind: landed(ra2.at[l, :, :, cols], s.at[l, 4]))


def first_share(l, me, fq, fi, q3, s7, q7):
    y, xl, z, xh, c, x, p, j = me
    row16 = pl.ds(pl.multiple_of(16 * y, 16), 16)

    for v, f in ((0, fq), (1, fi)):

        @pl.when(xl == v)
        def _():
            landed(f.at[l, row16], q3.at[l])

            at = f.at[l, row16]
            for d in (1, 2, 3):
                send(at, at, s7.at[l], q7.at[l, d], **along_y(y, d))
            send(at, at, s7.at[l], q7.at[l, 0], xl=1 - xl)


def first_pass(l, me, fq, fi, s7, q7):
    y, xl, z, xh, c, x, p, j = me
    for v, f in ((0, fq), (1, fi)):

        @pl.when(xl == v)
        def _():
            for d in (1, 3, 2):
                at = f.at[l, pl.ds(pl.multiple_of(16 * rem(y + 4 - d, 4), 16), 16)]
                landed(at, q7.at[l, d])
                send(at, at, s7.at[l], q7.at[l, 0], xl=1 - xl)


def owners_in(l, me, w2, fq, fi, q4, q7):
    xl = me[1]
    landed(w2.at[l, pl.ds(0, 240)], q4.at[l, 1])
    for v, f in ((0, fq), (1, fi)):

        @pl.when(xl != v)
        def _():
            landed(f.at[l], q7.at[l, 0])


def owners_left(l, me, w2, lns, ps, tot, red1, s3, s4, s5, s6, s7, s8):
    y, xl, z, xh, c, x, p, j = me
    landed(lns.at[l, pl.ds(0, LINE - 1)], s5.at[l])
    landed(ps.at[l, pl.ds(0, 15)], s6.at[l])
    landed(w2.at[l, pl.ds(0, 240)], s4.at[l, 2])

    @pl.when(xh == c)
    def _():
        landed(w2.at[l, pl.ds(0, 80)], s4.at[l, 0])

        @pl.when(xl != c)
        def _():
            landed(w2.at[l, pl.ds(0, 80)], s4.at[l, 1])

    by_kind(xl, lambda cols, kind: landed(red1.at[l, pl.ds(0, 112), cols], s3.at[l]))
    for v, unit in ((0, 48), (1, 64)):

        @pl.when(xl == v)
        def _():
            landed(w2.at[l, pl.ds(0, 7 * unit)], s7.at[l])

    landed(tot.at[l, c], s8.at[l])


def no_hook(*a):
    pass


def used_rows(len_ref):
    total = len_ref[0, 0]
    for k in range(1, SLOTS):
        total = total + len_ref[0, k]
    return lax.broadcasted_iota(jnp.int32, (CAP, 128), 0) < total


def make_table(row_of_lengths):
    shape = (CAP, 128)
    row = lax.broadcasted_iota(jnp.int32, shape, 0).astype(F32)
    lane = lanes(shape)
    start = jnp.zeros(shape, F32)
    end = jnp.zeros((1, 1), F32)
    for k in range(SLOTS):
        n = row_of_lengths[:, k : k + 1]
        end = end + n
        start = start + jnp.where(row >= end, n, 0.0)
    which = rem(lane, ROT // 2).astype(F32)
    angle = (row - start) * jnp.exp(which * (-2.0 * math.log(10000.0) / ROT))
    sine = jnp.sin(angle)
    sine = jnp.where(rem(lane, ROT) < ROT // 2, -sine, sine)
    return jnp.where(lane < 32, jnp.cos(angle), jnp.where(lane < 64, sine, start))


def whole_kernel(
    wqkv, win, wo, wfc, len_ref, gain_ref, bias_ref, bfc_ref, bin_ref, x0, cot,
    x2_o, g0_ref, fs_ref, fq, fi, fo, ff, prob_o, pre_o,
    w1, w2, sm, lens, sma, tabs, vec, bins,
    nall, qkv, a2, prob, pre, raw, gall, dp, x1,
    own, sibout, sibin, out, inn, own1, out1, inn1,
    g1q, g1i, g2, lns, loc, ga1, gb1, ga2, gb2, sga, sgb, ra1, rbq, rbi, ra2, rb2, sra, sbq, sbi,
    red1, red2, zs, ps, tot,
    as_, ar, bs, br, cs, cr, xs, xr, ys, yr, ts, tr, ms, mr, ns, nr,
    rows_s, rows_r, sbs, sbr, rss, rsr, spill, fill, x2s,
    s1, q1, s2, q2, s3, q3, s4, q4, s5, q5, s6, q6, s7, q7, s8, q8,
):
    y, xl, z, xh, c = place()
    x = 2 * xh + xl
    p = 4 * y + x
    j = 2 * z + c
    me = (y, xl, z, xh, c, x, p, j)
    bar = pltpu.get_barrier_semaphore()
    greet_line(bar, z, c)
    greet_plane(bar, y, x)
    for k in range(1, 8):
        signal(bar, y=rem(y + k // 2, 4), xl=rem(xl + k % 2, 2), c=1 - c)
    signal(bar, xl=1 - xl, xh=1 - xh, c=1 - c)

    source = (z == y) & (c == xl)
    sm[...] = jnp.zeros(sm.shape, F32)
    for r, ref in enumerate((gain_ref, bias_ref, bfc_ref)):
        v = ref[...].astype(F32)
        v = jnp.concatenate([v, v], axis=1)
        for l in range(LAYERS):
            sm[8 * l + r : 8 * l + r + 1, 0:128] = v[l : l + 1]
    v = bin_ref[...].astype(F32)
    for l in range(LAYERS):
        sm[8 * l + 3 : 8 * l + 4, :] = v[l : l + 1]
    tile = lanes((8, 128))
    mine = jnp.zeros((8, 128), F32)
    for k in range(SLOTS):
        mine = mine + jnp.where(tile == k, len_ref[0, k].astype(F32), 0.0)
    lens[j] = mine
    used = used_rows(len_ref)[:, 0:1]
    gall[1, 2 * z + c] = jnp.where(used, cot[...], 0.0).astype(BF)
    pl.semaphore_wait(bar, 30)

    @pl.when(source)
    def _():
        def to(jj):
            @pl.when(jj == j)
            def _():
                local(sm, sma.at[p], mr)

            @pl.when(jj != j)
            def _():
                send(sm, sma.at[p], ms, mr, **member(jj))

        loop(LINE, to)

    for k in range(1, LINE):
        send(lens.at[j], lens.at[j], ts, tr, **member(rem(j + k, LINE)))
    weights_z(0, me, wqkv, win, wo, wfc, w1, w2, as_, ar, cs, cr)
    g1 = gall.at[1]
    gs, gr = rows_s.at[2], rows_r.at[2]
    rows_sibling(g1, z, c, gs, gr)
    rows_send(g1, z, c, gs, gr)
    landed(sma.at[p], mr)

    def small_out(k):
        send(sma.at[p], sma.at[p], ns, nr, **plane_member(y, x, k))

    loop(15, lambda k: small_out(k + 1))
    weights_f1(0, me, w2, cr, xs, xr)
    weights_p1(0, me, w1, ar, bs, br)
    landed(sma.at[pl.ds(0, 15)], nr)
    half = lanes((16, 128)) < 64
    for t in range(8):
        vec[:, 128 * t : 128 * t + 128] = jnp.where(half, sma[2 * t, :, :128], sma[2 * t + 1, :, :128])
    for l in range(LAYERS):
        at = 8 * l + 3
        bins[8 * l : 8 * l + 1, 0:256] = sma[2 * j, at : at + 1, :]
        bins[8 * l : 8 * l + 1, 256:512] = sma[2 * j + 1, at : at + 1, :]

    def sums_of(n):
        sems = sbs.at[n], sbr.at[n], rss.at[n], rsr.at[n]
        if n == 1:
            return (own1, gall.at[0, pl.ds(0, 4)], gall.at[0, pl.ds(4, 4)], out1, inn1) + sems
        return (own, sibout, sibin, out, inn) + sems

    def rows_of(n):
        return rows_s.at[n], rows_r.at[n]

    n0 = nall.at[0]
    ss, rs = rows_of(0)
    n0[2 * z + c] = normed_rows(0, x0, vec)
    rows_sibling(n0, z, c, ss, rs)
    rows_send(n0, z, c, ss, rs)
    weights_f2(0, me, w2, xr, ys, yr)
    rows_pass(g1, z, c, gs, gr)
    landed(lens.at[pl.ds(0, LINE - 1)], tr)

    def table(s):
        tabs[s] = make_table(lens[s, 0:1, :])

    loop(LINE, table)
    weights_p2(0, me, w1, bs, br)
    rows_near(g1, z, c, gs, gr)
    rows_pass(n0, z, c, ss, rs)
    rows_far(g1, z, c, gs, gr)
    rows_near(n0, z, c, ss, rs)
    rows_far(n0, z, c, ss, rs)
    for buf, rr in ((n0, rs), (g1, gr)):
        landed(buf.at[0], rr.at[0])
        rows_near_in(buf, rr)
    weights_in1(0, w1, br)
    for buf, rr in ((n0, rs), (g1, gr)):
        rows_far_in(buf, rr)
    weights_z(1, me, wqkv, win, wo, wfc, w1, w2, as_, ar, cs, cr)

    def hook_f0(i, late=0):
        if late:

            @pl.when(i == 0)
            def _():
                weights_in2(0, me, w2, cr, yr)

        else:

            @pl.when(i == 1)
            def _():
                weights_p1(1, me, w1, ar, bs, br)

            @pl.when(i == 2)
            def _():
                weights_f1(1, me, w2, cr, xs, xr)
                weights_p2(1, me, w1, bs, br)

            @pl.when(i == 3)
            def _():
                weights_f2(1, me, w2, xr, ys, yr)

    forward_pass(
        0, z, c, vec, bins, w1.at[0], w2.at[0], tabs, n0, qkv.at[0], prob, a2.at[0], pre,
        raw, sums_of(0), rows_of(0), (prob_o, pre_o, spill), True, hook_f0,
    )
    x1[...] = forward_rows(0, x0, vec, sums_of(0))

    n1 = nall.at[1]
    ss, rs = rows_of(1)
    n1[2 * z + c] = normed_rows(1, x1, vec)
    rows_sibling(n1, z, c, ss, rs)

    @pl.when(c == 0)
    def _():
        rows_send(n1, z, c, ss, rs)

    rows_left(n0, rows_s.at[0])
    rows_left(g1, gs)
    landed(sibout, sbs.at[0])
    landed(out, rss.at[0])
    landed(prob, spill.at[0])
    landed(pre, spill.at[1])
    weights_in1(1, w1, br)
    weights_in2(1, me, w2, cr, yr)
    forward_pass(
        1, z, c, vec, bins, w1.at[1], w2.at[1], tabs, n1, qkv.at[1], prob, a2.at[1], pre,
        raw, sums_of(1), rows_of(1), None, False, no_hook,
    )

    second_grads(a2.at[1], g1, g2)
    second_p1(1, me, g2, ga1, gb1, s2, q2)
    landed(sibout, sbs.at[1])

    def hook1(i):
        @pl.when(i == 2)
        def _():
            second_p2(1, me, g2, ga1, gb1, ga2, gb2, sga, sgb, s2, q2)

        @pl.when(i == 3)
        def _():
            second_p3(1, me, ga2, gb2, sga, sgb, red2, fo, ff, s2, q2, s4, q4)

    backward_pass(
        z, c, w1.at[1], w2.at[1], tabs, qkv.at[1], prob, pre, raw, g1, dp, sums_of(2), rows_of(2), True,
        hook1,
    )
    local(prob_o, prob, fill.at[0])
    local(pre_o, pre, fill.at[1])
    first_grads(n1, dp, g1q, g1i)
    first_p1(1, me, g1q, g1i, ra1, rbq, rbi, s1, q1)
    second_share(1, me, w2, fo, ff, q4, s4)
    own1[...] = forward_rows(1, x1, vec, sums_of(1))
    local(own1, x2_o, x2s)
    g0_ref[...] = jnp.where(used_rows(len_ref)[:, 0:1], cot[...], 0.0)
    g0_ref[...] = backward_rows(1, z, c, g0_ref, x1, vec, g1, dp, lns.at[1], loc.at[1], sums_of(2))

    g0 = gall.at[0]
    ss, rs = rows_of(3)
    g0[2 * z + c] = g0_ref[...].astype(BF)
    rows_sibling(g0, z, c, ss, rs)

    @pl.when(c == 0)
    def _():
        rows_send(g0, z, c, ss, rs)

    small_start(1, me, lns, zs, s5, q5)
    rows_left(n1, rows_s.at[1])
    landed(out1, rss.at[1])
    landed(sibout, sbs.at[2])
    landed(out, rss.at[2])
    landed(prob, fill.at[0])
    landed(pre, fill.at[1])

    def hook0(i):
        @pl.when(i == 1)
        def _():
            small_spread(1, me, lns, loc, zs, ps, q5, s6, q6)
            first_p2(1, me, w1, g1q, g1i, ra1, rbq, rbi, ra2, rb2, sra, sbq, sbi, s1, q1)

        @pl.when(i == 2)
        def _():
            second_left(1, me, ga1, gb1, ga2, gb2, s2)
            first_p3(1, me, ra2, rb2, sra, sbq, sbi, red1, fq, fi, s1, q1, s3, q3)

        @pl.when(i == 3)
        def _():
            first_share(1, me, fq, fi, q3, s7, q7)
            first_left(1, me, w1, ra1, ra2, rb2, s1)

    backward_pass(
        z, c, w1.at[0], w2.at[0], tabs, qkv.at[0], prob, pre, raw, g0, dp, sums_of(3), rows_of(3), False,
        hook0,
    )
    second_grads(a2.at[0], g0, g2)
    second_p1(0, me, g2, ga1, gb1, s2, q2)
    first_pass(1, me, fq, fi, s7, q7)
    first_grads(n0, dp, g1q, g1i)
    first_p1(0, me, g1q, g1i, ra1, rbq, rbi, s1, q1)
    small_last(1, me, ps, tot, q6, s8, q8)
    second_p2(0, me, g2, ga1, gb1, ga2, gb2, sga, sgb, s2, q2)
    g0_ref[...] = backward_rows(0, z, c, g0_ref, x0, vec, g0, dp, lns.at[0], loc.at[0], sums_of(3))
    small_start(0, me, lns, zs, s5, q5)
    second_p3(0, me, ga2, gb2, sga, sgb, red2, fo, ff, s2, q2, s4, q4)
    first_p2(0, me, w1, g1q, g1i, ra1, rbq, rbi, ra2, rb2, sra, sbq, sbi, s1, q1)
    small_spread(0, me, lns, loc, zs, ps, q5, s6, q6)
    second_share(0, me, w2, fo, ff, q4, s4)
    first_p3(0, me, ra2, rb2, sra, sbq, sbi, red1, fq, fi, s1, q1, s3, q3)
    small_last(0, me, ps, tot, q6, s8, q8)
    first_share(0, me, fq, fi, q3, s7, q7)
    first_pass(0, me, fq, fi, s7, q7)

    rows_left(g0, rows_s.at[3])
    landed(sibout, sbs.at[3])
    landed(out, rss.at[3])
    second_left(0, me, ga1, gb1, ga2, gb2, s2)
    first_left(0, me, w1, ra1, ra2, rb2, s1)
    for l in range(LAYERS):
        weights_left(l, me, w1, w2, as_, cs, bs, xs, ys)
    landed(lens.at[pl.ds(0, LINE - 1)], ts)
    landed(sma.at[pl.ds(0, 15)], ns)
    landed(own1, x2s)

    @pl.when(source)
    def _():
        landed(sma.at[pl.ds(0, LINE - 1)], ms)

    for l in (1, 0):
        landed(tot.at[l, 1 - c], q8.at[l])
        fs_ref[l] = tot[l]
        owners_in(l, me, w2, fq, fi, q4, q7)
        owners_left(l, me, w2, lns, ps, tot, red1, s3, s4, s5, s6, s7, s8)


def whole(wqkv, win, wo, wfc, lengths, gain, bias, b_fc, b_in, x0, cot):
    n = LAYERS
    return pl.pallas_call(
        whole_kernel,
        out_shape=(
            jax.ShapeDtypeStruct((CAP, D), F32),
            jax.ShapeDtypeStruct((CAP, D), F32),
            jax.ShapeDtypeStruct((n, 2, 8, 128), F32),
            jax.ShapeDtypeStruct((n, 64, 3 * D), BF),
            jax.ShapeDtypeStruct((n, 64, FF), BF),
            jax.ShapeDtypeStruct((n, 64, D), BF),
            jax.ShapeDtypeStruct((n, 256, D), BF),
            jax.ShapeDtypeStruct((2 * LINE, CAP, CAP), F32),
            jax.ShapeDtypeStruct((LINE, CAP, HID), F32),
        ),
        in_specs=[ANY] * 4 + [pl.BlockSpec(memory_space=pltpu.SMEM)] + [INV] * 6,
        out_specs=(ANY,) + (INV,) * 2 + (ANY,) * 6,
        scratch_shapes=[
            VMEM((n, D, WIDE), BF), VMEM((n, DEEP, D), BF), VMEM((16, 256), F32), VMEM((LINE, 8, 128), F32),
            VMEM((16, 16, 256), F32), VMEM((LINE, CAP, 128), F32), VMEM((16, D), F32), VMEM((16, HID), F32),
            VMEM((n, LINE, CAP, D), BF), VMEM((n, LINE, CAP, QKV), BF), VMEM((n, LINE, CAP, DEEP), BF),
            VMEM((2 * LINE, CAP, CAP), F32), VMEM((LINE, CAP, HID), F32), VMEM((2 * CAP, DEEP), F32),
            VMEM((n, LINE, CAP, D), BF), VMEM((LINE, CAP, WIDE), BF),
            VMEM((CAP, D), F32),
            VMEM((CAP, D), F32), VMEM((4, CAP, D), BF), VMEM((4, CAP, D), BF),
            VMEM((3, CAP, D), BF), VMEM((3, CAP, D), BF),
            VMEM((CAP, D), F32), VMEM((3, CAP, D), BF), VMEM((3, CAP, D), BF),
            VMEM((2, 4, 128, QKV), BF), VMEM((2, 4, 128, HID), BF), VMEM((2, 4, 80, D), BF),
            VMEM((n, LINE, 8, 128), F32), VMEM((n, 8, 128), F32),
            VMEM((n, 3, 4, 80, 512), BF), VMEM((n, 3, 2, 80, 512), BF),
            VMEM((n, 3, 80, 512), BF), VMEM((n, 3, 80, 512), BF),
            VMEM((4, 80, 512), BF), VMEM((2, 80, 512), BF),
            VMEM((n, 3, 4, 64, HID), BF), VMEM((n, 3, 2, 64, QKV), BF), VMEM((n, 3, 2, 64, HID), BF),
            VMEM((n, 3, 64, HID), BF), VMEM((n, 3, 64, HID), BF),
            VMEM((4, 64, HID), BF), VMEM((2, 64, QKV), BF), VMEM((2, 64, HID), BF),
            VMEM((n, 128, HID), BF), VMEM((n, 80, D), BF),
            VMEM((n, LINE, 8, 128), F32), VMEM((n, 16, 8, 128), F32), VMEM((n, 2, 8, 128), F32),
            DMA((n,)), DMA((n,)), DMA((n,)), DMA((n, 7)), DMA((n, 2)), DMA((n,)), DMA((n,)), DMA((n,)),
            DMA((n,)), DMA((n,)), DMA, DMA, DMA, DMA, DMA, DMA,
            DMA((4,)), DMA((4, 8)), DMA((4,)), DMA((4, 4)), DMA((4,)), DMA((4,)), DMA((2,)), DMA((2,)), DMA,
            DMA((n, 8)), DMA((n, 4)), DMA((n, 4)), DMA((n, 4)), DMA((n,)), DMA((n,)), DMA((n, 3)), DMA((n, 2)),
            DMA((n,)), DMA((n,)), DMA((n,)), DMA((n,)), DMA((n,)), DMA((n, 4)), DMA((n,)), DMA((n,)),
        ],
        compiler_params=pltpu.CompilerParams(
            collective_id=0, has_side_effects=True, vmem_limit_bytes=63 * 2**20
        ),
        name="whole",
    )(wqkv, win, wo, wfc, lengths, gain, bias, b_fc, b_in, x0, cot)


def per_device(
    inputs, cotangent, lengths, ln_gain, ln_bias, w_qkv, w_attn_out, w_in, b_in, w_fc, b_fc
):
    xh, c = (lax.axis_index(a) for a in ("xh", "c"))
    hidden, grad, fs, fq, fi, fo, ff, _, _ = whole(
        w_qkv, w_in, w_attn_out, w_fc, lengths, ln_gain, ln_bias, b_fc, b_in, inputs, cotangent
    )
    mine = lax.dynamic_index_in_dim(fs, xh, 1, keepdims=False)
    pick = lax.dynamic_slice(mine[:, 0:3], (0, 0, 64 * c), (LAYERS, 3, 64))
    b_in_grad = lax.dynamic_slice(mine[:, 3:7].reshape(LAYERS, HID), (0, 256 * c), (LAYERS, 256))
    return (
        hidden,
        grad,
        pick[:, 0],
        pick[:, 1],
        fq.astype(F32),
        fo.astype(F32),
        fi.astype(F32),
        b_in_grad,
        ff.astype(F32),
        pick[:, 2],
    )


def solution(mesh):
    fine = Mesh(mesh.devices.reshape(4, 2, 4, 2, 2), AXES)
    rows = P(AXES, None)
    shard = ("z", "xh", "c")
    vector, matrix = P(None, shard), P(None, shard, None)
    in_specs = (
        rows, rows, rows, vector, vector, matrix, matrix, matrix, vector, matrix, vector,
    )
    out_specs = (
        rows, rows, vector, vector, matrix, matrix, matrix, vector, matrix, vector,
    )
    return jax.shard_map(
        per_device, mesh=fine, in_specs=in_specs, out_specs=out_specs, check_vma=False
    )
```
